128 devices in a mesh: dp: 32 (over y_lo, z, x), seq: 4 (over y_hi, core).
Axes of the slice: x: 4, y: 4 (y_hi: 2, y_lo: 2; y = y_hi * 2 + y_lo), z: 4, core: 2. Of those that a mesh axis runs over, the one named last changes fastest.
Arguments:
- inputs: bfloat16 [32, 580, 1024], P('dp', 'seq'), may hold values from -6 to 6
- token_mask: int32 [32, 580], P('dp', 'seq'), may hold values from 0 to 1, as said below
- first_gain: bfloat16 [1, 1024], P(None, ('dp', 'seq')), may hold values from 0.5 to 1.5
- first_shift: bfloat16 [1, 1024], P(None, ('dp', 'seq')), may hold values from -3 to 3
- query_key_value_weight: bfloat16 [1, 1024, 3072], P(None, ('dp', 'seq')), may hold values from -0.1875 to 0.1875
- query_value_bias: bfloat16 [1, 2048], P(None, ('dp', 'seq')), may hold values from -3 to 3
- output_weight: bfloat16 [1, 1024, 1024], P(None, ('dp', 'seq')), may hold values from -0.75 to 0.75
- output_bias: bfloat16 [1, 1024], P(None, ('dp', 'seq')), may hold values from -3 to 3
- second_gain: bfloat16 [1, 1024], P(None, ('dp', 'seq')), may hold values from 0.5 to 1.5
- second_shift: bfloat16 [1, 1024], P(None, ('dp', 'seq')), may hold values from -3 to 3
- up_weight: bfloat16 [1, 1024, 4096], P(None, ('dp', 'seq')), may hold values from -0.1875 to 0.1875
- up_bias: bfloat16 [1, 4096], P(None, ('dp', 'seq')), may hold values from -3 to 3
- down_weight: bfloat16 [1, 4096, 1024], P(None, ('dp', 'seq')), may hold values from -0.09375 to 0.09375
- down_bias: bfloat16 [1, 1024], P(None, ('dp', 'seq')), may hold values from -3 to 3
- cotangent: bfloat16 [32, 580, 1024], P('dp', 'seq'), may hold values from -6 to 6
Outputs:
- block_output: bfloat16 [32, 580, 1024], P('dp', 'seq')
- input_gradient: float32 [32, 580, 1024], P('dp', 'seq')
- first_gain_gradient: float32 [1, 1024], P(None, ('dp', 'seq'))
- first_shift_gradient: float32 [1, 1024], P(None, ('dp', 'seq'))
- query_key_value_weight_gradient: float32 [1, 1024, 3072], P(None, ('dp', 'seq'))
- query_value_bias_gradient: float32 [1, 2048], P(None, ('dp', 'seq'))
- output_weight_gradient: float32 [1, 1024, 1024], P(None, ('dp', 'seq'))
- output_bias_gradient: float32 [1, 1024], P(None, ('dp', 'seq'))
- second_gain_gradient: float32 [1, 1024], P(None, ('dp', 'seq'))
- second_shift_gradient: float32 [1, 1024], P(None, ('dp', 'seq'))
- up_weight_gradient: float32 [1, 1024, 4096], P(None, ('dp', 'seq'))
- up_bias_gradient: float32 [1, 4096], P(None, ('dp', 'seq'))
- down_weight_gradient: float32 [1, 4096, 1024], P(None, ('dp', 'seq'))
- down_bias_gradient: float32 [1, 1024], P(None, ('dp', 'seq'))
The draws below stay inside these ranges and needn't reach their ends.
Inputs may be any that keep to these rules, and one draw needn't show every extreme that they name: In every image the positions with token_mask 1 are the first ones, more than 435 of them; image 0 has exactly its last min(3, 144) positions at 0.
All inputs are finite; a program needn't handle non-finite values.
Results may differ from the reference program's by a relative error of at most 0.017.
Values may be sent and summed in bfloat16 or wider, within the bound.
No kernel may reach another device: no remote copies, remote signals or barrier semaphores. Data moves between devices by JAX's collectives and lax.ppermute only.
A program may use at most 192 MiB of HBM per device.

```python
import jax
import jax.numpy as jnp
from jax import lax

D = 1024
FF = 4096
HEADS = 16
HEAD_DIM = 64
LAYERS = 1
TOK_SEQ = 145
SEQ = 580
IMAGES = 32


def draw_token_mask(key, part):
    key = jax.random.fold_in(key, 11)
    dropped = jax.random.randint(key, (IMAGES,), 0, TOK_SEQ)
    dropped = dropped.at[0].set(min(3, TOK_SEQ - 1))
    position = jnp.arange(SEQ, dtype=jnp.int32)
    return (position[None, :] < (SEQ - dropped)[:, None]).astype(jnp.int32)


def raised(values, own_key, source, target, shards_of, factor):
    owner, partner = [(jnp.arange(values.shape[dim]) // (values.shape[dim] // shards_of)).reshape([-1 if axis == dim else 1 for axis in range(values.ndim)]) for dim in (source, target)]
    chosen = jax.random.permutation(own_key, shards_of)[partner]
    strong = (owner == chosen) | (owner == (partner + shards_of // 2) % shards_of)
    return jnp.where(strong, factor * values, values)


def block_levels(key, dims, shards, smallest, high):
    level, own = 1.0, jax.random.fold_in(key, 6)
    for dim, parts in shards:
        draws = jnp.exp(jax.random.uniform(jax.random.fold_in(own, dim), (parts,), jnp.float32, smallest / len(shards), high / len(shards)))
        level = level * jnp.repeat(draws, dims[dim] // parts).reshape([-1 if axis == dim else 1 for axis in range(len(dims))])
    return level


def bell_draw(own_key, shape, spread, most, shards=(), kind=jnp.bfloat16):
    array = jax.random.normal(own_key, shape, jnp.float32) * spread
    if len(shards) > 0:
        array = block_levels(own_key, shape, shards, -0.22, 0.18) * array
    return jnp.clip(array, min=-most, max=most).astype(kind)


def gaussian_with(stream_key, dims, spread, limit, pieces, heavy, kind=jnp.bfloat16):
    entries = spread * jax.random.normal(stream_key, dims, jnp.float32)
    if pieces:
        entries = entries * block_levels(stream_key, dims, pieces, -0.22, 0.18)
    return jnp.clip(raised(entries, jax.random.fold_in(stream_key, 3), *heavy), -limit, limit).astype(kind)


def setup_inputs(seed: int = 0) -> dict:
    seeds = jax.random.split(jax.random.key(seed), 16)
    inputs = bell_draw(seeds[0], (IMAGES, SEQ, D), 1.0, 6.0, ((0, 32), (1, 4)))
    token_mask = draw_token_mask(jax.random.fold_in(seeds[15], 71), 0)
    first_gain = jnp.clip(1.0 + 0.1 * jax.random.normal(seeds[2], (LAYERS, D), jnp.float32), 0.5, 1.5).astype(jnp.bfloat16)
    first_shift = bell_draw(seeds[3], (LAYERS, D), 0.3, 3.0, ((1, 128),))
    query_key_value_weight = bell_draw(seeds[4], (LAYERS, D, 3 * D), D ** -0.5, 0.1875, ((1, 128),))
    query_value_bias = bell_draw(seeds[5], (LAYERS, 2 * D), 0.5, 3.0, ((1, 128),))
    output_weight = bell_draw(seeds[6], (LAYERS, D, D), (D // 16) ** -0.5, 0.75, ((1, 128),))
    output_bias = bell_draw(seeds[7], (LAYERS, D), 0.5, 3.0, ((1, 128),))
    second_gain = jnp.clip(1.0 + 0.1 * jax.random.normal(seeds[8], (LAYERS, D), jnp.float32), 0.5, 1.5).astype(jnp.bfloat16)
    second_shift = bell_draw(seeds[9], (LAYERS, D), 0.3, 3.0, ((1, 128),))
    up_weight = bell_draw(seeds[10], (LAYERS, D, FF), D ** -0.5, 0.1875, ((1, 128),))
    up_bias = bell_draw(seeds[11], (LAYERS, FF), 0.5, 3.0, ((1, 128),))
    down_weight = bell_draw(seeds[12], (LAYERS, FF, D), FF ** -0.5, 0.09375, ((1, 128),))
    down_bias = bell_draw(seeds[13], (LAYERS, D), 0.5, 3.0, ((1, 128),))
    cotangent = gaussian_with(seeds[14], (IMAGES, SEQ, D), 1.0, 6.0, ((0, 32), (1, 4)), (0, 2, 32, 2.75))
    return dict(inputs=inputs, token_mask=token_mask, first_gain=first_gain, first_shift=first_shift, query_key_value_weight=query_key_value_weight, query_value_bias=query_value_bias, output_weight=output_weight, output_bias=output_bias, second_gain=second_gain, second_shift=second_shift, up_weight=up_weight, up_bias=up_bias, down_weight=down_weight, down_bias=down_bias, cotangent=cotangent)


exact_mode = lax.Precision.HIGHEST

@jax.custom_vjp
def low(v):
    return lax.optimization_barrier(v.astype(jnp.bfloat16)).astype(jnp.float32)

@jax.custom_vjp
def low_back(v):
    return v

def low_keep(v):
    return (low(v), None)

def low_pass(kept, grad):
    return (grad,)

def back_keep(v):
    return (v, None)

def back_low(kept, grad):
    return (low(grad),)
low.defvjp(low_keep, low_pass)
low_back.defvjp(back_keep, back_low)

def layer_norm(values_in, gain_vector, offset_vector):
    average = lax.optimization_barrier(jnp.mean(values_in, axis=-1, keepdims=True))
    centred = values_in - average
    variance = lax.optimization_barrier(jnp.mean(centred * centred, axis=-1, keepdims=True))
    return centred * lax.rsqrt(variance + 1e-06) * gain_vector + offset_vector

def gelu_exact(values_in):
    return jax.nn.gelu(values_in, approximate=False)

def block(hidden_in, keep_row, weights):
    attend_gain, attend_shift, inward_matrix, inward_bias, outward_matrix, outward_bias, feed_gain, feed_shift, expand_matrix, expand_bias, reduce_matrix, reduce_bias = weights
    normed_first = low(layer_norm(hidden_in, attend_gain, attend_shift))
    projected = jnp.dot(normed_first, inward_matrix, precision=exact_mode)
    queries = low(low_back(projected[:, :D] + inward_bias[:D]))
    keys_all = low(low_back(projected[:, D:2 * D]))
    values_all = low(low_back(projected[:, 2 * D:] + inward_bias[D:]))
    query_heads = queries.reshape(SEQ, HEADS, HEAD_DIM)
    key_heads = keys_all.reshape(SEQ, HEADS, HEAD_DIM)
    value_heads = values_all.reshape(SEQ, HEADS, HEAD_DIM)
    scores = jnp.einsum('qhd,khd->hqk', query_heads, key_heads, precision=exact_mode) * HEAD_DIM ** (-0.5)
    scores = jnp.where(keep_row[None, None, :] > 0, low_back(scores), -1e+30)
    shifted = scores - lax.optimization_barrier(jnp.max(scores, axis=-1, keepdims=True))
    powers = jnp.exp(shifted)
    probs = low(powers / lax.optimization_barrier(jnp.sum(powers, axis=-1, keepdims=True)))
    mixed = jnp.einsum('hqk,khd->qhd', probs, value_heads, precision=exact_mode).reshape(SEQ, D)
    mixed = low(low_back(mixed))
    residual = hidden_in + low_back(jnp.dot(mixed, outward_matrix, precision=exact_mode) + outward_bias)
    normed_second = low(layer_norm(residual, feed_gain, feed_shift))
    expanded = low_back(jnp.dot(normed_second, expand_matrix, precision=exact_mode) + expand_bias)
    activated = low(gelu_exact(expanded))
    return residual + low_back(jnp.dot(activated, reduce_matrix, precision=exact_mode) + reduce_bias)

def reference(inputs, token_mask, first_gain, first_shift, query_key_value_weight, query_value_bias, output_weight, output_bias, second_gain, second_shift, up_weight, up_bias, down_weight, down_bias, cotangent):
    weights = (first_gain.astype(jnp.float32), first_shift.astype(jnp.float32), query_key_value_weight.astype(jnp.float32), query_value_bias.astype(jnp.float32), output_weight.astype(jnp.float32), output_bias.astype(jnp.float32), second_gain.astype(jnp.float32), second_shift.astype(jnp.float32), up_weight.astype(jnp.float32), up_bias.astype(jnp.float32), down_weight.astype(jnp.float32), down_bias.astype(jnp.float32))

    def forward(start, weight_tuple):

        def one_image(pair):
            hidden, keep_row = pair
            for layer_index in range(LAYERS):
                hidden = block(hidden, keep_row, tuple((member[layer_index] for member in weight_tuple)))
            return hidden
        return lax.map(jax.checkpoint(one_image), (start, token_mask))
    final, pullback = jax.vjp(forward, inputs.astype(jnp.float32), weights)
    input_gradient, weight_gradients = pullback(cotangent.astype(jnp.float32))
    return (final.astype(jnp.bfloat16), input_gradient, weight_gradients[0], weight_gradients[1], weight_gradients[2], weight_gradients[3], weight_gradients[4], weight_gradients[5], weight_gradients[6], weight_gradients[7], weight_gradients[8], weight_gradients[9], weight_gradients[10], weight_gradients[11])
```

```python
import jax
import jax.numpy as jnp
from jax import lax
from jax.sharding import Mesh, PartitionSpec as P

HEADS = 16
HEAD_DIM = 64
TOK = 145
PAD = 160
LOCAL_HEADS = 4
GROUP = 4
WIDTH = 1024
BF = jnp.bfloat16
F32 = jnp.float32
DP = ("ylo", "z", "x")
SEQ = ("yhi", "core")
ALL = DP + SEQ
SWAP = [(0, 1), (1, 0)]


def over_y(v):
    return lax.ppermute(v, "yhi", SWAP)


def over_core(v):
    return lax.ppermute(v, "core", SWAP)


RELATIVE = (0, 2, 1, 3)


def gather_tokens(v):
    pair = jnp.stack([v, over_y(v)])
    return jnp.concatenate([pair, over_core(pair)])


def gather_heads(o):
    got = over_y(o)
    pair = jnp.stack([o, got[jnp.array([1, 0, 3, 2])]])
    other = over_core(pair)
    return jnp.concatenate([pair, other[:, jnp.array([2, 3, 0, 1])]])


def scatter_core(part):
    got = over_core(part[2:].astype(BF))
    return part[:2] + got.astype(F32)


def scatter_tokens(part):
    two = scatter_core(part)
    return two[0] + over_y(two[1].astype(BF)).astype(F32)


def rel_to_abs(v, seq_index):
    place = jnp.array([0, 2, 1, 3])
    return v[place[jnp.bitwise_xor(seq_index, jnp.arange(4))]]


def norm_stats(v):
    average = jnp.mean(v, axis=-1, keepdims=True)
    centred = v - average
    variance = jnp.mean(centred * centred, axis=-1, keepdims=True)
    scale = lax.rsqrt(variance + 1e-06)
    return centred * scale, scale


def norm_back(grad, gain, normed, scale):
    e = grad * gain
    return scale * (
        e
        - jnp.mean(e, axis=-1, keepdims=True)
        - normed * jnp.mean(e * normed, axis=-1, keepdims=True)
    )


def dot(a, b):
    return jnp.dot(a, b, preferred_element_type=F32)


def dot_t(a, b):
    return lax.dot_general(a, b, (((1,), (1,)), ((), ())), preferred_element_type=F32)


def t_dot(a, b):
    return lax.dot_general(a, b, (((0,), (0,)), ((), ())), preferred_element_type=F32)


def split_heads(v):
    return v.reshape(v.shape[0], LOCAL_HEADS, HEAD_DIM)


def body(
    inputs,
    token_mask,
    first_gain,
    first_shift,
    qkv_weight,
    qv_bias,
    out_weight,
    out_bias,
    second_gain,
    second_shift,
    up_weight,
    up_bias,
    down_weight,
    down_bias,
    cotangent,
):
    seq = lax.axis_index("yhi") * 2 + lax.axis_index("core")
    rows = GROUP * PAD

    down_pair = jnp.stack([down_weight[0], lax.ppermute(down_weight[0], "ylo", SWAP)])
    ylo = lax.axis_index("ylo")
    down_pair = jnp.where(ylo == 0, down_pair, down_pair[::-1])
    down_w = lax.all_gather(down_pair, ("z", "x"), axis=0, tiled=False).reshape(1024, WIDTH)

    mask_row = jnp.pad(token_mask.astype(BF), ((0, 0), (0, WIDTH - TOK)))
    x_block = jnp.concatenate(
        [inputs[0], mask_row, jnp.zeros((PAD - TOK - 1, WIDTH), BF)], axis=0
    )
    g_block = jnp.pad(cotangent[0], ((0, PAD - TOK), (0, 0)))
    both = gather_tokens(jnp.stack([x_block, g_block]))
    x_low, dm = both[:, 0].reshape(rows, WIDTH), both[:, 1].reshape(rows, WIDTH)
    keep = both[:, 0, TOK, :PAD].reshape(rows)

    qkv_cols = qkv_weight[0].reshape(8, 3, GROUP, 256).transpose(2, 0, 1, 3).reshape(GROUP, 8, 768)
    up_cols = (
        up_weight[0]
        .reshape(8, 2, 4, 4, GROUP, 32)
        .transpose(4, 0, 2, 3, 1, 5)
        .reshape(GROUP, 8, 1024)
    )
    out_cols = out_weight[0].reshape(8, GROUP, 256).transpose(1, 0, 2)
    extra = jnp.concatenate(
        [
            first_gain.reshape(8, 1),
            first_shift.reshape(8, 1),
            qv_bias.reshape(8, 2),
            out_bias.reshape(8, 1),
            second_gain.reshape(8, 1),
            second_shift.reshape(8, 1),
            up_bias.reshape(8, 4),
            down_bias.reshape(8, 1),
        ],
        axis=1,
    )
    extra = jnp.broadcast_to(jnp.pad(extra, ((0, 0), (0, 116)))[None], (GROUP, 8, 128))
    piece = jnp.concatenate([qkv_cols, up_cols, out_cols, extra], axis=2)
    send = jnp.broadcast_to(piece[None], (32, GROUP, 8, 2176)).reshape(1024, 2176)
    got = lax.all_to_all(send, ALL, 0, 0, tiled=True)
    qkv_w = got[:, :768]
    up_w = got[:, 768:1792]
    out_mine = got[:, 1792:2048]
    vectors = got[:, 2048:2060].astype(F32)
    gain_1, shift_1 = vectors[:, 0], vectors[:, 1]
    q_bias = lax.dynamic_slice(vectors[:, 2:4].reshape(2048), (seq * 256,), (256,))
    v_bias = lax.dynamic_slice(vectors[:, 2:4].reshape(2048), (1024 + seq * 256,), (256,))
    b_out, gain_2, shift_2 = vectors[:, 4], vectors[:, 5], vectors[:, 6]
    b_up = vectors[:, 7:11].reshape(2, 4, 4, GROUP, 32)
    b_up = lax.dynamic_index_in_dim(b_up, seq, 3, keepdims=False).transpose(1, 2, 0, 3).reshape(1024)
    b_down = vectors[:, 11]

    out_w = rel_to_abs(gather_tokens(out_mine), seq)
    out_w = out_w.reshape(GROUP, GROUP, 256, 256)[:, jnp.bitwise_xor(seq, jnp.array(RELATIVE))]
    out_w = out_w.transpose(1, 2, 0, 3).reshape(WIDTH, WIDTH)

    x = x_low.astype(F32)
    normed_1, scale_1 = norm_stats(x)
    n1 = (normed_1 * gain_1 + shift_1).astype(BF)
    proj = dot(n1, qkv_w)
    q = split_heads((proj[:, :256] + q_bias).astype(BF))
    k = split_heads(proj[:, 256:512].astype(BF))
    v = split_heads((proj[:, 512:] + v_bias).astype(BF))
    scores = jnp.einsum("qhd,khd->hqk", q, k, preferred_element_type=F32) * HEAD_DIM ** (-0.5)
    scores = jnp.where(keep[None, None, :] > 0, scores, -1e30)
    peak = jnp.max(scores, axis=-1, keepdims=True)
    lse = peak + jnp.log(jnp.sum(jnp.exp(scores - peak), axis=-1, keepdims=True))
    probs = jnp.exp(scores - lse)
    probs_low = probs.astype(BF)
    o = jnp.einsum("hqk,khd->qhd", probs_low, v, preferred_element_type=F32)
    o = o.astype(BF).reshape(GROUP, PAD, 256)
    o_all = gather_heads(o).transpose(1, 2, 0, 3).reshape(rows, WIDTH)
    r = x + dot(o_all, out_w) + b_out
    normed_2, scale_2 = norm_stats(r)
    n2 = (normed_2 * gain_2 + shift_2).astype(BF)
    u = dot(n2, up_w) + b_up
    cdf = 0.5 * (1.0 + lax.erf(u * (0.5**0.5)))
    z = (u * cdf).astype(BF)
    slope = cdf + u * jnp.exp(-0.5 * u * u) * 0.3989422804014327
    y_part = dot(z, down_w).reshape(GROUP, PAD, WIDTH)
    y = scatter_tokens(y_part) + r[:PAD] + b_down
    block_output = y[:TOK].astype(BF)[None]

    d_down_w = t_dot(z, dm)
    d_down_w = lax.psum_scatter(
        d_down_w.astype(BF).reshape(16, 64, WIDTH), ("z", "x"), scatter_dimension=0, tiled=True
    )[0].reshape(2, 32, WIDTH)
    mine = jnp.where(ylo == 0, d_down_w[0], d_down_w[1])
    theirs = jnp.where(ylo == 0, d_down_w[1], d_down_w[0])
    d_down_w = mine.astype(F32) + lax.ppermute(theirs, "ylo", SWAP).astype(F32)
    du = (slope * dot_t(dm, down_w)).astype(BF)
    d_up_w = t_dot(n2, du)
    d_up_b = jnp.sum(du, axis=0, dtype=F32)
    dn2 = dot_t(du, up_w).reshape(GROUP, PAD, WIDTH)
    two = scatter_core(dn2).astype(BF)
    dn2 = (two.astype(F32) + over_y(two).astype(F32)[::-1]).reshape(2 * PAD, WIDTH)
    half = 2 * PAD
    dr = dm[:half].astype(F32) + norm_back(dn2, gain_2, normed_2[:half], scale_2[:half])
    da = dr.astype(BF)
    da = jnp.concatenate([da, over_core(da)])
    d_gain_2 = jnp.sum(dn2[:PAD] * normed_2[:PAD], axis=0)
    d_shift_2 = jnp.sum(dn2[:PAD], axis=0)
    d_out_b = jnp.sum(da[:PAD], axis=0, dtype=F32)
    d_down_b = jnp.sum(dm[:PAD], axis=0, dtype=F32)
    d_out_w = t_dot(o_all, lax.dynamic_slice(da, (0, seq * 256), (rows, 256))).astype(BF)
    d_out_w = rel_to_abs(d_out_w.reshape(GROUP, 256, 256), seq).reshape(WIDTH, 256)
    do = split_heads(dot_t(da, out_w[:256]).astype(BF))
    d_probs = jnp.einsum("qhd,khd->hqk", do, v, preferred_element_type=F32)
    inner = jnp.sum(probs * d_probs, axis=-1, keepdims=True)
    ds = (probs * (d_probs - inner)).astype(BF)
    dq = jnp.einsum("hqk,khd->qhd", ds, k, preferred_element_type=F32) * HEAD_DIM ** (-0.5)
    dk = jnp.einsum("hqk,qhd->khd", ds, q, preferred_element_type=F32) * HEAD_DIM ** (-0.5)
    dv = jnp.einsum("hqk,qhd->khd", probs_low, do, preferred_element_type=F32)
    d_proj = jnp.concatenate([t.astype(BF).reshape(rows, 256) for t in (dq, dk, dv)], axis=1)
    d_bias = jnp.sum(d_proj, axis=0, dtype=F32)
    d_qkv_w = t_dot(n1, d_proj)
    dn1 = dot_t(d_proj, qkv_w)
    d_gain_1 = jnp.sum(dn1 * normed_1, axis=0)
    d_shift_1 = jnp.sum(dn1, axis=0)

    own = (jnp.arange(GROUP) == seq).astype(F32)
    d_qv_b = jnp.concatenate(
        [(own[:, None] * d_bias[None, :256]).reshape(-1), (own[:, None] * d_bias[None, 512:]).reshape(-1)]
    )
    d_up_b = d_up_b.reshape(4, 4, 2, 32).transpose(2, 0, 1, 3).reshape(32, 1, 32)
    d_up_b = (d_up_b * own[None, :, None]).reshape(1024, 4)
    extra = jnp.concatenate(
        [
            jnp.stack([d_gain_1, d_shift_1], axis=1),
            d_qv_b.reshape(1024, 2),
            jnp.stack([d_out_b, d_gain_2, d_shift_2], axis=1),
            d_up_b,
            d_down_b.reshape(1024, 1),
            jnp.zeros((1024, 116), F32),
        ],
        axis=1,
    )
    send = jnp.concatenate(
        [d_qkv_w.astype(BF), d_up_w.astype(BF), d_out_w, extra.astype(BF)], axis=1
    )
    got = lax.all_to_all(send, ALL, 0, 0, tiled=True)
    total = jnp.sum(got.reshape(32, GROUP, 8, 2176).astype(F32), axis=0)
    d_qkv_w = total[:, :, :768].reshape(GROUP, 8, 3, 256).transpose(1, 2, 0, 3).reshape(1, 8, 3072)
    d_up_w = (
        total[:, :, 768:1792]
        .reshape(GROUP, 8, 4, 4, 2, 32)
        .transpose(1, 4, 2, 3, 0, 5)
        .reshape(1, 8, 4096)
    )
    d_out_w = total[:, :, 1792:2048].transpose(1, 0, 2).reshape(1, 8, WIDTH)
    small = jnp.sum(total[:, :, 2048:2060], axis=0)

    def column(i):
        return small[:, i].reshape(1, 8)

    dn1_own = scatter_tokens(dn1.reshape(GROUP, PAD, WIDTH))
    g0 = dr[:PAD] + norm_back(dn1_own, gain_1, normed_1[:PAD], scale_1[:PAD])
    return (
        block_output,
        g0[:TOK][None],
        column(0),
        column(1),
        d_qkv_w,
        small[:, 2:4].reshape(1, 16),
        d_out_w,
        column(4),
        column(5),
        column(6),
        d_up_w,
        small[:, 7:11].reshape(1, 32),
        d_down_w[None],
        column(11),
    )


def solution(mesh):
    fine = Mesh(mesh.devices.reshape(2, 4, 4, 2, 2), ALL)
    tokens = P(DP, SEQ, None)
    vector = P(None, ALL)
    matrix = P(None, ALL, None)
    return jax.shard_map(
        body,
        mesh=fine,
        in_specs=(
            tokens,
            P(DP, SEQ),
            vector,
            vector,
            matrix,
            vector,
            matrix,
            vector,
            vector,
            vector,
            matrix,
            vector,
            matrix,
            vector,
            tokens,
        ),
        out_specs=(
            tokens,
            tokens,
            vector,
            vector,
            matrix,
            vector,
            matrix,
            vector,
            vector,
            vector,
            matrix,
            vector,
            matrix,
            vector,
        ),
        check_vma=False,
    )
```

```python
import jax
import jax.numpy as jnp
from jax import lax
from jax.experimental import pallas as pl
from jax.experimental.pallas import tpu as pltpu
from jax.sharding import Mesh, PartitionSpec as P

TOK = 145
PAD = 160
ROWS = 4 * PAD
HALF = 2 * PAD
WIDTH = 1024
BF = jnp.bfloat16
F32 = jnp.float32
DP = ("ylo", "z", "x")
SEQ = ("yhi", "core")
ALL = DP + SEQ
SWAP = [(0, 1), (1, 0)]
RELATIVE = (0, 2, 1, 3)
QKV_COLS = 768
OUT_COLS = 256
EXTRA = 128
REST = QKV_COLS + OUT_COLS + EXTRA


def over_y(v):
    return lax.ppermute(v, "yhi", SWAP)


def over_core(v):
    return lax.ppermute(v, "core", SWAP)


def dot(a, b):
    return jnp.dot(a, b, preferred_element_type=F32)


def dot_t(a, b):
    return lax.dot_general(a, b, (((1,), (1,)), ((), ())), preferred_element_type=F32)


def t_dot(a, b):
    return lax.dot_general(a, b, (((0,), (0,)), ((), ())), preferred_element_type=F32)


def iota(shape, dim):
    return lax.broadcasted_iota(jnp.int32, shape, dim)


def call(kernel, outs, *args, scratch=(), scalars=0, us=1.0):
    vmem = pl.BlockSpec(memory_space=pltpu.VMEM)
    specs = [pl.BlockSpec(memory_space=pltpu.SMEM)] * scalars + [vmem] * (len(args) - scalars)
    return pl.pallas_call(
        kernel,
        out_shape=[jax.ShapeDtypeStruct(s, d) for s, d in outs],
        in_specs=specs,
        out_specs=[vmem] * len(outs),
        scratch_shapes=list(scratch),
        compiler_params=pltpu.CompilerParams(vmem_limit_bytes=60 * 2**20),
        cost_estimate=pl.CostEstimate(
            flops=int(us * 1.1e9), bytes_accessed=2**20, transcendentals=0
        ),
    )(*args)


def block(b):
    return slice(b * PAD, (b + 1) * PAD)


def norm_stats(v):
    average = jnp.mean(v, axis=-1, keepdims=True)
    centred = v - average
    variance = jnp.mean(centred * centred, axis=-1, keepdims=True)
    scale = lax.rsqrt(variance + 1e-06)
    return centred * scale, scale


def norm_back(grad, gain, normed, scale):
    e = grad * gain
    return scale * (
        e
        - jnp.mean(e, axis=-1, keepdims=True)
        - normed * jnp.mean(e * normed, axis=-1, keepdims=True)
    )


def piece_columns(refs):
    out = jnp.zeros((8, EXTRA), F32)
    lane = iota((8, EXTRA), 1)
    place = 0
    for ref in refs:
        size = ref.shape[1]
        for c in range(size // 8):
            spread = jnp.broadcast_to(ref[...].astype(F32), (8, size))
            hit = iota((8, size), 1) == iota((8, size), 0) + 8 * c
            column = jnp.sum(jnp.where(hit, spread, 0.0), axis=1, keepdims=True)
            out = jnp.where(lane == place, column, out)
            place += 1
    return out


def regroup(tile_of, source_of):
    lane = iota((8, 128), 1)
    tiles = []
    for t in range(8):
        tile = jnp.zeros((8, 128), F32)
        for a in range(4):
            source, b = source_of(t, a)
            part = tile_of(source)
            if a != b:
                part = pltpu.roll(part, (32 * (a - b)) % 128, 1)
            tile = jnp.where(lane // 32 == a, part, tile)
        tiles.append(tile)
    return jnp.concatenate(tiles, axis=1)


def image_of(t, a):
    return 16 * (a % 2) + 2 * t + a // 2


def hidden_place(dp):
    return (dp % 16) // 2, 2 * (dp % 2) + dp // 16


def tokens_kernel(x, mask, out, tok):
    row = jnp.zeros((8, WIDTH), F32)
    tok[0:8] = row
    tok[0:1, 0:TOK] = mask[...].astype(F32)
    row = tok[0:8]
    lifted = [pltpu.roll(row, PAD * b, 1)[0:1] if b else row[0:1] for b in range(4)]
    tok[0:TOK] = x[0].astype(F32)
    for b in range(4):
        tok[TOK + b : TOK + b + 1] = lifted[b]
    tok[TOK + 4 :] = jnp.zeros((PAD - TOK - 4, WIDTH), F32)
    out[...] = tok[...].astype(BF)


def padded_kernel(g, out, tok):
    tok[0:TOK] = g[0].astype(F32)
    tok[TOK:] = jnp.zeros((PAD - TOK, WIDTH), F32)
    out[...] = tok[...].astype(BF)


def up_columns_kernel(up, out):
    for s in range(4):
        cols = regroup(
            lambda dp: up[0, :, 128 * dp : 128 * dp + 128].astype(F32),
            lambda t, a: (image_of(t, a), s),
        ).astype(BF)
        for b in range(2):
            out[b, s] = cols


def prepare_kernel(qkv, out_w, fg, fs, qvb, ob, sg, ss, ub, db, send):
    extra = piece_columns([fg, fs, qvb, ob, sg, ss, ub, db])
    rows = []
    for s in range(4):
        parts = [qkv[0, :, 1024 * i + 256 * s : 1024 * i + 256 * s + 256] for i in range(3)]
        parts = [p.astype(F32) for p in parts]
        parts.append(out_w[0, :, 256 * s : 256 * s + 256].astype(F32))
        parts.append(extra)
        rows.append(jnp.concatenate(parts, axis=1))
    piece = jnp.concatenate(rows, axis=0).astype(BF)
    for d in range(32):
        send[d] = piece


def bias_hot(c):
    row, col = iota((128, 256), 0), iota((128, 256), 1)
    hit = (col // 16 == row // 8) & (col % 16 == 8 * c + row % 8)
    return jnp.where(hit, 1.0, 0.0).astype(BF)


def head_mask(h):
    return iota((1, 256), 1) // 64 == h


def masked(v, h):
    return jnp.where(head_mask(h), v, jnp.zeros_like(v))


def key_keep(x_own, x_yp, x_cp, x_dg):
    refs = (x_own, x_yp, x_cp, x_dg)
    return sum(r[TOK + b : TOK + b + 1, 0:ROWS].astype(F32) for b, r in enumerate(refs)) > 0


def attend_kernel(seq, x_own, x_yp, x_cp, x_dg, w, n1, qkv, o, lse, vec):
    s = seq[0]
    vec[...] = w[:, QKV_COLS + OUT_COLS : REST].astype(F32).T[0:16]
    gain, shift = vec[0:1], vec[1:2]
    for b, ref in enumerate((x_own, x_yp, x_cp, x_dg)):
        normed, _ = norm_stats(ref[...].astype(F32))
        n1[block(b)] = (normed * gain + shift).astype(BF)
    biases = []
    for start in (0, 512):
        at = pl.ds(pl.multiple_of(start + 128 * s, 128), 128)
        pieces = [jnp.broadcast_to(vec[2 + c : 3 + c, at], (8, 128)).astype(BF) for c in (0, 1)]
        biases.append((dot(pieces[0], bias_hot(0)) + dot(pieces[1], bias_hot(1)))[0:1])
    for i, bias in enumerate((biases[0], None, biases[1])):
        at = slice(256 * i, 256 * i + 256)
        proj = dot(n1[...], w[:, at])
        qkv[:, at] = (proj if bias is None else proj + bias).astype(BF)
    keep = key_keep(x_own, x_yp, x_cp, x_dg)
    q = qkv[:, 0:256] * jnp.asarray(0.125, BF)
    k, v = qkv[:, 256:512], qkv[:, 512:768]
    total = jnp.zeros((ROWS, 256), F32)
    logs = jnp.zeros((ROWS, 128), F32)
    for h in range(4):
        scores = jnp.where(keep, dot_t(masked(q, h), k), -1e30)
        peak = jnp.max(scores, axis=1, keepdims=True)
        powers = jnp.exp(scores - peak)
        weight = jnp.sum(powers, axis=1, keepdims=True)
        probs = (powers * (1.0 / weight)).astype(BF)
        total = total + dot(probs, masked(v, h))
        logs = jnp.where(iota((ROWS, 128), 1) == h, peak + jnp.log(weight), logs)
    o[...] = total.astype(BF)
    lse[...] = logs


def up_bias_row(vec, s):
    lane = iota((8, WIDTH), 1)
    out = jnp.zeros((8, WIDTH), F32)
    for c in range(4):
        row = jnp.broadcast_to(vec[7 + c : 8 + c], (8, WIDTH))
        row = pltpu.roll(row, lax.rem(8 * (c - s) + WIDTH, WIDTH), 1)
        out = jnp.where((lane // 8) % 4 == c, row, out)
    return regroup(
        lambda t: out[:, 128 * t : 128 * t + 128],
        lambda t, a: divmod(image_of(t, a), 4),
    )[0:1]


def hidden_kernel(
    seq,
    o_own,
    o_yp,
    o_cp,
    o_dg,
    x_own,
    x_yp,
    x_cp,
    x_dg,
    w_own,
    w_yp,
    w_cp,
    w_dg,
    vec,
    hidden_w,
    g_own,
    g_yp,
    g_cp,
    g_dg,
    n2,
    z,
    du,
    dm,
    dn2_mine,
    dn2_theirs,
    normed_out,
    scale_out,
    r_own,
    r,
):
    s = seq[0]
    place = [jnp.bitwise_xor(s, m) for m in RELATIVE]
    for b, ref in enumerate((g_own, g_yp, g_cp, g_dg)):
        dm[block(b)] = ref[...]
    heads = []
    for j, ref in enumerate((o_own, o_yp, o_cp, o_dg)):
        heads.append(jnp.concatenate([ref[block(b ^ j)] for b in range(4)], axis=0))
    for c, w in enumerate((w_own, w_yp, w_cp, w_dg)):
        total = jnp.zeros((ROWS, 256), F32)
        for j in range(4):
            rows = pl.ds(pl.multiple_of(256 * place[j], 256), 256)
            total = total + dot(heads[j], w[rows, :])
        r[:, pl.ds(pl.multiple_of(256 * place[c], 256), 256)] = total
    gain, shift, b_out = vec[5:6], vec[6:7], vec[4:5]
    for b, ref in enumerate((x_own, x_yp, x_cp, x_dg)):
        rows = r[block(b)] + ref[...].astype(F32) + b_out
        if b == 0:
            r_own[...] = rows
        normed, scale = norm_stats(rows)
        n2[block(b)] = (normed * gain + shift).astype(BF)
        if b < 2:
            normed_out[block(b)] = normed
            scale_out[block(b)] = jnp.broadcast_to(scale, (PAD, 128))
    bias = up_bias_row(vec, s)
    up = [hidden_w[:, 32 * b : 32 * b + 32, 0:1024].reshape(512, 1024) for b in range(2)]
    down = hidden_w[:, :, 1024:].reshape(1024, 1024)
    for c in range(4):
        at = slice(256 * c, 256 * c + 256)
        u = dot(n2[:, 0:512], up[0][:, at]) + dot(n2[:, 512:], up[1][:, at]) + bias[:, at]
        cdf = 0.5 * (1.0 + lax.erf(u * (0.5**0.5)))
        z[:, at] = (u * cdf).astype(BF)
        slope = cdf + u * jnp.exp(-0.5 * u * u) * 0.3989422804014327
        du[:, at] = (slope * dot_t(dm[...], down[at, :])).astype(BF)
    for b in range(2):
        at = slice(512 * b, 512 * b + 512)
        dn2_mine[:, at] = dot_t(du[0:HALF], up[b])
        dn2_theirs[:, at] = dot_t(du[HALF:], up[b]).astype(BF)


def down_grad_kernel(z, dm, out):
    out[...] = t_dot(z[...], dm[...]).astype(BF)


def up_grad_kernel(n2, du, dm, out, small):
    out[...] = t_dot(n2[...], du[...]).astype(BF)
    small[...] = jnp.zeros((8, WIDTH), F32)
    sums = jnp.broadcast_to(jnp.sum(du[...].astype(F32), axis=0, keepdims=True), (8, WIDTH))
    small[0:1] = regroup(
        lambda t: sums[:, 128 * t : 128 * t + 128],
        lambda t, b: hidden_place(4 * t + b),
    )[0:1]
    small[1:2] = jnp.sum(dm[block(0)].astype(F32), axis=0, keepdims=True)


def out_kernel(z, hidden_w, y_mine, y_theirs):
    down = hidden_w[:, :, 1024:].reshape(1024, 1024)
    y_mine[...] = dot(z[0:HALF], down)
    y_theirs[...] = dot(z[HALF:], down).astype(BF)


def residual_kernel(two, got, g_own, g_yp, normed, scale, vec, da, dr, small):
    gain = vec[5:6]
    small[...] = jnp.zeros((8, WIDTH), F32)
    for b, ref in enumerate((g_own, g_yp)):
        dn2 = two[block(b)].astype(F32) + got[block(1 - b)].astype(F32)
        grad = ref[...].astype(F32) + norm_back(dn2, gain, normed[block(b)], scale[block(b), 0:1])
        low = grad.astype(BF)
        da[block(b)] = low
        if b == 0:
            dr[...] = grad
            small[0:1] = jnp.sum(low.astype(F32), axis=0, keepdims=True)
            small[1:2] = jnp.sum(dn2 * normed[block(b)], axis=0, keepdims=True)
            small[2:3] = jnp.sum(dn2, axis=0, keepdims=True)


def attend_grad_kernel(
    seq,
    da_mine,
    da_cp,
    o_own,
    o_yp,
    o_cp,
    o_dg,
    w_own,
    w_yp,
    w_cp,
    w_dg,
    x_own,
    x_yp,
    x_cp,
    x_dg,
    qkv_w,
    qkv,
    lse,
    n1,
    small_b,
    small_c,
    dn1_mine,
    dn1_theirs,
    send,
    da,
    d_proj,
    rows_out,
):
    s = seq[0]
    place = [jnp.bitwise_xor(s, m) for m in RELATIVE]
    da[0:HALF] = da_mine[...]
    da[HALF:] = da_cp[...]
    own_rows = pl.ds(pl.multiple_of(256 * s, 256), 256)
    grad_o = jnp.zeros((ROWS, 256), F32)
    for c, w in enumerate((w_own, w_yp, w_cp, w_dg)):
        cols = pl.ds(pl.multiple_of(256 * place[c], 256), 256)
        grad_o = grad_o + dot_t(da[:, cols], w[own_rows, :])
    do = grad_o.astype(BF)
    keep = key_keep(x_own, x_yp, x_cp, x_dg)
    q, k, v = qkv[:, 0:256], qkv[:, 256:512], qkv[:, 512:768]
    scaled = q * jnp.asarray(0.125, BF)
    dq, dk, dv = (jnp.zeros((ROWS, 256), F32) for _ in range(3))
    for h in range(4):
        scores = jnp.where(keep, dot_t(masked(scaled, h), k), -1e30)
        probs = jnp.exp(scores - lse[:, h : h + 1])
        do_h = masked(do, h)
        d_probs = dot_t(do_h, v)
        inner = jnp.sum(probs * d_probs, axis=1, keepdims=True)
        ds = (probs * (d_probs - inner)).astype(BF)
        dq = dq + dot(ds, masked(k, h))
        dk = dk + t_dot(ds, masked(q, h))
        dv = dv + t_dot(probs.astype(BF), do_h)
    d_proj[:, 0:256] = (dq * 0.125).astype(BF)
    d_proj[:, 256:512] = (dk * 0.125).astype(BF)
    d_proj[:, 512:768] = dv.astype(BF)
    send[:, 0:QKV_COLS] = t_dot(n1[...], d_proj[...]).astype(BF)
    my_cols = pl.ds(pl.multiple_of(256 * s, 256), 256)
    for j, ref in enumerate((o_own, o_yp, o_cp, o_dg)):
        heads = jnp.concatenate([ref[block(b ^ j)] for b in range(4)], axis=0)
        rows = pl.ds(pl.multiple_of(256 * place[j], 256), 256)
        send[rows, QKV_COLS : QKV_COLS + OUT_COLS] = t_dot(heads, da[:, my_cols]).astype(BF)
    d_gain = jnp.zeros((1, WIDTH), F32)
    d_shift = jnp.zeros((1, WIDTH), F32)
    for b, ref in enumerate((x_own, x_yp, x_cp, x_dg)):
        normed, _ = norm_stats(ref[...].astype(F32))
        part = dot_t(d_proj[block(b)], qkv_w[:, 0:QKV_COLS])
        d_gain = d_gain + jnp.sum(part * normed, axis=0, keepdims=True)
        d_shift = d_shift + jnp.sum(part, axis=0, keepdims=True)
        if b < 2:
            dn1_mine[block(b)] = part
        else:
            dn1_theirs[block(b - 2)] = part.astype(BF)
    rows_out[...] = jnp.zeros((EXTRA, WIDTH), F32)
    rows_out[0:1] = d_gain
    rows_out[1:2] = d_shift
    for start, first in ((0, 0), (512, 512)):
        sums = jnp.sum(d_proj[:, first : first + 256].astype(F32), axis=0, keepdims=True)
        sums = jnp.broadcast_to(sums, (8, 256)).astype(BF)
        at = pl.ds(pl.multiple_of(start + 128 * s, 128), 128)
        for c in (0, 1):
            rows_out[2 + c : 3 + c, at] = dot_t(sums, bias_hot(c))[0:1]
    rows_out[4:7] = small_c[0:3]
    lane = iota((8, WIDTH), 1)
    row = jnp.broadcast_to(small_b[0:1], (8, WIDTH))
    for c in range(4):
        part = jnp.where((lane // 8) % 4 == c, row, 0.0)
        rows_out[7 + c : 8 + c] = pltpu.roll(part, lax.rem(8 * (s - c) + WIDTH, WIDTH), 1)[0:1]
    rows_out[11:12] = small_b[1:2]
    send[:, QKV_COLS + OUT_COLS :] = rows_out[...].T.astype(BF)


def input_grad_kernel(mine, got, dr, x_own, vec, out):
    normed, scale = norm_stats(x_own[...].astype(F32))
    dn1 = mine[...] + got[...].astype(F32)
    grad = dr[...] + norm_back(dn1, vec[0:1], normed, scale)
    out[0] = grad[0:TOK]


def sum_of(ref):
    total = ref[0].astype(F32)
    for d in range(1, ref.shape[0]):
        total = total + ref[d].astype(F32)
    return total


def sum_up_kernel(got, out):
    total = sum_of(got)
    lane = iota((8, 128), 1)
    for dp in range(32):
        t, a = hidden_place(dp)
        tile = jnp.zeros((8, 128), F32)
        for s in range(4):
            part = total[8 * s : 8 * s + 8, 128 * t : 128 * t + 128]
            if s != a:
                part = pltpu.roll(part, (32 * (s - a)) % 128, 1)
            tile = jnp.where(lane // 32 == s, part, tile)
        out[0, :, 128 * dp : 128 * dp + 128] = tile


def sum_rest_kernel(got, qkv, out, *vectors):
    total = sum_of(got)
    for s in range(4):
        rows = slice(8 * s, 8 * s + 8)
        for i in range(3):
            at = 1024 * i + 256 * s
            qkv[0, :, at : at + 256] = total[rows, 256 * i : 256 * i + 256]
        out[0, :, 256 * s : 256 * s + 256] = total[rows, QKV_COLS : QKV_COLS + OUT_COLS]
    extra = sum(total[8 * s : 8 * s + 8, QKV_COLS + OUT_COLS :] for s in range(4))
    place = 0
    for ref in vectors:
        size = ref.shape[1]
        value = jnp.zeros((8, size), F32)
        for c in range(size // 8):
            column = jnp.broadcast_to(extra[:, place : place + 1], (8, size))
            hit = iota((8, size), 1) == iota((8, size), 0) + 8 * c
            value = jnp.where(hit, column, value)
            place += 1
        ref[...] = jnp.sum(value, axis=0, keepdims=True)


def body(
    inputs,
    token_mask,
    first_gain,
    first_shift,
    qkv_weight,
    qv_bias,
    out_weight,
    out_bias,
    second_gain,
    second_shift,
    up_weight,
    up_bias,
    down_weight,
    down_bias,
    cotangent,
):
    seq = (lax.axis_index("yhi") * 2 + lax.axis_index("core")).astype(jnp.int32).reshape(1)
    ylo = lax.axis_index("ylo")
    down_yp = lax.ppermute(down_weight[0], "ylo", SWAP)
    first = jnp.where(ylo == 0, down_weight[0], down_yp)
    second = jnp.where(ylo == 0, down_yp, down_weight[0])
    down_pair = jnp.concatenate([first, second])

    (x,) = call(
        tokens_kernel,
        [((PAD, WIDTH), BF)],
        inputs,
        token_mask,
        scratch=[pltpu.VMEM((PAD, WIDTH), F32)],
    )
    x_yp = over_y(x)
    xs = (x, x_yp, over_core(x), over_core(x_yp))
    (up_send,) = call(up_columns_kernel, [((2, 4, 8, 1024), BF)], up_weight, us=2)
    up_got = lax.all_to_all(
        up_send.reshape(64, 1024), ("ylo", "yhi", "core"), 0, 0, tiled=True
    )
    (send,) = call(
        prepare_kernel,
        [((32, 32, REST), BF)],
        qkv_weight,
        out_weight,
        first_gain,
        first_shift,
        qv_bias,
        out_bias,
        second_gain,
        second_shift,
        up_bias,
        down_bias,
        us=3,
    )
    (g,) = call(
        padded_kernel,
        [((PAD, WIDTH), BF)],
        cotangent,
        scratch=[pltpu.VMEM((PAD, WIDTH), F32)],
    )
    bulk = jnp.concatenate([up_got, down_pair], axis=1)
    send, bulk, x_yp, g = lax.optimization_barrier((send, bulk, x_yp, g))
    hidden_w = lax.all_gather(bulk, ("z", "x"), axis=0, tiled=True).reshape(16, 64, 2048)
    weights = lax.all_to_all(send.reshape(1024, REST), ALL, 0, 0, tiled=True)
    weights, g = lax.optimization_barrier((weights, g))
    g_yp = over_y(g)
    gs = (g, g_yp, over_core(g), over_core(g_yp))
    w_own = weights[:, QKV_COLS : QKV_COLS + OUT_COLS]
    w_yp = over_y(w_own)
    ws = (w_own, w_yp, over_core(w_own), over_core(w_yp))

    n1, qkv, o, lse, vec = call(
        attend_kernel,
        [
            ((ROWS, WIDTH), BF),
            ((ROWS, QKV_COLS), BF),
            ((ROWS, 256), BF),
            ((ROWS, 128), F32),
            ((16, WIDTH), F32),
        ],
        seq,
        *xs,
        weights,
        scalars=1,
        us=8,
    )
    o_yp = over_y(o)
    os = (o, o_yp, over_core(o), over_core(o_yp))
    n2, z, du, dm, dn2_mine, dn2_theirs, normed_2, scale_2, r = call(
        hidden_kernel,
        [
            ((ROWS, WIDTH), BF),
            ((ROWS, WIDTH), BF),
            ((ROWS, WIDTH), BF),
            ((ROWS, WIDTH), BF),
            ((HALF, WIDTH), F32),
            ((HALF, WIDTH), BF),
            ((HALF, WIDTH), F32),
            ((HALF, 128), F32),
            ((PAD, WIDTH), F32),
        ],
        seq,
        *os,
        *xs,
        *ws,
        vec,
        hidden_w,
        *gs,
        scratch=[pltpu.VMEM((ROWS, WIDTH), F32)],
        scalars=1,
        us=12,
    )
    two = (dn2_mine + over_core(dn2_theirs).astype(F32)).astype(BF)
    two, z = lax.optimization_barrier((two, z))
    two_yp = over_y(two)
    (d_down,) = call(down_grad_kernel, [((1024, WIDTH), BF)], z, dm, us=3)
    d_down, du = lax.optimization_barrier((d_down, du))
    d_down = lax.psum_scatter(d_down, "z", scatter_dimension=0, tiled=True)
    d_down = lax.psum_scatter(d_down, "x", scatter_dimension=0, tiled=True)
    d_up, small_b = call(
        up_grad_kernel, [((1024, WIDTH), BF), ((8, WIDTH), F32)], n2, du, dm, us=3
    )
    d_up, two_yp = lax.optimization_barrier((d_up, two_yp))
    d_up = lax.all_to_all(d_up, ALL, 0, 0, tiled=True)
    da, dr, small_c = call(
        residual_kernel,
        [((HALF, WIDTH), BF), ((PAD, WIDTH), F32), ((8, WIDTH), F32)],
        two,
        two_yp,
        g,
        g_yp,
        normed_2,
        scale_2,
        vec,
        us=4,
    )
    da_cp = over_core(da)
    z, da_cp = lax.optimization_barrier((z, da_cp))
    dn1_mine, dn1_theirs, send = call(
        attend_grad_kernel,
        [((HALF, WIDTH), F32), ((HALF, WIDTH), BF), ((1024, REST), BF)],
        seq,
        da,
        da_cp,
        *os,
        *ws,
        *xs,
        weights,
        qkv,
        lse,
        n1,
        small_b,
        small_c,
        scratch=[
            pltpu.VMEM((ROWS, WIDTH), BF),
            pltpu.VMEM((ROWS, QKV_COLS), BF),
            pltpu.VMEM((EXTRA, WIDTH), F32),
        ],
        scalars=1,
        us=17,
    )
    send, z = lax.optimization_barrier((send, z))
    got = lax.all_to_all(send, ALL, 0, 0, tiled=True)
    dn1_two = dn1_mine + over_core(dn1_theirs).astype(F32)
    dn1_yp = over_y(dn1_two[PAD:].astype(BF))
    (g0,) = call(
        input_grad_kernel, [((1, TOK, WIDTH), F32)], dn1_two[:PAD], dn1_yp, dr, x, vec, us=2
    )
    y_mine, y_theirs = call(
        out_kernel, [((HALF, WIDTH), F32), ((HALF, WIDTH), BF)], z, hidden_w, us=4
    )
    y_two = y_mine + over_core(y_theirs).astype(F32)
    y = y_two[:PAD] + over_y(y_two[PAD:].astype(BF)).astype(F32) + r + vec[11]
    block_output = y[:TOK].astype(BF)[None]

    mine = jnp.where(ylo == 0, d_down[:32], d_down[32:]).astype(F32)
    theirs = jnp.where(ylo == 0, d_down[32:], d_down[:32])
    d_down = (mine + lax.ppermute(theirs, "ylo", SWAP).astype(F32))[None]
    (d_up,) = call(sum_up_kernel, [((1, 8, 4096), F32)], d_up.reshape(32, 32, 1024), us=3)
    d_qkv, d_out, d_fg, d_fs, d_qvb, d_ob, d_sg, d_ss, d_ub, d_db = call(
        sum_rest_kernel,
        [((1, 8, 3072), F32), ((1, 8, WIDTH), F32)]
        + [((1, n), F32) for n in (8, 8, 16, 8, 8, 8, 32, 8)],
        got.reshape(32, 32, REST),
        us=3,
    )
    return (
        block_output,
        g0,
        d_fg,
        d_fs,
        d_qkv,
        d_qvb,
        d_out,
        d_ob,
        d_sg,
        d_ss,
        d_up,
        d_ub,
        d_down,
        d_db,
    )


def solution(mesh):
    fine = Mesh(mesh.devices.reshape(2, 4, 4, 2, 2), ALL)
    tokens = P(DP, SEQ, None)
    vector = P(None, ALL)
    matrix = P(None, ALL, None)
    return jax.shard_map(
        body,
        mesh=fine,
        in_specs=(
            tokens,
            P(DP, SEQ),
            vector,
            vector,
            matrix,
            vector,
            matrix,
            vector,
            vector,
            vector,
            matrix,
            vector,
            matrix,
            vector,
            tokens,
        ),
        out_specs=(
            tokens,
            tokens,
            vector,
            vector,
            matrix,
            vector,
            matrix,
            vector,
            vector,
            vector,
            matrix,
            vector,
            matrix,
            vector,
        ),
        check_vma=False,
    )
```

```python
import jax
import jax.numpy as jnp
from jax import lax
from jax.experimental import pallas as pl
from jax.experimental.pallas import tpu as pltpu
from jax.sharding import Mesh, PartitionSpec as P

TOK = 145
PAD = 160
ROWS = 4 * PAD
HALF = 2 * PAD
SCALE = 1e9
WIDTH = 1024
BF = jnp.bfloat16
F32 = jnp.float32
DP = ("ylo", "z", "x")
SEQ = ("yhi", "core")
ALL = DP + SEQ
SWAP = [(0, 1), (1, 0)]
RELATIVE = (0, 2, 1, 3)
QKV_COLS = 768
OUT_COLS = 256
EXTRA = 128
REST = QKV_COLS + OUT_COLS + EXTRA


LINES_X = [[[(r * 4 + z) * 4 + x for x in range(4)] for z in range(4)] for r in range(2)]
LINES_Z = [[[(r * 4 + z) * 4 + x for z in range(4)] for x in range(4)] for r in range(2)]


def lines(along):
    return [
        [place * 4 + 2 * yhi + core for place in line]
        for core in range(2)
        for yhi in range(2)
        for half in along[core]
        for line in half
    ]


STAGE_A = lines((LINES_X, LINES_Z))
STAGE_B = lines((LINES_Z, LINES_X))


def exchange(v, groups):
    return lax.all_to_all(v, ALL, 0, 0, axis_index_groups=groups, tiled=True)


def over_y(v):
    return lax.ppermute(v, "yhi", SWAP)


def over_core(v):
    return lax.ppermute(v, "core", SWAP)


def dot(a, b):
    return jnp.dot(a, b, preferred_element_type=F32)


def dot_t(a, b):
    return lax.dot_general(a, b, (((1,), (1,)), ((), ())), preferred_element_type=F32)


def t_dot(a, b):
    return lax.dot_general(a, b, (((0,), (0,)), ((), ())), preferred_element_type=F32)


def iota(shape, dim):
    return lax.broadcasted_iota(jnp.int32, shape, dim)


def call(kernel, outs, *args, scratch=(), scalars=0, deps=(), us=0.0):
    vmem = pl.BlockSpec(memory_space=pltpu.VMEM)
    specs = [pl.BlockSpec(memory_space=pltpu.SMEM)] * scalars + [vmem] * (len(args) - scalars)
    specs += [pl.BlockSpec(memory_space=pl.ANY)] * len(deps)

    def run(*refs):
        kernel(*refs[: len(args)], *refs[len(args) + len(deps) :])

    return pl.pallas_call(
        run,
        out_shape=[jax.ShapeDtypeStruct(s, d) for s, d in outs],
        in_specs=specs,
        out_specs=[vmem] * len(outs),
        scratch_shapes=list(scratch),
        compiler_params=pltpu.CompilerParams(vmem_limit_bytes=60 * 2**20),
        cost_estimate=pl.CostEstimate(
            flops=int(us * SCALE), bytes_accessed=0, transcendentals=0
        ),
        name=kernel.__name__.removesuffix("_kernel"),
    )(*args, *deps)


def after(v, *deps):
    anywhere = pl.BlockSpec(memory_space=pl.ANY)
    return pl.pallas_call(
        lambda *refs: None,
        out_shape=jax.ShapeDtypeStruct(v.shape, v.dtype),
        in_specs=[anywhere] * (1 + len(deps)),
        out_specs=anywhere,
        input_output_aliases={0: 0},
        cost_estimate=pl.CostEstimate(flops=0, bytes_accessed=0, transcendentals=0),
        name="after",
    )(v, *deps)


def block(b):
    return slice(b * PAD, (b + 1) * PAD)


def norm_stats(v):
    average = jnp.mean(v, axis=-1, keepdims=True)
    centred = v - average
    variance = jnp.mean(centred * centred, axis=-1, keepdims=True)
    scale = lax.rsqrt(variance + 1e-06)
    return centred * scale, scale


def norm_back(grad, gain, normed, scale):
    e = grad * gain
    return scale * (
        e
        - jnp.mean(e, axis=-1, keepdims=True)
        - normed * jnp.mean(e * normed, axis=-1, keepdims=True)
    )


def piece_columns(refs):
    out = jnp.zeros((8, EXTRA), F32)
    lane = iota((8, EXTRA), 1)
    place = 0
    for ref in refs:
        size = ref.shape[1]
        for c in range(size // 8):
            spread = jnp.broadcast_to(ref[...].astype(F32), (8, size))
            hit = iota((8, size), 1) == iota((8, size), 0) + 8 * c
            column = jnp.sum(jnp.where(hit, spread, 0.0), axis=1, keepdims=True)
            out = jnp.where(lane == place, column, out)
            place += 1
    return out


def regroup(tile_of, source_of):
    lane = iota((8, 128), 1)
    tiles = []
    for t in range(8):
        tile = jnp.zeros((8, 128), F32)
        for a in range(4):
            source, b = source_of(t, a)
            part = tile_of(source)
            if a != b:
                part = pltpu.roll(part, (32 * (a - b)) % 128, 1)
            tile = jnp.where(lane // 32 == a, part, tile)
        tiles.append(tile)
    return jnp.concatenate(tiles, axis=1)


def image_of(t, a):
    return 16 * (a % 2) + 2 * t + a // 2


def hidden_place(dp):
    return (dp % 16) // 2, 2 * (dp % 2) + dp // 16


def tokens_kernel(x, mask, g, out, g_out, tok):
    row = jnp.zeros((8, WIDTH), F32)
    tok[0:8] = row
    tok[0:1, 0:TOK] = mask[...].astype(F32)
    row = tok[0:8]
    lifted = [pltpu.roll(row, PAD * b, 1)[0:1] if b else row[0:1] for b in range(4)]
    tok[0:TOK] = x[0].astype(F32)
    for b in range(4):
        tok[TOK + b : TOK + b + 1] = lifted[b]
    tok[TOK + 4 :] = jnp.zeros((PAD - TOK - 4, WIDTH), F32)
    out[...] = tok[...].astype(BF)
    tok[0:TOK] = g[0].astype(F32)
    tok[TOK:] = jnp.zeros((PAD - TOK, WIDTH), F32)
    g_out[...] = tok[...].astype(BF)


def up_columns_kernel(up, out):
    for s in range(4):
        cols = regroup(
            lambda dp: up[0, :, 128 * dp : 128 * dp + 128].astype(F32),
            lambda t, a: (image_of(t, a), s),
        ).astype(BF)
        for b in range(2):
            out[b, s] = cols


def prepare_kernel(qkv, out_w, fg, fs, qvb, ob, sg, ss, ub, db, send):
    extra = piece_columns([fg, fs, qvb, ob, sg, ss, ub, db])
    rows = []
    for s in range(4):
        parts = [qkv[0, :, 1024 * i + 256 * s : 1024 * i + 256 * s + 256] for i in range(3)]
        parts = [p.astype(F32) for p in parts]
        parts.append(out_w[0, :, 256 * s : 256 * s + 256].astype(F32))
        parts.append(extra)
        rows.append(jnp.concatenate(parts, axis=1))
    piece = jnp.concatenate(rows, axis=0).astype(BF)
    for d in range(32):
        send[d] = piece


def bias_hot(c):
    row, col = iota((128, 256), 0), iota((128, 256), 1)
    hit = (col // 16 == row // 8) & (col % 16 == 8 * c + row % 8)
    return jnp.where(hit, 1.0, 0.0).astype(BF)


def plane_place(core, zx):
    z, x = zx // 4, zx % 4
    return jnp.where(core == 0, x, z), jnp.where(core == 0, z, x)


def head_mask(h):
    return iota((1, 256), 1) // 64 == h


def masked(v, h):
    return jnp.where(head_mask(h), v, jnp.zeros_like(v))


def key_keep(x_own, x_yp, x_cp, x_dg):
    refs = (x_own, x_yp, x_cp, x_dg)
    return sum(r[TOK + b : TOK + b + 1, 0:ROWS].astype(F32) for b, r in enumerate(refs)) > 0


def attend_kernel(seq, x_own, x_yp, x_cp, x_dg, w, n1, qkv, o, lse, vec):
    s = seq[0]
    vec[...] = w[:, QKV_COLS + OUT_COLS : REST].astype(F32).T[0:16]
    gain, shift = vec[0:1], vec[1:2]
    for b, ref in enumerate((x_own, x_yp, x_cp, x_dg)):
        normed, _ = norm_stats(ref[...].astype(F32))
        n1[block(b)] = (normed * gain + shift).astype(BF)
    biases = []
    for start in (0, 512):
        at = pl.ds(pl.multiple_of(start + 128 * s, 128), 128)
        pieces = [jnp.broadcast_to(vec[2 + c : 3 + c, at], (8, 128)).astype(BF) for c in (0, 1)]
        biases.append((dot(pieces[0], bias_hot(0)) + dot(pieces[1], bias_hot(1)))[0:1])
    for i, bias in enumerate((biases[0], None, biases[1])):
        at = slice(256 * i, 256 * i + 256)
        proj = dot(n1[...], w[:, at])
        qkv[:, at] = (proj if bias is None else proj + bias).astype(BF)
    keep = key_keep(x_own, x_yp, x_cp, x_dg)
    q = qkv[:, 0:256] * jnp.asarray(0.125, BF)
    k, v = qkv[:, 256:512], qkv[:, 512:768]
    total = jnp.zeros((ROWS, 256), F32)
    logs = jnp.zeros((ROWS, 128), F32)
    for h in range(4):
        scores = jnp.where(keep, dot_t(masked(q, h), k), -1e30)
        peak = jnp.max(scores, axis=1, keepdims=True)
        powers = jnp.exp(scores - peak)
        weight = jnp.sum(powers, axis=1, keepdims=True)
        probs = (powers * (1.0 / weight)).astype(BF)
        total = total + dot(probs, masked(v, h))
        logs = jnp.where(iota((ROWS, 128), 1) == h, peak + jnp.log(weight), logs)
    o[...] = total.astype(BF)
    lse[...] = logs


def up_bias_row(vec, s):
    lane = iota((8, WIDTH), 1)
    out = jnp.zeros((8, WIDTH), F32)
    for c in range(4):
        row = jnp.broadcast_to(vec[7 + c : 8 + c], (8, WIDTH))
        row = pltpu.roll(row, lax.rem(8 * (c - s) + WIDTH, WIDTH), 1)
        out = jnp.where((lane // 8) % 4 == c, row, out)
    return regroup(
        lambda t: out[:, 128 * t : 128 * t + 128],
        lambda t, a: divmod(image_of(t, a), 4),
    )[0:1]


def hidden_kernel(
    seq,
    o_own,
    o_yp,
    o_cp,
    o_dg,
    x_own,
    x_yp,
    x_cp,
    x_dg,
    w_own,
    w_yp,
    w_cp,
    w_dg,
    vec,
    hidden_w,
    g_own,
    g_yp,
    g_cp,
    g_dg,
    n2,
    z,
    du,
    dm,
    dn2_mine,
    dn2_theirs,
    normed_out,
    scale_out,
    r_own,
    r,
):
    s = seq[0]
    place = [jnp.bitwise_xor(s, m) for m in RELATIVE]
    for b, ref in enumerate((g_own, g_yp, g_cp, g_dg)):
        dm[block(b)] = ref[...]
    heads = []
    for j, ref in enumerate((o_own, o_yp, o_cp, o_dg)):
        heads.append(jnp.concatenate([ref[block(b ^ j)] for b in range(4)], axis=0))
    for c, w in enumerate((w_own, w_yp, w_cp, w_dg)):
        total = jnp.zeros((ROWS, 256), F32)
        for j in range(4):
            rows = pl.ds(pl.multiple_of(256 * place[j], 256), 256)
            total = total + dot(heads[j], w[rows, :])
        r[:, pl.ds(pl.multiple_of(256 * place[c], 256), 256)] = total
    gain, shift, b_out = vec[5:6], vec[6:7], vec[4:5]
    for b, ref in enumerate((x_own, x_yp, x_cp, x_dg)):
        rows = r[block(b)] + ref[...].astype(F32) + b_out
        if b == 0:
            r_own[...] = rows
        normed, scale = norm_stats(rows)
        n2[block(b)] = (normed * gain + shift).astype(BF)
        if b < 2:
            normed_out[block(b)] = normed
            scale_out[block(b)] = jnp.broadcast_to(scale, (PAD, 128))
    bias = up_bias_row(vec, s)
    up = [hidden_w[:, 32 * b : 32 * b + 32, 0:1024].reshape(512, 1024) for b in range(2)]
    down = hidden_w[:, :, 1024:].reshape(1024, 1024)
    for c in range(4):
        at = slice(256 * c, 256 * c + 256)
        u = dot(n2[:, 0:512], up[0][:, at]) + dot(n2[:, 512:], up[1][:, at]) + bias[:, at]
        cdf = 0.5 * (1.0 + lax.erf(u * (0.5**0.5)))
        z[:, at] = (u * cdf).astype(BF)
        slope = cdf + u * jnp.exp(-0.5 * u * u) * 0.3989422804014327
        du[:, at] = (slope * dot_t(dm[...], down[at, :])).astype(BF)
    for b in range(2):
        at = slice(512 * b, 512 * b + 512)
        dn2_mine[:, at] = dot_t(du[0:HALF], up[b])
        dn2_theirs[:, at] = dot_t(du[HALF:], up[b]).astype(BF)


def hidden_grad_kernel(core, z, du, dm, n2, hidden_w, out, small, y_mine, y_theirs):
    down = hidden_w[:, :, 1024:].reshape(1024, 1024)
    y_mine[...] = dot(z[0:HALF], down)
    y_theirs[...] = dot(z[HALF:], down).astype(BF)
    d_up = t_dot(n2[...], du[...]).astype(BF)
    d_down = t_dot(z[...], dm[...]).astype(BF)
    for zx in range(16):
        a, b = plane_place(core[0], zx)
        for half in range(2):
            rows = slice(512 * half + 32 * zx, 512 * half + 32 * zx + 32)
            out[a, b, 32 * half : 32 * half + 32, 0:1024] = d_up[rows]
        out[a, b, :, 1024:] = d_down[64 * zx : 64 * zx + 64]
    small[...] = jnp.zeros((8, WIDTH), F32)
    sums = jnp.broadcast_to(jnp.sum(du[...].astype(F32), axis=0, keepdims=True), (8, WIDTH))
    small[0:1] = regroup(
        lambda t: sums[:, 128 * t : 128 * t + 128],
        lambda t, b: hidden_place(4 * t + b),
    )[0:1]
    small[1:2] = jnp.sum(dm[block(0)].astype(F32), axis=0, keepdims=True)


def residual_kernel(two, got, g_own, g_yp, normed, scale, vec, da, dr, small):
    gain = vec[5:6]
    small[...] = jnp.zeros((8, WIDTH), F32)
    for b, ref in enumerate((g_own, g_yp)):
        dn2 = two[block(b)].astype(F32) + got[block(1 - b)].astype(F32)
        grad = ref[...].astype(F32) + norm_back(dn2, gain, normed[block(b)], scale[block(b), 0:1])
        low = grad.astype(BF)
        da[block(b)] = low
        if b == 0:
            dr[...] = grad
            small[0:1] = jnp.sum(low.astype(F32), axis=0, keepdims=True)
            small[1:2] = jnp.sum(dn2 * normed[block(b)], axis=0, keepdims=True)
            small[2:3] = jnp.sum(dn2, axis=0, keepdims=True)


def attend_grad_kernel(
    seq,
    core,
    da_mine,
    da_cp,
    w_own,
    w_yp,
    w_cp,
    w_dg,
    x_own,
    x_yp,
    x_cp,
    x_dg,
    qkv_w,
    qkv,
    lse,
    n1,
    o_own,
    o_yp,
    o_cp,
    o_dg,
    small_b,
    small_c,
    dn1_mine,
    dn1_theirs,
    send,
    da,
    d_proj,
    rows_out,
    natural,
):
    s = seq[0]
    place = [jnp.bitwise_xor(s, m) for m in RELATIVE]
    da[0:HALF] = da_mine[...]
    da[HALF:] = da_cp[...]
    own_rows = pl.ds(pl.multiple_of(256 * s, 256), 256)
    grad_o = jnp.zeros((ROWS, 256), F32)
    for c, w in enumerate((w_own, w_yp, w_cp, w_dg)):
        cols = pl.ds(pl.multiple_of(256 * place[c], 256), 256)
        grad_o = grad_o + dot_t(da[:, cols], w[own_rows, :])
    do = grad_o.astype(BF)
    keep = key_keep(x_own, x_yp, x_cp, x_dg)
    q, k, v = qkv[:, 0:256], qkv[:, 256:512], qkv[:, 512:768]
    scaled = q * jnp.asarray(0.125, BF)
    dq, dk, dv = (jnp.zeros((ROWS, 256), F32) for _ in range(3))
    for h in range(4):
        scores = jnp.where(keep, dot_t(masked(scaled, h), k), -1e30)
        probs = jnp.exp(scores - lse[:, h : h + 1])
        do_h = masked(do, h)
        d_probs = dot_t(do_h, v)
        inner = jnp.sum(probs * d_probs, axis=1, keepdims=True)
        ds = (probs * (d_probs - inner)).astype(BF)
        dq = dq + dot(ds, masked(k, h))
        dk = dk + t_dot(ds, masked(q, h))
        dv = dv + t_dot(probs.astype(BF), do_h)
    d_proj[:, 0:256] = (dq * 0.125).astype(BF)
    d_proj[:, 256:512] = (dk * 0.125).astype(BF)
    d_proj[:, 512:768] = dv.astype(BF)
    d_gain = jnp.zeros((1, WIDTH), F32)
    d_shift = jnp.zeros((1, WIDTH), F32)
    for b, ref in enumerate((x_own, x_yp, x_cp, x_dg)):
        normed, _ = norm_stats(ref[...].astype(F32))
        part = dot_t(d_proj[block(b)], qkv_w[:, 0:QKV_COLS])
        d_gain = d_gain + jnp.sum(part * normed, axis=0, keepdims=True)
        d_shift = d_shift + jnp.sum(part, axis=0, keepdims=True)
        if b < 2:
            dn1_mine[block(b)] = part
        else:
            dn1_theirs[block(b - 2)] = part.astype(BF)
    natural[:, 0:QKV_COLS] = t_dot(n1[...], d_proj[...]).astype(BF)
    my_cols = pl.ds(pl.multiple_of(256 * s, 256), 256)
    for j, ref in enumerate((o_own, o_yp, o_cp, o_dg)):
        heads = jnp.concatenate([ref[block(b ^ j)] for b in range(4)], axis=0)
        rows = pl.ds(pl.multiple_of(256 * place[j], 256), 256)
        natural[rows, QKV_COLS : QKV_COLS + OUT_COLS] = t_dot(heads, da[:, my_cols]).astype(BF)
    rows_out[...] = jnp.zeros((EXTRA, WIDTH), F32)
    rows_out[0:1] = d_gain
    rows_out[1:2] = d_shift
    for start, first in ((0, 0), (512, 512)):
        sums = jnp.sum(d_proj[:, first : first + 256].astype(F32), axis=0, keepdims=True)
        sums = jnp.broadcast_to(sums, (8, 256)).astype(BF)
        at = pl.ds(pl.multiple_of(start + 128 * s, 128), 128)
        for c in (0, 1):
            rows_out[2 + c : 3 + c, at] = dot_t(sums, bias_hot(c))[0:1]
    rows_out[4:7] = small_c[0:3]
    lane = iota((8, WIDTH), 1)
    row = jnp.broadcast_to(small_b[0:1], (8, WIDTH))
    for c in range(4):
        part = jnp.where((lane // 8) % 4 == c, row, 0.0)
        rows_out[7 + c : 8 + c] = pltpu.roll(part, lax.rem(8 * (s - c) + WIDTH, WIDTH), 1)[0:1]
    rows_out[11:12] = small_b[1:2]
    natural[:, QKV_COLS + OUT_COLS :] = rows_out[...].T.astype(BF)
    for zx in range(16):
        a, b = plane_place(core[0], zx)
        for half in range(2):
            rows = slice(512 * half + 32 * zx, 512 * half + 32 * zx + 32)
            send[a, b, 32 * half : 32 * half + 32] = natural[rows]


def input_grad_kernel(mine, got_cp, got_yp, dr, x_own, vec, out):
    normed, scale = norm_stats(x_own[...].astype(F32))
    dn1 = mine[block(0)] + got_cp[block(0)].astype(F32) + got_yp[...].astype(F32)
    grad = dr[...] + norm_back(dn1, vec[0:1], normed, scale)
    out[:, 0] = grad[0:TOK]


def output_kernel(mine, got_cp, got_yp, r, vec, out):
    y = mine[block(0)] + got_cp[block(0)].astype(F32) + got_yp[...].astype(F32)
    out[0] = (y + r[...] + vec[11:12])[0:TOK].astype(BF)


def bulk_kernel(ylo, up, down_own, down_yp, out, pair):
    pair[ylo[0]] = down_own[...]
    pair[1 - ylo[0]] = down_yp[...]
    out[:, 0:1024] = up[...]
    for b in range(2):
        out[32 * b : 32 * b + 32, 1024:] = pair[b]


def sum_of(ref):
    total = ref[0].astype(F32)
    for d in range(1, ref.shape[0]):
        total = total + ref[d].astype(F32)
    return total


def sum_low_kernel(got, out):
    out[...] = sum_of(got).astype(BF)


def sum_join_kernel(got, hidden, out):
    out[:, 0:REST] = sum_of(got).astype(BF)
    out[:, REST:] = hidden[:, 0:1024]


def sum_down_kernel(ylo, part, got, out):
    rows = pl.ds(pl.multiple_of(32 * ylo[0], 32), 32)
    out[0] = part[rows, 1024:].astype(F32) + got[...].astype(F32)


def sum_rest_kernel(got, up, qkv, out, *vectors):
    total = jnp.concatenate(
        [got[s].astype(F32) + got[4 + s].astype(F32) for s in range(4)], axis=0
    )
    lane = iota((8, 128), 1)
    for dp in range(32):
        t, a = hidden_place(dp)
        tile = jnp.zeros((8, 128), F32)
        for s in range(4):
            part = total[8 * s : 8 * s + 8, REST + 128 * t : REST + 128 * t + 128]
            if s != a:
                part = pltpu.roll(part, (32 * (s - a)) % 128, 1)
            tile = jnp.where(lane // 32 == s, part, tile)
        up[0, :, 128 * dp : 128 * dp + 128] = tile
    for s in range(4):
        rows = slice(8 * s, 8 * s + 8)
        for i in range(3):
            at = 1024 * i + 256 * s
            qkv[0, :, at : at + 256] = total[rows, 256 * i : 256 * i + 256]
        out[0, :, 256 * s : 256 * s + 256] = total[rows, QKV_COLS : QKV_COLS + OUT_COLS]
    extra = sum(total[8 * s : 8 * s + 8, QKV_COLS + OUT_COLS : REST] for s in range(4))
    place = 0
    for ref in vectors:
        size = ref.shape[1]
        value = jnp.zeros((8, size), F32)
        for c in range(size // 8):
            column = jnp.broadcast_to(extra[:, place : place + 1], (8, size))
            hit = iota((8, size), 1) == iota((8, size), 0) + 8 * c
            value = jnp.where(hit, column, value)
            place += 1
        ref[...] = jnp.sum(value, axis=0, keepdims=True)


def body(
    inputs,
    token_mask,
    first_gain,
    first_shift,
    qkv_weight,
    qv_bias,
    out_weight,
    out_bias,
    second_gain,
    second_shift,
    up_weight,
    up_bias,
    down_weight,
    down_bias,
    cotangent,
):
    core = lax.axis_index("core").astype(jnp.int32).reshape(1)
    seq = lax.axis_index("yhi").astype(jnp.int32).reshape(1) * 2 + core
    ylo = lax.axis_index("ylo").astype(jnp.int32).reshape(1)
    down_yp = lax.ppermute(down_weight[0], "ylo", SWAP)

    x, g = call(
        tokens_kernel,
        [((PAD, WIDTH), BF), ((PAD, WIDTH), BF)],
        inputs,
        token_mask,
        cotangent,
        scratch=[pltpu.VMEM((PAD, WIDTH), F32)],
        us=2,
    )
    (up_send,) = call(up_columns_kernel, [((2, 4, 8, 1024), BF)], up_weight, deps=(x,), us=2)
    up_got = lax.all_to_all(
        up_send.reshape(64, 1024), ("ylo", "yhi", "core"), 0, 0, tiled=True
    )
    x_yp, g_yp = over_y(x), over_y(g)
    (send,) = call(
        prepare_kernel,
        [((32, 32, REST), BF)],
        qkv_weight,
        out_weight,
        first_gain,
        first_shift,
        qv_bias,
        out_bias,
        second_gain,
        second_shift,
        up_bias,
        down_bias,
        deps=(up_send,),
        us=300,
    )
    (bulk,) = call(
        bulk_kernel,
        [((64, 2048), BF)],
        ylo,
        up_got,
        down_weight[0],
        down_yp,
        scratch=[pltpu.VMEM((2, 32, WIDTH), BF)],
        scalars=1,
        deps=(send, x_yp),
    )
    hidden_w = lax.all_gather(bulk, ("z", "x"), axis=0, tiled=True).reshape(16, 64, 2048)
    send = after(send, bulk)
    weights = lax.all_to_all(send.reshape(1024, REST), ALL, 0, 0, tiled=True)
    xs = (x, x_yp, over_core(x), over_core(x_yp))
    gs = (g, g_yp, over_core(g), over_core(g_yp))
    w_own = weights[:, QKV_COLS : QKV_COLS + OUT_COLS]
    w_yp = over_y(w_own)
    ws = (w_own, w_yp, over_core(w_own), over_core(w_yp))

    n1, qkv, o, lse, vec = call(
        attend_kernel,
        [
            ((ROWS, WIDTH), BF),
            ((ROWS, QKV_COLS), BF),
            ((ROWS, 256), BF),
            ((ROWS, 128), F32),
            ((16, WIDTH), F32),
        ],
        seq,
        *xs,
        weights,
        scalars=1,
        us=8,
        deps=(g_yp,),
    )
    o_yp = over_y(o)
    os = (o, o_yp, over_core(o), over_core(o_yp))
    n2, z, du, dm, dn2_mine, dn2_theirs, normed_2, scale_2, r = call(
        hidden_kernel,
        [
            ((ROWS, WIDTH), BF),
            ((ROWS, WIDTH), BF),
            ((ROWS, WIDTH), BF),
            ((ROWS, WIDTH), BF),
            ((HALF, WIDTH), F32),
            ((HALF, WIDTH), BF),
            ((HALF, WIDTH), F32),
            ((HALF, 128), F32),
            ((PAD, WIDTH), F32),
        ],
        seq,
        *os,
        *xs,
        *ws,
        vec,
        hidden_w,
        *gs,
        scratch=[pltpu.VMEM((ROWS, WIDTH), F32)],
        scalars=1,
        us=12,
    )
    two = (dn2_mine + over_core(dn2_theirs).astype(F32)).astype(BF)
    two_yp = over_y(two)
    d_hidden, small_b, y_mine, y_theirs = call(
        hidden_grad_kernel,
        [
            ((4, 4, 64, 2048), BF),
            ((8, WIDTH), F32),
            ((HALF, WIDTH), F32),
            ((HALF, WIDTH), BF),
        ],
        core,
        z,
        du,
        dm,
        n2,
        hidden_w,
        scalars=1,
        deps=(over_core(two[:16, :128]),),
        us=300,
    )
    d_hidden = lax.psum_scatter(
        d_hidden.reshape(1024, 2048),
        ALL,
        axis_index_groups=STAGE_A,
        scatter_dimension=0,
        tiled=True,
    )
    y_cp = over_core(y_theirs)
    da, dr, small_c = call(
        residual_kernel,
        [((HALF, WIDTH), BF), ((PAD, WIDTH), F32), ((8, WIDTH), F32)],
        two,
        two_yp,
        g,
        g_yp,
        normed_2,
        scale_2,
        vec,
        deps=(y_theirs,),
        us=150,
    )
    da_cp = over_core(da)
    y_low = (y_mine[PAD:] + y_cp[PAD:].astype(F32)).astype(BF)
    y_yp = over_y(y_low)
    dn1_mine, dn1_theirs, send = call(
        attend_grad_kernel,
        [((HALF, WIDTH), F32), ((HALF, WIDTH), BF), ((4, 4, 64, REST), BF)],
        seq,
        core,
        da,
        da_cp,
        *ws,
        *xs,
        weights,
        qkv,
        lse,
        n1,
        *os,
        small_b,
        small_c,
        scratch=[
            pltpu.VMEM((ROWS, WIDTH), BF),
            pltpu.VMEM((ROWS, QKV_COLS), BF),
            pltpu.VMEM((EXTRA, WIDTH), F32),
            pltpu.VMEM((1024, REST), BF),
        ],
        scalars=2,
        deps=(y_low,),
        us=15,
    )
    got = exchange(send.reshape(1024, REST), STAGE_A)
    dn1_cp = over_core(dn1_theirs)
    d_hidden = lax.psum_scatter(
        d_hidden, ALL, axis_index_groups=STAGE_B, scatter_dimension=0, tiled=True
    )
    dn1_low = (dn1_mine[PAD:] + dn1_cp[PAD:].astype(F32)).astype(BF)
    dn1_yp = over_y(dn1_low)
    (got,) = call(sum_low_kernel, [((256, REST), BF)], got.reshape(4, 256, REST))
    got = exchange(got, STAGE_B)
    (block_output,) = call(
        output_kernel, [((1, TOK, WIDTH), BF)], y_mine, y_cp, y_yp, r, vec
    )
    (g0,) = call(
        input_grad_kernel,
        [((TOK, 1, WIDTH), F32)],
        dn1_mine,
        dn1_cp,
        dn1_yp,
        dr,
        x,
        vec,
    )
    g0 = g0.transpose(1, 0, 2)
    (last,) = call(
        sum_join_kernel,
        [((64, REST + 1024), BF)],
        got.reshape(4, 64, REST),
        d_hidden,
        deps=(block_output, g0),
    )
    got = lax.all_to_all(last, ("ylo", "yhi", "core"), 0, 0, tiled=True)
    theirs = jnp.where(ylo[0] == 0, d_hidden[32:, 1024:], d_hidden[:32, 1024:])
    (d_down,) = call(
        sum_down_kernel,
        [((1, 32, WIDTH), F32)],
        ylo,
        d_hidden,
        lax.ppermute(theirs, "ylo", SWAP),
        scalars=1,
    )
    d_up, d_qkv, d_out, d_fg, d_fs, d_qvb, d_ob, d_sg, d_ss, d_ub, d_db = call(
        sum_rest_kernel,
        [((1, 8, 4096), F32), ((1, 8, 3072), F32), ((1, 8, WIDTH), F32)]
        + [((1, n), F32) for n in (8, 8, 16, 8, 8, 8, 32, 8)],
        got.reshape(8, 8, REST + 1024),
        deps=(d_down,),
    )
    return (
        block_output,
        g0,
        d_fg,
        d_fs,
        d_qkv,
        d_qvb,
        d_out,
        d_ob,
        d_sg,
        d_ss,
        d_up,
        d_ub,
        d_down,
        d_db,
    )


def solution(mesh):
    fine = Mesh(mesh.devices.reshape(2, 4, 4, 2, 2), ALL)
    tokens = P(DP, SEQ, None)
    vector = P(None, ALL)
    matrix = P(None, ALL, None)
    return jax.shard_map(
        body,
        mesh=fine,
        in_specs=(
            tokens,
            P(DP, SEQ),
            vector,
            vector,
            matrix,
            vector,
            matrix,
            vector,
            vector,
            vector,
            matrix,
            vector,
            matrix,
            vector,
            tokens,
        ),
        out_specs=(
            tokens,
            tokens,
            vector,
            vector,
            matrix,
            vector,
            matrix,
            vector,
            vector,
            vector,
            matrix,
            vector,
            matrix,
            vector,
        ),
        check_vma=False,
    )
```

```python
import functools

import jax
import jax.numpy as jnp
from jax import lax
from jax.experimental import pallas as pl
from jax.experimental.pallas import tpu as pltpu
from jax.sharding import Mesh, PartitionSpec as P

TOK = 145
PAD = 160
ROWS = 4 * PAD
HALF = 2 * PAD
SCALE = 1e9
HBM = pltpu.HBM
WIDTH = 1024
BF = jnp.bfloat16
F32 = jnp.float32
DP = ("ylo", "z", "x")
SEQ = ("yhi", "core")
ALL = DP + SEQ
SWAP = [(0, 1), (1, 0)]
RELATIVE = (0, 2, 1, 3)
QKV_COLS = 768
OUT_COLS = 256
EXTRA = 128
REST = QKV_COLS + OUT_COLS + EXTRA
JOINT = REST + 2048


LINES_X = [[[(r * 4 + z) * 4 + x for x in range(4)] for z in range(4)] for r in range(2)]
LINES_Z = [[[(r * 4 + z) * 4 + x for z in range(4)] for x in range(4)] for r in range(2)]


def lines(along):
    return [
        [place * 4 + 2 * yhi + core for place in line]
        for core in range(2)
        for yhi in range(2)
        for half in along[core]
        for line in half
    ]


STAGE_A = lines((LINES_X, LINES_Z))
STAGE_B = lines((LINES_Z, LINES_X))


def exchange(v, groups):
    return lax.all_to_all(v, ALL, 0, 0, axis_index_groups=groups, tiled=True)


def over_y(v):
    return lax.ppermute(v, "yhi", SWAP)


def over_core(v):
    return lax.ppermute(v, "core", SWAP)


def dot(a, b):
    return jnp.dot(a, b, preferred_element_type=F32)


def dot_t(a, b):
    return lax.dot_general(a, b, (((1,), (1,)), ((), ())), preferred_element_type=F32)


def t_dot(a, b):
    return lax.dot_general(a, b, (((0,), (0,)), ((), ())), preferred_element_type=F32)


def iota(shape, dim):
    return lax.broadcasted_iota(jnp.int32, shape, dim)


def call(kernel, outs, *args, scratch=(), scalars=0, deps=(), us=0.0, room=32):
    vmem = pl.BlockSpec(memory_space=pltpu.VMEM)
    specs = [pl.BlockSpec(memory_space=pltpu.SMEM)] * scalars + [vmem] * (len(args) - scalars)
    specs += [pl.BlockSpec(memory_space=pl.ANY)] * len(deps)

    def run(*refs):
        kernel(*refs[: len(args)], *refs[len(args) + len(deps) :])

    return pl.pallas_call(
        run,
        out_shape=[(o[2] if len(o) > 2 else jax.ShapeDtypeStruct)(o[0], o[1]) for o in outs],
        in_specs=specs,
        out_specs=[vmem] * len(outs),
        scratch_shapes=list(scratch),
        compiler_params=pltpu.CompilerParams(vmem_limit_bytes=room * 2**20),
        cost_estimate=pl.CostEstimate(
            flops=int(us * SCALE), bytes_accessed=0, transcendentals=0
        ),
        name=getattr(kernel, "func", kernel).__name__.removesuffix("_kernel"),
    )(*args, *deps)


def hbm(*values):
    return tuple(pltpu.with_memory_space_constraint(v, HBM) for v in values)


def after(v, *deps):
    anywhere = pl.BlockSpec(memory_space=pl.ANY)
    return pl.pallas_call(
        lambda *refs: None,
        out_shape=jax.ShapeDtypeStruct(v.shape, v.dtype),
        in_specs=[anywhere] * (1 + len(deps)),
        out_specs=anywhere,
        input_output_aliases={0: 0},
        cost_estimate=pl.CostEstimate(flops=0, bytes_accessed=0, transcendentals=0),
        name="after",
    )(v, *deps)


def block(b):
    return slice(b * PAD, (b + 1) * PAD)


def norm_stats(v):
    average = jnp.mean(v, axis=-1, keepdims=True)
    centred = v - average
    variance = jnp.mean(centred * centred, axis=-1, keepdims=True)
    scale = lax.rsqrt(variance + 1e-06)
    return centred * scale, scale


def norm_back(grad, gain, normed, scale):
    e = grad * gain
    return scale * (
        e
        - jnp.mean(e, axis=-1, keepdims=True)
        - normed * jnp.mean(e * normed, axis=-1, keepdims=True)
    )


def piece_columns(refs):
    out = jnp.zeros((8, EXTRA), F32)
    lane = iota((8, EXTRA), 1)
    place = 0
    for ref in refs:
        size = ref.shape[1]
        for c in range(size // 8):
            spread = jnp.broadcast_to(ref[...].astype(F32), (8, size))
            hit = iota((8, size), 1) == iota((8, size), 0) + 8 * c
            column = jnp.sum(jnp.where(hit, spread, 0.0), axis=1, keepdims=True)
            out = jnp.where(lane == place, column, out)
            place += 1
    return out


def hidden_hot():
    row, col = iota((512, 512), 0), iota((512, 512), 1)
    hit = row == 32 * (col % 128 // 8) + 8 * (col // 128) + col % 8
    return jnp.where(hit, 1.0, 0.0).astype(BF)


def tokens_kernel(x, mask, g, out, g_out, tok):
    row = jnp.zeros((8, WIDTH), F32)
    tok[0:8] = row
    tok[0:1, 0:TOK] = mask[...].astype(F32)
    row = tok[0:8]
    lifted = [pltpu.roll(row, PAD * b, 1)[0:1] if b else row[0:1] for b in range(4)]
    tok[0:TOK] = x[0].astype(F32)
    for b in range(4):
        tok[TOK + b : TOK + b + 1] = lifted[b]
    tok[TOK + 4 :] = jnp.zeros((PAD - TOK - 4, WIDTH), F32)
    out[...] = tok[...].astype(BF)
    tok[0:TOK] = g[0].astype(F32)
    tok[TOK:] = jnp.zeros((PAD - TOK, WIDTH), F32)
    g_out[...] = tok[...].astype(BF)


def prepare_kernel(qkv, out_w, up, down, fg, fs, qvb, ob, sg, ss, ub, db, send):
    extra = piece_columns([fg, fs, qvb, ob, sg, ss, ub, db])
    rows = jnp.concatenate([up[0, :, 512 * t : 512 * t + 512] for t in range(8)], axis=0)
    up_cols = dot(rows, hidden_hot())
    for s in range(4):
        parts = [qkv[0, :, 1024 * i + 256 * s : 1024 * i + 256 * s + 256] for i in range(3)]
        parts = [p.astype(F32) for p in parts]
        parts.append(out_w[0, :, 256 * s : 256 * s + 256].astype(F32))
        parts.append(extra)
        parts += [up_cols[8 * t : 8 * t + 8, 128 * s : 128 * s + 128] for t in range(8)]
        parts.append(down[0, 8 * s : 8 * s + 8].astype(F32))
        piece = jnp.concatenate(parts, axis=1).astype(BF)
        for b in range(2):
            send[b, s] = piece


def spread_kernel(pieces, out):
    for d in range(4):
        out[d] = pieces[...]


def copies_kernel(first, got, out):
    width = out.shape[2]
    part = got[:, first : first + width]
    for d in range(4):
        out[d] = part


def unpack_kernel(core, got, w_qkv, w_out, vec, extra):
    for zx in range(16):
        a, b = plane_place(core[0], zx)
        for half in range(2):
            rows = slice(512 * half + 32 * zx, 512 * half + 32 * zx + 32)
            part = got[b, a, 32 * half : 32 * half + 32]
            w_qkv[rows] = part[:, 0:QKV_COLS]
            w_out[rows] = part[:, QKV_COLS : QKV_COLS + OUT_COLS]
            extra[rows] = part[:, QKV_COLS + OUT_COLS :].astype(F32)
    vec[...] = extra[...].T[0:16]


def bias_hot(c):
    row, col = iota((128, 256), 0), iota((128, 256), 1)
    hit = (col // 16 == row // 8) & (col % 16 == 8 * c + row % 8)
    return jnp.where(hit, 1.0, 0.0).astype(BF)


def plane_place(core, zx):
    z, x = zx // 4, zx % 4
    return jnp.where(core == 0, x, z), jnp.where(core == 0, z, x)


def head_mask(h):
    return iota((1, 256), 1) // 64 == h


def masked(v, h):
    return jnp.where(head_mask(h), v, jnp.zeros_like(v))


def key_keep(x_own, x_yp, x_cp, x_dg):
    refs = (x_own, x_yp, x_cp, x_dg)
    return sum(r[TOK + b : TOK + b + 1, 0:ROWS].astype(F32) for b, r in enumerate(refs)) > 0


def attend_kernel(seq, x_own, x_yp, x_cp, x_dg, w, vec, n1, qkv, o, lse):
    s = seq[0]
    gain, shift = vec[0:1], vec[1:2]
    for b, ref in enumerate((x_own, x_yp, x_cp, x_dg)):
        normed, _ = norm_stats(ref[...].astype(F32))
        n1[block(b)] = (normed * gain + shift).astype(BF)
    biases = []
    for start in (0, 512):
        at = pl.ds(pl.multiple_of(start + 128 * s, 128), 128)
        pieces = [jnp.broadcast_to(vec[2 + c : 3 + c, at], (8, 128)).astype(BF) for c in (0, 1)]
        biases.append((dot(pieces[0], bias_hot(0)) + dot(pieces[1], bias_hot(1)))[0:1])
    for i, bias in enumerate((biases[0], None, biases[1])):
        at = slice(256 * i, 256 * i + 256)
        proj = dot(n1[...], w[:, at])
        qkv[:, at] = (proj if bias is None else proj + bias).astype(BF)
    keep = key_keep(x_own, x_yp, x_cp, x_dg)
    q = qkv[:, 0:256] * jnp.asarray(0.125, BF)
    k, v = qkv[:, 256:512], qkv[:, 512:768]
    total = jnp.zeros((ROWS, 256), F32)
    logs = jnp.zeros((ROWS, 128), F32)
    for h in range(4):
        scores = jnp.where(keep, dot_t(masked(q, h), k), -1e30)
        peak = jnp.max(scores, axis=1, keepdims=True)
        powers = jnp.exp(scores - peak)
        weight = jnp.sum(powers, axis=1, keepdims=True)
        probs = (powers * (1.0 / weight)).astype(BF)
        total = total + dot(probs, masked(v, h))
        logs = jnp.where(iota((ROWS, 128), 1) == h, peak + jnp.log(weight), logs)
    o[...] = total.astype(BF)
    lse[...] = logs


def hidden_kernel(
    seq,
    o_own,
    o_yp,
    o_cp,
    o_dg,
    x_own,
    x_yp,
    x_cp,
    x_dg,
    w_own,
    w_yp,
    w_cp,
    w_dg,
    vec,
    hidden_got,
    g_own,
    g_yp,
    g_cp,
    g_dg,
    n2,
    z,
    du,
    dn2_mine,
    dn2_theirs,
    normed_out,
    scale_out,
    down,
    r_own,
    r,
    up,
    dm,
):
    s = seq[0]
    place = [jnp.bitwise_xor(s, m) for m in RELATIVE]
    for b, ref in enumerate((g_own, g_yp, g_cp, g_dg)):
        dm[block(b)] = ref[...]
    heads = []
    for j, ref in enumerate((o_own, o_yp, o_cp, o_dg)):
        heads.append(jnp.concatenate([ref[block(b ^ j)] for b in range(4)], axis=0))
    for c, w in enumerate((w_own, w_yp, w_cp, w_dg)):
        total = jnp.zeros((ROWS, 256), F32)
        for j in range(4):
            rows = pl.ds(pl.multiple_of(256 * place[j], 256), 256)
            total = total + dot(heads[j], w[rows, :])
        r[:, pl.ds(pl.multiple_of(256 * place[c], 256), 256)] = total
    gain, shift, b_out = vec[5:6], vec[6:7], vec[4:5]
    for b, ref in enumerate((x_own, x_yp, x_cp, x_dg)):
        rows = r[block(b)] + ref[...].astype(F32) + b_out
        if b == 0:
            r_own[...] = rows
        normed, scale = norm_stats(rows)
        n2[block(b)] = (normed * gain + shift).astype(BF)
        if b < 2:
            normed_out[block(b)] = normed
            scale_out[block(b)] = jnp.broadcast_to(scale, (PAD, 128))
    bias = vec[pl.ds(7 + s, 1)]
    for zx in range(16):
        a, b = plane_place(s % 2, zx)
        for half in range(2):
            rows = slice(512 * half + 32 * zx, 512 * half + 32 * zx + 32)
            part = hidden_got[b, a, 32 * half : 32 * half + 32]
            up[rows] = part[:, 0:1024]
            down[rows] = part[:, 1024:]
    for c in range(4):
        at = slice(256 * c, 256 * c + 256)
        u = dot(n2[...], up[:, at]) + bias[:, at]
        cdf = 0.5 * (1.0 + lax.erf(u * (0.5**0.5)))
        z[:, at] = (u * cdf).astype(BF)
        slope = cdf + u * jnp.exp(-0.5 * u * u) * 0.3989422804014327
        du[:, at] = (slope * dot_t(dm[...], down[at, :])).astype(BF)
    dn2_mine[...] = dot_t(du[0:HALF], up[...])
    dn2_theirs[...] = dot_t(du[HALF:], up[...]).astype(BF)


def hidden_grad_kernel(
    core, z, du, n2, down, g_own, g_yp, g_cp, g_dg, out, small, y_mine, y_theirs
):
    y_mine[...] = dot(z[0:HALF], down[...])
    y_theirs[...] = dot(z[HALF:], down[...]).astype(BF)
    dm = jnp.concatenate([g[...] for g in (g_own, g_yp, g_cp, g_dg)], axis=0)
    d_up = t_dot(n2[...], du[...]).astype(BF)
    d_down = t_dot(z[...], dm).astype(BF)
    for zx in range(16):
        a, b = plane_place(core[0], zx)
        for half in range(2):
            rows = slice(512 * half + 32 * zx, 512 * half + 32 * zx + 32)
            out[a, b, 32 * half : 32 * half + 32, 0:1024] = d_up[rows]
            out[a, b, 32 * half : 32 * half + 32, 1024:] = d_down[rows]
    small[...] = jnp.zeros((8, WIDTH), F32)
    small[0:1] = jnp.sum(du[...].astype(F32), axis=0, keepdims=True)
    small[1:2] = jnp.sum(g_own[...].astype(F32), axis=0, keepdims=True)


def residual_kernel(two, got, g_own, g_yp, normed, scale, vec, da, dr, small):
    gain = vec[5:6]
    small[...] = jnp.zeros((8, WIDTH), F32)
    for b, ref in enumerate((g_own, g_yp)):
        dn2 = two[block(b)].astype(F32) + got[block(1 - b)].astype(F32)
        grad = ref[...].astype(F32) + norm_back(dn2, gain, normed[block(b)], scale[block(b), 0:1])
        low = grad.astype(BF)
        da[block(b)] = low
        if b == 0:
            dr[...] = grad
            small[0:1] = jnp.sum(low.astype(F32), axis=0, keepdims=True)
            small[1:2] = jnp.sum(dn2 * normed[block(b)], axis=0, keepdims=True)
            small[2:3] = jnp.sum(dn2, axis=0, keepdims=True)


def attend_grad_kernel(
    seq,
    core,
    da_mine,
    da_cp,
    w_own,
    w_yp,
    w_cp,
    w_dg,
    x_own,
    x_yp,
    x_cp,
    x_dg,
    qkv_w,
    qkv,
    lse,
    n1,
    o_own,
    o_yp,
    o_cp,
    o_dg,
    small_b,
    small_c,
    dn1_mine,
    dn1_theirs,
    send,
    da,
    d_proj,
    rows_out,
    natural,
):
    s = seq[0]
    place = [jnp.bitwise_xor(s, m) for m in RELATIVE]
    da[0:HALF] = da_mine[...]
    da[HALF:] = da_cp[...]
    own_rows = pl.ds(pl.multiple_of(256 * s, 256), 256)
    grad_o = jnp.zeros((ROWS, 256), F32)
    for c, w in enumerate((w_own, w_yp, w_cp, w_dg)):
        cols = pl.ds(pl.multiple_of(256 * place[c], 256), 256)
        grad_o = grad_o + dot_t(da[:, cols], w[own_rows, :])
    do = grad_o.astype(BF)
    keep = key_keep(x_own, x_yp, x_cp, x_dg)
    q, k, v = qkv[:, 0:256], qkv[:, 256:512], qkv[:, 512:768]
    scaled = q * jnp.asarray(0.125, BF)
    dq, dk, dv = (jnp.zeros((ROWS, 256), F32) for _ in range(3))
    for h in range(4):
        scores = jnp.where(keep, dot_t(masked(scaled, h), k), -1e30)
        probs = jnp.exp(scores - lse[:, h : h + 1])
        do_h = masked(do, h)
        d_probs = dot_t(do_h, v)
        inner = jnp.sum(probs * d_probs, axis=1, keepdims=True)
        ds = (probs * (d_probs - inner)).astype(BF)
        dq = dq + dot(ds, masked(k, h))
        dk = dk + t_dot(ds, masked(q, h))
        dv = dv + t_dot(probs.astype(BF), do_h)
    d_proj[:, 0:256] = (dq * 0.125).astype(BF)
    d_proj[:, 256:512] = (dk * 0.125).astype(BF)
    d_proj[:, 512:768] = dv.astype(BF)
    d_gain = jnp.zeros((1, WIDTH), F32)
    d_shift = jnp.zeros((1, WIDTH), F32)
    for b, ref in enumerate((x_own, x_yp, x_cp, x_dg)):
        normed, _ = norm_stats(ref[...].astype(F32))
        part = dot_t(d_proj[block(b)], qkv_w[:, 0:QKV_COLS])
        d_gain = d_gain + jnp.sum(part * normed, axis=0, keepdims=True)
        d_shift = d_shift + jnp.sum(part, axis=0, keepdims=True)
        if b < 2:
            dn1_mine[block(b)] = part
        else:
            dn1_theirs[block(b - 2)] = part.astype(BF)
    natural[:, 0:QKV_COLS] = t_dot(n1[...], d_proj[...]).astype(BF)
    my_cols = pl.ds(pl.multiple_of(256 * s, 256), 256)
    for j, ref in enumerate((o_own, o_yp, o_cp, o_dg)):
        heads = jnp.concatenate([ref[block(b ^ j)] for b in range(4)], axis=0)
        rows = pl.ds(pl.multiple_of(256 * place[j], 256), 256)
        natural[rows, QKV_COLS : QKV_COLS + OUT_COLS] = t_dot(heads, da[:, my_cols]).astype(BF)
    rows_out[...] = jnp.zeros((EXTRA, WIDTH), F32)
    rows_out[0:1] = d_gain
    rows_out[1:2] = d_shift
    for start, first in ((0, 0), (512, 512)):
        sums = jnp.sum(d_proj[:, first : first + 256].astype(F32), axis=0, keepdims=True)
        sums = jnp.broadcast_to(sums, (8, 256)).astype(BF)
        at = pl.ds(pl.multiple_of(start + 128 * s, 128), 128)
        for c in (0, 1):
            rows_out[2 + c : 3 + c, at] = dot_t(sums, bias_hot(c))[0:1]
    rows_out[4:7] = small_c[0:3]
    rows_out[pl.ds(7 + s, 1)] = small_b[0:1]
    rows_out[11:12] = small_b[1:2]
    natural[:, QKV_COLS + OUT_COLS :] = rows_out[...].T.astype(BF)
    for zx in range(16):
        a, b = plane_place(core[0], zx)
        for half in range(2):
            rows = slice(512 * half + 32 * zx, 512 * half + 32 * zx + 32)
            send[a, b, 32 * half : 32 * half + 32] = natural[rows]


def input_grad_kernel(mine, got_cp, got_yp, dr, x_own, vec, out):
    normed, scale = norm_stats(x_own[...].astype(F32))
    dn1 = mine[block(0)] + got_cp[block(0)].astype(F32) + got_yp[...].astype(F32)
    grad = dr[...] + norm_back(dn1, vec[0:1], normed, scale)
    out[:, 0] = grad[0:TOK]


def output_kernel(mine, got_cp, got_yp, r, vec, out):
    y = mine[block(0)] + got_cp[block(0)].astype(F32) + got_yp[...].astype(F32)
    out[0] = (y + r[...] + vec[11:12])[0:TOK].astype(BF)


def sum_of(ref):
    total = ref[0].astype(F32)
    for d in range(1, ref.shape[0]):
        total = total + ref[d].astype(F32)
    return total


def sum_low_kernel(got, out):
    out[...] = sum_of(got).astype(BF)


def sum_join_kernel(got, hidden, out):
    out[:, 0:REST] = sum_of(got).astype(BF)
    out[:, REST:] = hidden[...]


def sum_rest_kernel(got, down, up, qkv, out, *vectors):
    total = jnp.concatenate(
        [got[s].astype(F32) + got[4 + s].astype(F32) for s in range(4)], axis=0
    )
    down[0] = total[:, REST + 1024 :]
    cols = [
        jnp.concatenate(
            [
                total[8 * s : 8 * s + 8, REST + 128 * t : REST + 128 * t + 128]
                for s in range(4)
            ],
            axis=1,
        )
        for t in range(8)
    ]
    cols = jnp.concatenate(cols, axis=0)
    high = cols.astype(BF)
    low = (cols - high.astype(F32)).astype(BF)
    natural = dot_t(high, hidden_hot()) + dot_t(low, hidden_hot())
    for t in range(8):
        up[0, :, 512 * t : 512 * t + 512] = natural[8 * t : 8 * t + 8]
    for s in range(4):
        rows = slice(8 * s, 8 * s + 8)
        for i in range(3):
            at = 1024 * i + 256 * s
            qkv[0, :, at : at + 256] = total[rows, 256 * i : 256 * i + 256]
        out[0, :, 256 * s : 256 * s + 256] = total[rows, QKV_COLS : QKV_COLS + OUT_COLS]
    extra = sum(total[8 * s : 8 * s + 8, QKV_COLS + OUT_COLS : REST] for s in range(4))
    place = 0
    for ref in vectors:
        size = ref.shape[1]
        value = jnp.zeros((8, size), F32)
        for c in range(size // 8):
            column = jnp.broadcast_to(extra[:, place : place + 1], (8, size))
            hit = iota((8, size), 1) == iota((8, size), 0) + 8 * c
            value = jnp.where(hit, column, value)
            place += 1
        ref[...] = jnp.sum(value, axis=0, keepdims=True)


def body(
    inputs,
    token_mask,
    first_gain,
    first_shift,
    qkv_weight,
    qv_bias,
    out_weight,
    out_bias,
    second_gain,
    second_shift,
    up_weight,
    up_bias,
    down_weight,
    down_bias,
    cotangent,
):
    core = lax.axis_index("core").astype(jnp.int32).reshape(1)
    seq = lax.axis_index("yhi").astype(jnp.int32).reshape(1) * 2 + core

    x, g = call(
        tokens_kernel,
        [((PAD, WIDTH), BF, HBM), ((PAD, WIDTH), BF, HBM)],
        inputs,
        token_mask,
        cotangent,
        scratch=[pltpu.VMEM((PAD, WIDTH), F32)],
        us=2,
    )
    (send,) = call(
        prepare_kernel,
        [((2, 4, 8, JOINT), BF)],
        qkv_weight,
        out_weight,
        up_weight,
        down_weight,
        first_gain,
        first_shift,
        qv_bias,
        out_bias,
        second_gain,
        second_shift,
        up_bias,
        down_bias,
        deps=(x,),
    )
    pieces = lax.all_to_all(
        send.reshape(64, JOINT), ("ylo", "yhi", "core"), 0, 0, tiled=True
    )
    x_yp, g_yp = over_y(x), over_y(g)
    (send,) = call(spread_kernel, [((4, 64, JOINT), BF)], pieces)
    pieces = exchange(send.reshape(256, JOINT), STAGE_A)
    (send,) = call(
        functools.partial(copies_kernel, 0), [((4, 256, REST), BF, HBM)], pieces, deps=(x_yp,)
    )
    got = exchange(send.reshape(1024, REST), STAGE_B)
    (send,) = call(functools.partial(copies_kernel, REST), [((4, 256, 2048), BF, HBM)], pieces, deps=(g_yp,))
    hidden_got = exchange(send.reshape(1024, 2048), STAGE_B).reshape(4, 4, 64, 2048)
    xs = (x, x_yp, over_core(x), over_core(x_yp))
    gs = (g, g_yp, over_core(g), over_core(g_yp))
    w_qkv, w_own, vec = call(
        unpack_kernel,
        [((1024, QKV_COLS), BF), ((1024, OUT_COLS), BF), ((16, WIDTH), F32)],
        core,
        got.reshape(4, 4, 64, REST),
        scratch=[pltpu.VMEM((1024, EXTRA), F32)],
        scalars=1,
    )
    w_yp = over_y(w_own)
    ws = (w_own, w_yp, over_core(w_own), over_core(w_yp))

    n1, qkv, o, lse = call(
        attend_kernel,
        [
            ((ROWS, WIDTH), BF, HBM),
            ((ROWS, QKV_COLS), BF, HBM),
            ((ROWS, 256), BF, HBM),
            ((ROWS, 128), F32, HBM),
        ],
        seq,
        *hbm(*xs),
        w_qkv,
        vec,
        scalars=1,
        us=8,
    )
    o_yp = over_y(o)
    os = (o, o_yp, over_core(o), over_core(o_yp))
    n2, z, du, dn2_mine, dn2_theirs, normed_2, scale_2, down_w, r = call(
        hidden_kernel,
        [
            ((ROWS, WIDTH), BF),
            ((ROWS, WIDTH), BF),
            ((ROWS, WIDTH), BF),
            ((HALF, WIDTH), F32),
            ((HALF, WIDTH), BF),
            ((HALF, WIDTH), F32, HBM),
            ((HALF, 128), F32, HBM),
            ((1024, WIDTH), BF),
            ((PAD, WIDTH), F32, HBM),
        ],
        seq,
        *hbm(*os),
        *hbm(*xs),
        *hbm(*ws),
        vec,
        hidden_got,
        *hbm(*gs),
        scratch=[
            pltpu.VMEM((ROWS, WIDTH), F32),
            pltpu.VMEM((1024, WIDTH), BF),
            pltpu.VMEM((ROWS, WIDTH), BF),
        ],
        scalars=1,
        us=12,
    )
    two = (dn2_mine + over_core(dn2_theirs).astype(F32)).astype(BF)
    two_yp = over_y(two)
    d_hidden, small_b, y_mine, y_theirs = call(
        hidden_grad_kernel,
        [
            ((4, 4, 64, 2048), BF, HBM),
            ((8, WIDTH), F32),
            ((HALF, WIDTH), F32, HBM),
            ((HALF, WIDTH), BF, HBM),
        ],
        core,
        z,
        du,
        n2,
        down_w,
        *hbm(*gs),
        scalars=1,
        deps=(over_core(two[:16, :128]),),
        us=300,
    )
    d_hidden = exchange(d_hidden.reshape(1024, 2048), STAGE_A)
    y_cp = over_core(y_theirs)
    da, dr, small_c = call(
        residual_kernel,
        [((HALF, WIDTH), BF), ((PAD, WIDTH), F32, HBM), ((8, WIDTH), F32)],
        two,
        two_yp,
        *hbm(g, g_yp, normed_2, scale_2),
        vec,
        deps=(y_theirs,),
        us=150,
    )
    da_cp = over_core(da)
    y_low = (y_mine[PAD:] + y_cp[PAD:].astype(F32)).astype(BF)
    y_yp = over_y(y_low)
    dn1_mine, dn1_theirs, send = call(
        attend_grad_kernel,
        [((HALF, WIDTH), F32, HBM), ((HALF, WIDTH), BF, HBM), ((4, 4, 64, REST), BF, HBM)],
        seq,
        core,
        da,
        da_cp,
        *hbm(*ws),
        *hbm(*xs),
        w_qkv,
        *hbm(qkv, lse, n1),
        *hbm(*os),
        small_b,
        small_c,
        scratch=[
            pltpu.VMEM((ROWS, WIDTH), BF),
            pltpu.VMEM((ROWS, QKV_COLS), BF),
            pltpu.VMEM((EXTRA, WIDTH), F32),
            pltpu.VMEM((1024, REST), BF),
        ],
        scalars=2,
        deps=(y_low,),
        us=15,
    )
    got = exchange(send.reshape(1024, REST), STAGE_A)
    dn1_cp = over_core(dn1_theirs)
    dn1_low = (dn1_mine[PAD:] + dn1_cp[PAD:].astype(F32)).astype(BF)
    dn1_yp = over_y(dn1_low)
    (d_hidden,) = call(sum_low_kernel, [((256, 2048), BF)], d_hidden.reshape(4, 256, 2048))
    (got,) = call(
        sum_join_kernel,
        [((256, JOINT), BF, HBM)],
        got.reshape(4, 256, REST),
        d_hidden,
        deps=(dn1_low,),
    )
    got = exchange(got, STAGE_B)
    (send,) = call(
        sum_low_kernel, [((64, JOINT), BF)], got.reshape(4, 64, JOINT), deps=(dn1_yp, y_yp)
    )
    got = lax.all_to_all(send, ("ylo", "yhi", "core"), 0, 0, tiled=True)
    (block_output,) = call(
        output_kernel, [((1, TOK, WIDTH), BF)], *hbm(y_mine, y_cp, y_yp, r), vec
    )
    (g0,) = call(
        input_grad_kernel,
        [((TOK, 1, WIDTH), F32)],
        *hbm(dn1_mine, dn1_cp, dn1_yp, dr, x),
        vec,
    )
    g0 = g0.transpose(1, 0, 2)
    d_down, d_up, d_qkv, d_out, d_fg, d_fs, d_qvb, d_ob, d_sg, d_ss, d_ub, d_db = call(
        sum_rest_kernel,
        [
            ((1, 32, WIDTH), F32),
            ((1, 8, 4096), F32),
            ((1, 8, 3072), F32),
            ((1, 8, WIDTH), F32),
        ]
        + [((1, n), F32) for n in (8, 8, 16, 8, 8, 8, 32, 8)],
        got.reshape(8, 8, JOINT),
        deps=(block_output, g0),
    )
    return (
        block_output,
        g0,
        d_fg,
        d_fs,
        d_qkv,
        d_qvb,
        d_out,
        d_ob,
        d_sg,
        d_ss,
        d_up,
        d_ub,
        d_down,
        d_db,
    )


def solution(mesh):
    fine = Mesh(mesh.devices.reshape(2, 4, 4, 2, 2), ALL)
    tokens = P(DP, SEQ, None)
    vector = P(None, ALL)
    matrix = P(None, ALL, None)
    return jax.shard_map(
        body,
        mesh=fine,
        in_specs=(
            tokens,
            P(DP, SEQ),
            vector,
            vector,
            matrix,
            vector,
            matrix,
            vector,
            vector,
            vector,
            matrix,
            vector,
            matrix,
            vector,
            tokens,
        ),
        out_specs=(
            tokens,
            tokens,
            vector,
            vector,
            matrix,
            vector,
            matrix,
            vector,
            vector,
            vector,
            matrix,
            vector,
            matrix,
            vector,
        ),
        check_vma=False,
    )
```

```python
import functools

import jax
import jax.numpy as jnp
from jax import lax
from jax.experimental import pallas as pl
from jax.experimental.pallas import tpu as pltpu
from jax.sharding import Mesh, PartitionSpec as P

TOK = 145
PAD = 160
ROWS = 4 * PAD
HALF = 2 * PAD
SCALE = 1e9
HBM = pltpu.HBM
WIDTH = 1024
BF = jnp.bfloat16
F32 = jnp.float32
DP = ("ylo", "z", "x")
SEQ = ("yhi", "core")
ALL = DP + SEQ
SWAP = [(0, 1), (1, 0)]
RELATIVE = (0, 2, 1, 3)
QKV_COLS = 768
OUT_COLS = 256
EXTRA = 128
REST = QKV_COLS + OUT_COLS + EXTRA
JOINT = REST + 2048


LINES_X = [[[(r * 4 + z) * 4 + x for x in range(4)] for z in range(4)] for r in range(2)]
LINES_Z = [[[(r * 4 + z) * 4 + x for z in range(4)] for x in range(4)] for r in range(2)]


def lines(along):
    return [
        [place * 4 + 2 * yhi + core for place in line]
        for core in range(2)
        for yhi in range(2)
        for half in along[core]
        for line in half
    ]


STAGE_A = lines((LINES_X, LINES_Z))
STAGE_B = lines((LINES_Z, LINES_X))


def exchange(v, groups):
    return lax.all_to_all(v, ALL, 0, 0, axis_index_groups=groups, tiled=True)


def shift(v, groups, by):
    pairs = [(line[i], line[(i + by) % 4]) for line in groups for i in range(4)]
    return lax.ppermute(v, ALL, pairs)


def over_y(v):
    return lax.ppermute(v, "yhi", SWAP)


def over_core(v):
    return lax.ppermute(v, "core", SWAP)


def dot(a, b):
    return jnp.dot(a, b, preferred_element_type=F32)


def dot_t(a, b):
    return lax.dot_general(a, b, (((1,), (1,)), ((), ())), preferred_element_type=F32)


def t_dot(a, b):
    return lax.dot_general(a, b, (((0,), (0,)), ((), ())), preferred_element_type=F32)


def iota(shape, dim):
    return lax.broadcasted_iota(jnp.int32, shape, dim)


def call(kernel, outs, *args, scratch=(), scalars=0, deps=(), us=0.0, room=32):
    vmem = pl.BlockSpec(memory_space=pltpu.VMEM)
    specs = [pl.BlockSpec(memory_space=pltpu.SMEM)] * scalars + [vmem] * (len(args) - scalars)
    specs += [pl.BlockSpec(memory_space=pl.ANY)] * len(deps)

    def run(*refs):
        kernel(*refs[: len(args)], *refs[len(args) + len(deps) :])

    return pl.pallas_call(
        run,
        out_shape=[(o[2] if len(o) > 2 else jax.ShapeDtypeStruct)(o[0], o[1]) for o in outs],
        in_specs=specs,
        out_specs=[vmem] * len(outs),
        scratch_shapes=list(scratch),
        compiler_params=pltpu.CompilerParams(vmem_limit_bytes=room * 2**20),
        cost_estimate=pl.CostEstimate(
            flops=int(us * SCALE), bytes_accessed=0, transcendentals=0
        ),
        name=getattr(kernel, "func", kernel).__name__.removesuffix("_kernel"),
    )(*args, *deps)


def hbm(*values):
    return tuple(pltpu.with_memory_space_constraint(v, HBM) for v in values)


def after(v, *deps):
    anywhere = pl.BlockSpec(memory_space=pl.ANY)
    return pl.pallas_call(
        lambda *refs: None,
        out_shape=jax.ShapeDtypeStruct(v.shape, v.dtype),
        in_specs=[anywhere] * (1 + len(deps)),
        out_specs=anywhere,
        input_output_aliases={0: 0},
        cost_estimate=pl.CostEstimate(flops=0, bytes_accessed=0, transcendentals=0),
        name="after",
    )(v, *deps)


def block(b):
    return slice(b * PAD, (b + 1) * PAD)


def norm_stats(v):
    average = jnp.mean(v, axis=-1, keepdims=True)
    centred = v - average
    variance = jnp.mean(centred * centred, axis=-1, keepdims=True)
    scale = lax.rsqrt(variance + 1e-06)
    return centred * scale, scale


def norm_back(grad, gain, normed, scale):
    e = grad * gain
    return scale * (
        e
        - jnp.mean(e, axis=-1, keepdims=True)
        - normed * jnp.mean(e * normed, axis=-1, keepdims=True)
    )


def piece_columns(refs):
    out = jnp.zeros((8, EXTRA), F32)
    lane = iota((8, EXTRA), 1)
    place = 0
    for ref in refs:
        size = ref.shape[1]
        for c in range(size // 8):
            spread = jnp.broadcast_to(ref[...].astype(F32), (8, size))
            hit = iota((8, size), 1) == iota((8, size), 0) + 8 * c
            column = jnp.sum(jnp.where(hit, spread, 0.0), axis=1, keepdims=True)
            out = jnp.where(lane == place, column, out)
            place += 1
    return out


def hidden_hot():
    row, col = iota((512, 512), 0), iota((512, 512), 1)
    hit = row == 32 * (col % 128 // 8) + 8 * (col // 128) + col % 8
    return jnp.where(hit, 1.0, 0.0).astype(BF)


def tokens_kernel(x, mask, g, out, g_out, tok):
    row = jnp.zeros((8, WIDTH), F32)
    tok[0:8] = row
    tok[0:1, 0:TOK] = mask[...].astype(F32)
    row = tok[0:8]
    lifted = [pltpu.roll(row, PAD * b, 1)[0:1] if b else row[0:1] for b in range(4)]
    tok[0:TOK] = x[0].astype(F32)
    for b in range(4):
        tok[TOK + b : TOK + b + 1] = lifted[b]
    tok[TOK + 4 :] = jnp.zeros((PAD - TOK - 4, WIDTH), F32)
    out[...] = tok[...].astype(BF)
    tok[0:TOK] = g[0].astype(F32)
    tok[TOK:] = jnp.zeros((PAD - TOK, WIDTH), F32)
    g_out[...] = tok[...].astype(BF)


def prepare_kernel(qkv, out_w, up, down, fg, fs, qvb, ob, sg, ss, ub, db, send):
    extra = piece_columns([fg, fs, qvb, ob, sg, ss, ub, db])
    rows = jnp.concatenate([up[0, :, 512 * t : 512 * t + 512] for t in range(8)], axis=0)
    up_cols = dot(rows, hidden_hot())
    for s in range(4):
        parts = [qkv[0, :, 1024 * i + 256 * s : 1024 * i + 256 * s + 256] for i in range(3)]
        parts = [p.astype(F32) for p in parts]
        parts.append(out_w[0, :, 256 * s : 256 * s + 256].astype(F32))
        parts.append(extra)
        parts += [up_cols[8 * t : 8 * t + 8, 128 * s : 128 * s + 128] for t in range(8)]
        parts.append(down[0, 8 * s : 8 * s + 8].astype(F32))
        piece = jnp.concatenate(parts, axis=1).astype(BF)
        for b in range(2):
            send[b, s] = piece


def spread_kernel(pieces, out):
    for d in range(4):
        out[d] = pieces[...]


def line_kernel(got, attend, hidden):
    for d in range(4):
        attend[d] = got[:, 0:REST]
    hidden[...] = got[:, REST:]


def unpack_kernel(core, got, w_qkv, w_out, vec, extra):
    for zx in range(16):
        a, b = plane_place(core[0], zx)
        for half in range(2):
            rows = slice(512 * half + 32 * zx, 512 * half + 32 * zx + 32)
            part = got[b, a, 32 * half : 32 * half + 32]
            w_qkv[rows] = part[:, 0:QKV_COLS]
            w_out[rows] = part[:, QKV_COLS : QKV_COLS + OUT_COLS]
            extra[rows] = part[:, QKV_COLS + OUT_COLS :].astype(F32)
    vec[...] = extra[...].T[0:16]


def bias_hot(c):
    row, col = iota((128, 256), 0), iota((128, 256), 1)
    hit = (col // 16 == row // 8) & (col % 16 == 8 * c + row % 8)
    return jnp.where(hit, 1.0, 0.0).astype(BF)


def plane_place(core, zx):
    z, x = zx // 4, zx % 4
    return jnp.where(core == 0, x, z), jnp.where(core == 0, z, x)


def head_mask(h):
    return iota((1, 256), 1) // 64 == h


def masked(v, h):
    return jnp.where(head_mask(h), v, jnp.zeros_like(v))


def key_keep(x_own, x_yp, x_cp, x_dg):
    refs = (x_own, x_yp, x_cp, x_dg)
    return sum(r[TOK + b : TOK + b + 1, 0:ROWS].astype(F32) for b, r in enumerate(refs)) > 0


def attend_kernel(seq, x_own, x_yp, x_cp, x_dg, w, vec, n1, qkv, o, lse):
    s = seq[0]
    gain, shift = vec[0:1], vec[1:2]
    for b, ref in enumerate((x_own, x_yp, x_cp, x_dg)):
        normed, _ = norm_stats(ref[...].astype(F32))
        n1[block(b)] = (normed * gain + shift).astype(BF)
    biases = []
    for start in (0, 512):
        at = pl.ds(pl.multiple_of(start + 128 * s, 128), 128)
        pieces = [jnp.broadcast_to(vec[2 + c : 3 + c, at], (8, 128)).astype(BF) for c in (0, 1)]
        biases.append((dot(pieces[0], bias_hot(0)) + dot(pieces[1], bias_hot(1)))[0:1])
    for i, bias in enumerate((biases[0], None, biases[1])):
        at = slice(256 * i, 256 * i + 256)
        proj = dot(n1[...], w[:, at])
        qkv[:, at] = (proj if bias is None else proj + bias).astype(BF)
    keep = key_keep(x_own, x_yp, x_cp, x_dg)
    q = qkv[:, 0:256] * jnp.asarray(0.125, BF)
    k, v = qkv[:, 256:512], qkv[:, 512:768]
    total = jnp.zeros((ROWS, 256), F32)
    logs = jnp.zeros((ROWS, 128), F32)
    for h in range(4):
        scores = jnp.where(keep, dot_t(masked(q, h), k), -1e30)
        peak = jnp.max(scores, axis=1, keepdims=True)
        powers = jnp.exp(scores - peak)
        weight = jnp.sum(powers, axis=1, keepdims=True)
        probs = (powers * (1.0 / weight)).astype(BF)
        total = total + dot(probs, masked(v, h))
        logs = jnp.where(iota((ROWS, 128), 1) == h, peak + jnp.log(weight), logs)
    o[...] = total.astype(BF)
    lse[...] = logs


def hidden_kernel(
    seq,
    places,
    o_own,
    o_yp,
    o_cp,
    o_dg,
    x_own,
    x_yp,
    x_cp,
    x_dg,
    w_own,
    w_yp,
    w_cp,
    w_dg,
    vec,
    line_own,
    line_1,
    line_2,
    line_3,
    g_own,
    g_yp,
    g_cp,
    g_dg,
    n2,
    z,
    du,
    dn2_mine,
    dn2_theirs,
    normed_out,
    scale_out,
    down,
    r_own,
    r,
    up,
    dm,
):
    s = seq[0]
    place = [jnp.bitwise_xor(s, m) for m in RELATIVE]
    for b, ref in enumerate((g_own, g_yp, g_cp, g_dg)):
        dm[block(b)] = ref[...]
    heads = []
    for j, ref in enumerate((o_own, o_yp, o_cp, o_dg)):
        heads.append(jnp.concatenate([ref[block(b ^ j)] for b in range(4)], axis=0))
    for c, w in enumerate((w_own, w_yp, w_cp, w_dg)):
        total = jnp.zeros((ROWS, 256), F32)
        for j in range(4):
            rows = pl.ds(pl.multiple_of(256 * place[j], 256), 256)
            total = total + dot(heads[j], w[rows, :])
        r[:, pl.ds(pl.multiple_of(256 * place[c], 256), 256)] = total
    gain, shift, b_out = vec[5:6], vec[6:7], vec[4:5]
    for b, ref in enumerate((x_own, x_yp, x_cp, x_dg)):
        rows = r[block(b)] + ref[...].astype(F32) + b_out
        if b == 0:
            r_own[...] = rows
        normed, scale = norm_stats(rows)
        n2[block(b)] = (normed * gain + shift).astype(BF)
        if b < 2:
            normed_out[block(b)] = normed
            scale_out[block(b)] = jnp.broadcast_to(scale, (PAD, 128))
    bias = vec[pl.ds(7 + s, 1)]
    for by, ref in enumerate((line_own, line_1, line_2, line_3)):
        b = lax.rem(places[1] + 4 - by, 4)
        for a in range(4):
            zx = jnp.where(s % 2 == 0, 4 * b + a, 4 * a + b)
            for half in range(2):
                rows = pl.ds(pl.multiple_of(512 * half + 32 * zx, 32), 32)
                up[rows] = ref[a, 32 * half : 32 * half + 32, 0:1024]
                down[rows] = ref[a, 32 * half : 32 * half + 32, 1024:]
    for c in range(4):
        at = slice(256 * c, 256 * c + 256)
        u = dot(n2[...], up[:, at]) + bias[:, at]
        cdf = 0.5 * (1.0 + lax.erf(u * (0.5**0.5)))
        z[:, at] = (u * cdf).astype(BF)
        slope = cdf + u * jnp.exp(-0.5 * u * u) * 0.3989422804014327
        du[:, at] = (slope * dot_t(dm[...], down[at, :])).astype(BF)
    dn2_mine[...] = dot_t(du[0:HALF], up[...])
    dn2_theirs[...] = dot_t(du[HALF:], up[...]).astype(BF)


def hidden_grad_kernel(
    core, z, du, n2, down, g_own, g_yp, g_cp, g_dg, out, small, y_own, y_two, y_theirs
):
    y_own[...] = dot(z[block(0)], down[...])
    y_two[...] = dot(z[block(1)], down[...]).astype(BF)
    y_theirs[...] = dot(z[HALF:], down[...]).astype(BF)
    dm = jnp.concatenate([g[...] for g in (g_own, g_yp, g_cp, g_dg)], axis=0)
    d_up = t_dot(n2[...], du[...]).astype(BF)
    d_down = t_dot(z[...], dm).astype(BF)
    for zx in range(16):
        a, b = plane_place(core[0], zx)
        for half in range(2):
            rows = slice(512 * half + 32 * zx, 512 * half + 32 * zx + 32)
            out[a, b, 32 * half : 32 * half + 32, 0:1024] = d_up[rows]
            out[a, b, 32 * half : 32 * half + 32, 1024:] = d_down[rows]
    small[...] = jnp.zeros((8, WIDTH), F32)
    small[0:1] = jnp.sum(du[...].astype(F32), axis=0, keepdims=True)
    small[1:2] = jnp.sum(g_own[...].astype(F32), axis=0, keepdims=True)


def residual_kernel(two, got, g_own, g_yp, normed, scale, vec, da, dr, small):
    gain = vec[5:6]
    small[...] = jnp.zeros((8, WIDTH), F32)
    for b, ref in enumerate((g_own, g_yp)):
        dn2 = two[block(b)].astype(F32) + got[block(1 - b)].astype(F32)
        grad = ref[...].astype(F32) + norm_back(dn2, gain, normed[block(b)], scale[block(b), 0:1])
        low = grad.astype(BF)
        da[block(b)] = low
        if b == 0:
            dr[...] = grad
            small[0:1] = jnp.sum(low.astype(F32), axis=0, keepdims=True)
            small[1:2] = jnp.sum(dn2 * normed[block(b)], axis=0, keepdims=True)
            small[2:3] = jnp.sum(dn2, axis=0, keepdims=True)


def attend_grad_kernel(
    seq,
    core,
    da_mine,
    da_cp,
    w_own,
    w_yp,
    w_cp,
    w_dg,
    x_own,
    x_yp,
    x_cp,
    x_dg,
    qkv_w,
    qkv,
    lse,
    n1,
    o_own,
    o_yp,
    o_cp,
    o_dg,
    small_b,
    small_c,
    dn1_own,
    dn1_two,
    dn1_theirs,
    send,
    da,
    d_proj,
    rows_out,
    natural,
):
    s = seq[0]
    place = [jnp.bitwise_xor(s, m) for m in RELATIVE]
    da[0:HALF] = da_mine[...]
    da[HALF:] = da_cp[...]
    own_rows = pl.ds(pl.multiple_of(256 * s, 256), 256)
    grad_o = jnp.zeros((ROWS, 256), F32)
    for c, w in enumerate((w_own, w_yp, w_cp, w_dg)):
        cols = pl.ds(pl.multiple_of(256 * place[c], 256), 256)
        grad_o = grad_o + dot_t(da[:, cols], w[own_rows, :])
    do = grad_o.astype(BF)
    keep = key_keep(x_own, x_yp, x_cp, x_dg)
    q, k, v = qkv[:, 0:256], qkv[:, 256:512], qkv[:, 512:768]
    scaled = q * jnp.asarray(0.125, BF)
    dq, dk, dv = (jnp.zeros((ROWS, 256), F32) for _ in range(3))
    for h in range(4):
        scores = jnp.where(keep, dot_t(masked(scaled, h), k), -1e30)
        probs = jnp.exp(scores - lse[:, h : h + 1])
        do_h = masked(do, h)
        d_probs = dot_t(do_h, v)
        inner = jnp.sum(probs * d_probs, axis=1, keepdims=True)
        ds = (probs * (d_probs - inner)).astype(BF)
        dq = dq + dot(ds, masked(k, h))
        dk = dk + t_dot(ds, masked(q, h))
        dv = dv + t_dot(probs.astype(BF), do_h)
    d_proj[:, 0:256] = (dq * 0.125).astype(BF)
    d_proj[:, 256:512] = (dk * 0.125).astype(BF)
    d_proj[:, 512:768] = dv.astype(BF)
    d_gain = jnp.zeros((1, WIDTH), F32)
    d_shift = jnp.zeros((1, WIDTH), F32)
    for b, ref in enumerate((x_own, x_yp, x_cp, x_dg)):
        normed, _ = norm_stats(ref[...].astype(F32))
        part = dot_t(d_proj[block(b)], qkv_w[:, 0:QKV_COLS])
        d_gain = d_gain + jnp.sum(part * normed, axis=0, keepdims=True)
        d_shift = d_shift + jnp.sum(part, axis=0, keepdims=True)
        if b == 0:
            dn1_own[...] = part
        elif b == 1:
            dn1_two[...] = part.astype(BF)
        else:
            dn1_theirs[block(b - 2)] = part.astype(BF)
    natural[:, 0:QKV_COLS] = t_dot(n1[...], d_proj[...]).astype(BF)
    my_cols = pl.ds(pl.multiple_of(256 * s, 256), 256)
    for j, ref in enumerate((o_own, o_yp, o_cp, o_dg)):
        heads = jnp.concatenate([ref[block(b ^ j)] for b in range(4)], axis=0)
        rows = pl.ds(pl.multiple_of(256 * place[j], 256), 256)
        natural[rows, QKV_COLS : QKV_COLS + OUT_COLS] = t_dot(heads, da[:, my_cols]).astype(BF)
    rows_out[...] = jnp.zeros((EXTRA, WIDTH), F32)
    rows_out[0:1] = d_gain
    rows_out[1:2] = d_shift
    for start, first in ((0, 0), (512, 512)):
        sums = jnp.sum(d_proj[:, first : first + 256].astype(F32), axis=0, keepdims=True)
        sums = jnp.broadcast_to(sums, (8, 256)).astype(BF)
        at = pl.ds(pl.multiple_of(start + 128 * s, 128), 128)
        for c in (0, 1):
            rows_out[2 + c : 3 + c, at] = dot_t(sums, bias_hot(c))[0:1]
    rows_out[4:7] = small_c[0:3]
    rows_out[pl.ds(7 + s, 1)] = small_b[0:1]
    rows_out[11:12] = small_b[1:2]
    natural[:, QKV_COLS + OUT_COLS :] = rows_out[...].T.astype(BF)
    for zx in range(16):
        a, b = plane_place(core[0], zx)
        for half in range(2):
            rows = slice(512 * half + 32 * zx, 512 * half + 32 * zx + 32)
            send[a, b, 32 * half : 32 * half + 32] = natural[rows]


def input_grad_kernel(mine, got_cp, got_yp, dr, x_own, vec, out):
    normed, scale = norm_stats(x_own[...].astype(F32))
    dn1 = mine[...] + got_cp[block(0)].astype(F32) + got_yp[...].astype(F32)
    grad = dr[...] + norm_back(dn1, vec[0:1], normed, scale)
    out[:, 0] = grad[0:TOK]


def output_kernel(mine, got_cp, got_yp, r, vec, out):
    y = mine[...] + got_cp[block(0)].astype(F32) + got_yp[...].astype(F32)
    out[0] = (y + r[...] + vec[11:12])[0:TOK].astype(BF)


def sum_of(ref):
    total = ref[0].astype(F32)
    for d in range(1, ref.shape[0]):
        total = total + ref[d].astype(F32)
    return total


def sum_low_kernel(got, out):
    out[...] = sum_of(got).astype(BF)


def sum_line_kernel(places, got, own, to_1, to_2, to_3, total):
    total[...] = sum_of(got)
    own[...] = total[places[1]]
    for by, ref in ((1, to_1), (2, to_2), (3, to_3)):
        ref[...] = total[lax.rem(places[1] + by, 4)].astype(BF)


def sum_join_kernel(got, own, got_1, got_2, got_3, out):
    out[:, 0:REST] = sum_of(got).astype(BF)
    hidden = own[...]
    for ref in (got_1, got_2, got_3):
        hidden = hidden + ref[...].astype(F32)
    out[:, REST:] = hidden.astype(BF)


def sum_rest_kernel(got, down, up, qkv, out, *vectors):
    total = jnp.concatenate(
        [got[s].astype(F32) + got[4 + s].astype(F32) for s in range(4)], axis=0
    )
    down[0] = total[:, REST + 1024 :]
    cols = [
        jnp.concatenate(
            [
                total[8 * s : 8 * s + 8, REST + 128 * t : REST + 128 * t + 128]
                for s in range(4)
            ],
            axis=1,
        )
        for t in range(8)
    ]
    cols = jnp.concatenate(cols, axis=0)
    high = cols.astype(BF)
    low = (cols - high.astype(F32)).astype(BF)
    natural = dot_t(high, hidden_hot()) + dot_t(low, hidden_hot())
    for t in range(8):
        up[0, :, 512 * t : 512 * t + 512] = natural[8 * t : 8 * t + 8]
    for s in range(4):
        rows = slice(8 * s, 8 * s + 8)
        for i in range(3):
            at = 1024 * i + 256 * s
            qkv[0, :, at : at + 256] = total[rows, 256 * i : 256 * i + 256]
        out[0, :, 256 * s : 256 * s + 256] = total[rows, QKV_COLS : QKV_COLS + OUT_COLS]
    extra = sum(total[8 * s : 8 * s + 8, QKV_COLS + OUT_COLS : REST] for s in range(4))
    place = 0
    for ref in vectors:
        size = ref.shape[1]
        value = jnp.zeros((8, size), F32)
        for c in range(size // 8):
            column = jnp.broadcast_to(extra[:, place : place + 1], (8, size))
            hit = iota((8, size), 1) == iota((8, size), 0) + 8 * c
            value = jnp.where(hit, column, value)
            place += 1
        ref[...] = jnp.sum(value, axis=0, keepdims=True)


def body(
    inputs,
    token_mask,
    first_gain,
    first_shift,
    qkv_weight,
    qv_bias,
    out_weight,
    out_bias,
    second_gain,
    second_shift,
    up_weight,
    up_bias,
    down_weight,
    down_bias,
    cotangent,
):
    core = lax.axis_index("core").astype(jnp.int32).reshape(1)
    seq = lax.axis_index("yhi").astype(jnp.int32).reshape(1) * 2 + core
    z_place, x_place = lax.axis_index("z"), lax.axis_index("x")
    places = jnp.where(
        core == 0, jnp.stack([x_place, z_place]), jnp.stack([z_place, x_place])
    ).astype(jnp.int32)

    (send,) = call(
        prepare_kernel,
        [((2, 4, 8, JOINT), BF)],
        *hbm(
            qkv_weight,
            out_weight,
            up_weight,
            down_weight,
            first_gain,
            first_shift,
            qv_bias,
            out_bias,
            second_gain,
            second_shift,
            up_bias,
            down_bias,
        ),
    )
    x, g = call(
        tokens_kernel,
        [((PAD, WIDTH), BF, HBM), ((PAD, WIDTH), BF, HBM)],
        *hbm(inputs, token_mask, cotangent),
        scratch=[pltpu.VMEM((PAD, WIDTH), F32)],
        us=2,
        deps=(send,),
    )
    pieces = lax.all_to_all(
        send.reshape(64, JOINT), ("ylo", "yhi", "core"), 0, 0, tiled=True
    )
    x_yp, g_yp = over_y(x), over_y(g)
    x_cp, g_cp = over_core(x), over_core(g)
    (send,) = call(spread_kernel, [((4, 64, JOINT), BF)], pieces, deps=(x_cp, g_cp))
    pieces = exchange(send.reshape(256, JOINT), STAGE_A)
    send, line = call(
        line_kernel,
        [((4, 256, REST), BF, HBM), ((256, 2048), BF)],
        pieces,
        deps=(x_yp,),
    )
    got = exchange(send.reshape(1024, REST), STAGE_B)
    line = after(line, g_yp).reshape(4, 64, 2048)
    lines = [line] + [shift(line, STAGE_B, by) for by in (1, 2, 3)]
    xs = (x, x_yp, x_cp, over_core(x_yp))
    gs = (g, g_yp, g_cp, over_core(g_yp))
    w_qkv, w_own, vec = call(
        unpack_kernel,
        [((1024, QKV_COLS), BF), ((1024, OUT_COLS), BF), ((16, WIDTH), F32)],
        core,
        got.reshape(4, 4, 64, REST),
        scratch=[pltpu.VMEM((1024, EXTRA), F32)],
        scalars=1,
        deps=(g_yp,),
    )
    w_yp = over_y(w_own)
    ws = (w_own, w_yp, over_core(w_own), over_core(w_yp))

    n1, qkv, o, lse = call(
        attend_kernel,
        [
            ((ROWS, WIDTH), BF, HBM),
            ((ROWS, QKV_COLS), BF, HBM),
            ((ROWS, 256), BF, HBM),
            ((ROWS, 128), F32, HBM),
        ],
        seq,
        *xs,
        w_qkv,
        vec,
        scalars=1,
        us=8,
    )
    o_yp = over_y(o)
    os = (o, o_yp, over_core(o), over_core(o_yp))
    n2, z, du, dn2_mine, dn2_theirs, normed_2, scale_2, down_w, r = call(
        hidden_kernel,
        [
            ((ROWS, WIDTH), BF),
            ((ROWS, WIDTH), BF),
            ((ROWS, WIDTH), BF),
            ((HALF, WIDTH), F32),
            ((HALF, WIDTH), BF),
            ((HALF, WIDTH), F32, HBM),
            ((HALF, 128), F32, HBM),
            ((1024, WIDTH), BF),
            ((PAD, WIDTH), F32, HBM),
        ],
        seq,
        places,
        *os,
        *xs,
        *ws,
        vec,
        *lines,
        *gs,
        scratch=[
            pltpu.VMEM((ROWS, WIDTH), F32),
            pltpu.VMEM((1024, WIDTH), BF),
            pltpu.VMEM((ROWS, WIDTH), BF),
        ],
        scalars=2,
        us=12,
    )
    two = (dn2_mine + over_core(dn2_theirs).astype(F32)).astype(BF)
    two_yp = over_y(two)
    d_hidden, small_b, y_own, y_two, y_theirs = call(
        hidden_grad_kernel,
        [
            ((4, 4, 64, 2048), BF, HBM),
            ((8, WIDTH), F32),
            ((PAD, WIDTH), F32, HBM),
            ((PAD, WIDTH), BF, HBM),
            ((HALF, WIDTH), BF, HBM),
        ],
        core,
        z,
        du,
        n2,
        down_w,
        *gs,
        scalars=1,
        deps=(two,),
        us=300,
    )
    d_hidden = exchange(d_hidden.reshape(1024, 2048), STAGE_A)
    y_cp = over_core(y_theirs)
    da, dr, small_c = call(
        residual_kernel,
        [((HALF, WIDTH), BF), ((PAD, WIDTH), F32, HBM), ((8, WIDTH), F32)],
        two,
        two_yp,
        g,
        g_yp,
        normed_2,
        scale_2,
        vec,
        deps=(y_theirs,),
        us=150,
    )
    da_cp = over_core(da)
    y_low = (y_two.astype(F32) + y_cp[PAD:].astype(F32)).astype(BF)
    y_yp = over_y(y_low)
    dn1_own, dn1_two, dn1_theirs, send = call(
        attend_grad_kernel,
        [
            ((PAD, WIDTH), F32, HBM),
            ((PAD, WIDTH), BF, HBM),
            ((HALF, WIDTH), BF, HBM),
            ((4, 4, 64, REST), BF, HBM),
        ],
        seq,
        core,
        da,
        da_cp,
        *ws,
        *xs,
        *hbm(w_qkv, qkv, lse, n1),
        *os,
        small_b,
        small_c,
        scratch=[
            pltpu.VMEM((ROWS, WIDTH), BF),
            pltpu.VMEM((ROWS, QKV_COLS), BF),
            pltpu.VMEM((EXTRA, WIDTH), F32),
            pltpu.VMEM((1024, REST), BF),
        ],
        scalars=2,
        us=15,
    )
    got = exchange(after(send.reshape(1024, REST), d_hidden), STAGE_A)
    dn1_cp = over_core(dn1_theirs)
    dn1_low = (dn1_two.astype(F32) + dn1_cp[PAD:].astype(F32)).astype(BF)
    dn1_yp = over_y(dn1_low)
    hidden_own, *parts = call(
        sum_line_kernel,
        [((64, 2048), F32)] + [((64, 2048), BF)] * 3,
        places,
        d_hidden.reshape(4, 4, 64, 2048),
        scratch=[pltpu.VMEM((4, 64, 2048), F32)],
        scalars=1,
    )
    parts = [shift(part, STAGE_B, by) for by, part in zip((1, 2, 3), parts)]
    (send,) = call(
        sum_low_kernel, [((256, REST), BF, HBM)], got.reshape(4, 256, REST), deps=(dn1_low, y_yp, hidden_own)
    )
    got = exchange(send, STAGE_B)
    (send,) = call(
        sum_join_kernel,
        [((64, JOINT), BF)],
        got.reshape(4, 64, REST),
        hidden_own,
        *parts,
        deps=(dn1_yp,),
    )
    got = lax.all_to_all(send, ("ylo", "yhi", "core"), 0, 0, tiled=True)
    (block_output,) = call(
        output_kernel, [((1, TOK, WIDTH), BF)], *hbm(y_own, y_cp, y_yp, r), vec
    )
    (g0,) = call(
        input_grad_kernel,
        [((TOK, 1, WIDTH), F32)],
        *hbm(dn1_own, dn1_cp, dn1_yp, dr, x),
        vec,
    )
    g0 = g0.transpose(1, 0, 2)
    d_down, d_up, d_qkv, d_out, d_fg, d_fs, d_qvb, d_ob, d_sg, d_ss, d_ub, d_db = call(
        sum_rest_kernel,
        [
            ((1, 32, WIDTH), F32),
            ((1, 8, 4096), F32),
            ((1, 8, 3072), F32),
            ((1, 8, WIDTH), F32),
        ]
        + [((1, n), F32) for n in (8, 8, 16, 8, 8, 8, 32, 8)],
        got.reshape(8, 8, JOINT),
        deps=(block_output, g0),
    )
    return (
        block_output,
        g0,
        d_fg,
        d_fs,
        d_qkv,
        d_qvb,
        d_out,
        d_ob,
        d_sg,
        d_ss,
        d_up,
        d_ub,
        d_down,
        d_db,
    )


def solution(mesh):
    fine = Mesh(mesh.devices.reshape(2, 4, 4, 2, 2), ALL)
    tokens = P(DP, SEQ, None)
    vector = P(None, ALL)
    matrix = P(None, ALL, None)
    return jax.shard_map(
        body,
        mesh=fine,
        in_specs=(
            tokens,
            P(DP, SEQ),
            vector,
            vector,
            matrix,
            vector,
            matrix,
            vector,
            vector,
            vector,
            matrix,
            vector,
            matrix,
            vector,
            tokens,
        ),
        out_specs=(
            tokens,
            tokens,
            vector,
            vector,
            matrix,
            vector,
            matrix,
            vector,
            vector,
            vector,
            matrix,
            vector,
            matrix,
            vector,
        ),
        check_vma=False,
    )
```

```python
import functools

import jax
import jax.numpy as jnp
from jax import lax
from jax.experimental import pallas as pl
from jax.experimental.pallas import tpu as pltpu
from jax.sharding import Mesh, PartitionSpec as P

TOK = 145
PAD = 160
ROWS = 4 * PAD
HALF = 2 * PAD
SCALE = 1e9
HBM = pltpu.HBM
WIDTH = 1024
BF = jnp.bfloat16
F32 = jnp.float32
DP = ("ylo", "z", "x")
SEQ = ("yhi", "core")
ALL = DP + SEQ
SWAP = [(0, 1), (1, 0)]
RELATIVE = (0, 2, 1, 3)
QKV_COLS = 768
OUT_COLS = 256
EXTRA = 128
REST = QKV_COLS + OUT_COLS + EXTRA
JOINT = REST + 2048


LINES_X = [[[(r * 4 + z) * 4 + x for x in range(4)] for z in range(4)] for r in range(2)]
LINES_Z = [[[(r * 4 + z) * 4 + x for z in range(4)] for x in range(4)] for r in range(2)]


def lines(along):
    return [
        [place * 4 + 2 * yhi + core for place in line]
        for core in range(2)
        for yhi in range(2)
        for half in along[core]
        for line in half
    ]


STAGE_A = lines((LINES_X, LINES_Z))
STAGE_B = lines((LINES_Z, LINES_X))


def exchange(v, groups):
    return lax.all_to_all(v, ALL, 0, 0, axis_index_groups=groups, tiled=True)


def shift(v, groups, by):
    pairs = [(line[i], line[(i + by) % 4]) for line in groups for i in range(4)]
    return lax.ppermute(v, ALL, pairs)


def over_y(v):
    return lax.ppermute(v, "yhi", SWAP)


def over_core(v):
    return lax.ppermute(v, "core", SWAP)


def dot(a, b):
    return jnp.dot(a, b, preferred_element_type=F32)


def dot_t(a, b):
    return lax.dot_general(a, b, (((1,), (1,)), ((), ())), preferred_element_type=F32)


def t_dot(a, b):
    return lax.dot_general(a, b, (((0,), (0,)), ((), ())), preferred_element_type=F32)


def iota(shape, dim):
    return lax.broadcasted_iota(jnp.int32, shape, dim)


def call(kernel, outs, *args, scratch=(), scalars=0, deps=(), us=0.0, room=32):
    vmem = pl.BlockSpec(memory_space=pltpu.VMEM)
    specs = [pl.BlockSpec(memory_space=pltpu.SMEM)] * scalars + [vmem] * (len(args) - scalars)
    specs += [pl.BlockSpec(memory_space=pl.ANY)] * len(deps)

    def run(*refs):
        kernel(*refs[: len(args)], *refs[len(args) + len(deps) :])

    return pl.pallas_call(
        run,
        out_shape=[(o[2] if len(o) > 2 else jax.ShapeDtypeStruct)(o[0], o[1]) for o in outs],
        in_specs=specs,
        out_specs=[vmem] * len(outs),
        scratch_shapes=list(scratch),
        compiler_params=pltpu.CompilerParams(vmem_limit_bytes=room * 2**20),
        cost_estimate=pl.CostEstimate(
            flops=int(us * SCALE), bytes_accessed=0, transcendentals=0
        ),
        name=getattr(kernel, "func", kernel).__name__.removesuffix("_kernel"),
    )(*args, *deps)


def hbm(*values):
    return tuple(pltpu.with_memory_space_constraint(v, HBM) for v in values)


def after(v, *deps):
    anywhere = pl.BlockSpec(memory_space=pl.ANY)
    return pl.pallas_call(
        lambda *refs: None,
        out_shape=jax.ShapeDtypeStruct(v.shape, v.dtype),
        in_specs=[anywhere] * (1 + len(deps)),
        out_specs=anywhere,
        input_output_aliases={0: 0},
        cost_estimate=pl.CostEstimate(flops=0, bytes_accessed=0, transcendentals=0),
        name="after",
    )(v, *deps)


def block(b):
    return slice(b * PAD, (b + 1) * PAD)


def norm_stats(v):
    average = jnp.mean(v, axis=-1, keepdims=True)
    centred = v - average
    variance = jnp.mean(centred * centred, axis=-1, keepdims=True)
    scale = lax.rsqrt(variance + 1e-06)
    return centred * scale, scale


def norm_back(grad, gain, normed, scale):
    e = grad * gain
    return scale * (
        e
        - jnp.mean(e, axis=-1, keepdims=True)
        - normed * jnp.mean(e * normed, axis=-1, keepdims=True)
    )


def piece_columns(refs):
    out = jnp.zeros((8, EXTRA), F32)
    lane = iota((8, EXTRA), 1)
    place = 0
    for ref in refs:
        size = ref.shape[1]
        for c in range(size // 8):
            spread = jnp.broadcast_to(ref[...].astype(F32), (8, size))
            hit = iota((8, size), 1) == iota((8, size), 0) + 8 * c
            column = jnp.sum(jnp.where(hit, spread, 0.0), axis=1, keepdims=True)
            out = jnp.where(lane == place, column, out)
            place += 1
    return out


def hidden_hot():
    row, col = iota((512, 512), 0), iota((512, 512), 1)
    hit = row == 32 * (col % 128 // 8) + 8 * (col // 128) + col % 8
    return jnp.where(hit, 1.0, 0.0).astype(BF)


def tokens_kernel(x, mask, g, out, g_out, tok):
    row = jnp.zeros((8, WIDTH), F32)
    tok[0:8] = row
    tok[0:1, 0:TOK] = mask[...].astype(F32)
    row = tok[0:8]
    lifted = [pltpu.roll(row, PAD * b, 1)[0:1] if b else row[0:1] for b in range(4)]
    tok[0:TOK] = x[0].astype(F32)
    for b in range(4):
        tok[TOK + b : TOK + b + 1] = lifted[b]
    tok[TOK + 4 :] = jnp.zeros((PAD - TOK - 4, WIDTH), F32)
    out[...] = tok[...].astype(BF)
    tok[0:TOK] = g[0].astype(F32)
    tok[TOK:] = jnp.zeros((PAD - TOK, WIDTH), F32)
    g_out[...] = tok[...].astype(BF)


def prepare_kernel(qkv, out_w, up, down, fg, fs, qvb, ob, sg, ss, ub, db, send):
    extra = piece_columns([fg, fs, qvb, ob, sg, ss, ub, db])
    rows = jnp.concatenate([up[0, :, 512 * t : 512 * t + 512] for t in range(8)], axis=0)
    up_cols = dot(rows, hidden_hot())
    for s in range(4):
        parts = [qkv[0, :, 1024 * i + 256 * s : 1024 * i + 256 * s + 256] for i in range(3)]
        parts = [p.astype(F32) for p in parts]
        parts.append(out_w[0, :, 256 * s : 256 * s + 256].astype(F32))
        parts.append(extra)
        parts += [up_cols[8 * t : 8 * t + 8, 128 * s : 128 * s + 128] for t in range(8)]
        parts.append(down[0, 8 * s : 8 * s + 8].astype(F32))
        piece = jnp.concatenate(parts, axis=1).astype(BF)
        for b in range(2):
            send[b, s] = piece


def spread_kernel(pieces, out):
    for d in range(4):
        out[d] = pieces[...]


def line_kernel(got, attend, hidden):
    for d in range(4):
        attend[d] = got[:, 0:REST]
    hidden[...] = got[:, REST:]


def unpack_kernel(core, got, w_qkv, w_out, vec, extra):
    for zx in range(16):
        a, b = plane_place(core[0], zx)
        for half in range(2):
            rows = slice(512 * half + 32 * zx, 512 * half + 32 * zx + 32)
            part = got[b, a, 32 * half : 32 * half + 32]
            w_qkv[rows] = part[:, 0:QKV_COLS]
            w_out[rows] = part[:, QKV_COLS : QKV_COLS + OUT_COLS]
            extra[rows] = part[:, QKV_COLS + OUT_COLS :].astype(F32)
    vec[...] = extra[...].T[0:16]


def bias_hot(c):
    row, col = iota((128, 256), 0), iota((128, 256), 1)
    hit = (col // 16 == row // 8) & (col % 16 == 8 * c + row % 8)
    return jnp.where(hit, 1.0, 0.0).astype(BF)


def plane_place(core, zx):
    z, x = zx // 4, zx % 4
    return jnp.where(core == 0, x, z), jnp.where(core == 0, z, x)


def head_mask(h):
    return iota((1, 256), 1) // 64 == h


def masked(v, h):
    return jnp.where(head_mask(h), v, jnp.zeros_like(v))


def key_keep(x_own, x_yp, x_cp, x_dg):
    refs = (x_own, x_yp, x_cp, x_dg)
    return sum(r[TOK + b : TOK + b + 1, 0:ROWS].astype(F32) for b, r in enumerate(refs)) > 0


def attend_kernel(seq, x_own, x_yp, x_cp, x_dg, w, vec, n1, qkv, o, lse):
    s = seq[0]
    gain, shift = vec[0:1], vec[1:2]
    for b, ref in enumerate((x_own, x_yp, x_cp, x_dg)):
        normed, _ = norm_stats(ref[...].astype(F32))
        n1[block(b)] = (normed * gain + shift).astype(BF)
    biases = []
    for start in (0, 512):
        at = pl.ds(pl.multiple_of(start + 128 * s, 128), 128)
        pieces = [jnp.broadcast_to(vec[2 + c : 3 + c, at], (8, 128)).astype(BF) for c in (0, 1)]
        biases.append((dot(pieces[0], bias_hot(0)) + dot(pieces[1], bias_hot(1)))[0:1])
    for i, bias in enumerate((biases[0], None, biases[1])):
        at = slice(256 * i, 256 * i + 256)
        proj = dot(n1[...], w[:, at])
        qkv[:, at] = (proj if bias is None else proj + bias).astype(BF)
    keep = key_keep(x_own, x_yp, x_cp, x_dg)
    q = qkv[:, 0:256] * jnp.asarray(0.125, BF)
    k, v = qkv[:, 256:512], qkv[:, 512:768]
    total = jnp.zeros((ROWS, 256), F32)
    logs = jnp.zeros((ROWS, 128), F32)
    for h in range(4):
        scores = jnp.where(keep, dot_t(masked(q, h), k), -1e30)
        peak = jnp.max(scores, axis=1, keepdims=True)
        powers = jnp.exp(scores - peak)
        weight = jnp.sum(powers, axis=1, keepdims=True)
        probs = (powers * (1.0 / weight)).astype(BF)
        total = total + dot(probs, masked(v, h))
        logs = jnp.where(iota((ROWS, 128), 1) == h, peak + jnp.log(weight), logs)
    o[...] = total.astype(BF)
    lse[...] = logs


def hidden_kernel(
    seq,
    places,
    o_own,
    o_yp,
    o_cp,
    o_dg,
    x_own,
    x_yp,
    x_cp,
    x_dg,
    w_own,
    w_yp,
    w_cp,
    w_dg,
    vec,
    line_own,
    line_1,
    line_2,
    line_3,
    g_own,
    g_yp,
    g_cp,
    g_dg,
    n2,
    z,
    du,
    dn2_mine,
    dn2_theirs,
    normed_out,
    scale_out,
    down,
    r_own,
    r,
    up,
    dm,
):
    s = seq[0]
    place = [jnp.bitwise_xor(s, m) for m in RELATIVE]
    for b, ref in enumerate((g_own, g_yp, g_cp, g_dg)):
        dm[block(b)] = ref[...]
    heads = []
    for j, ref in enumerate((o_own, o_yp, o_cp, o_dg)):
        heads.append(jnp.concatenate([ref[block(b ^ j)] for b in range(4)], axis=0))
    for c, w in enumerate((w_own, w_yp, w_cp, w_dg)):
        total = jnp.zeros((ROWS, 256), F32)
        for j in range(4):
            rows = pl.ds(pl.multiple_of(256 * place[j], 256), 256)
            total = total + dot(heads[j], w[rows, :])
        r[:, pl.ds(pl.multiple_of(256 * place[c], 256), 256)] = total
    gain, shift, b_out = vec[5:6], vec[6:7], vec[4:5]
    for b, ref in enumerate((x_own, x_yp, x_cp, x_dg)):
        rows = r[block(b)] + ref[...].astype(F32) + b_out
        if b == 0:
            r_own[...] = rows
        normed, scale = norm_stats(rows)
        n2[block(b)] = (normed * gain + shift).astype(BF)
        if b < 2:
            normed_out[block(b)] = normed
            scale_out[block(b)] = jnp.broadcast_to(scale, (PAD, 128))
    bias = vec[pl.ds(7 + s, 1)]
    for by, ref in enumerate((line_own, line_1, line_2, line_3)):
        b = lax.rem(places[1] + 4 - by, 4)
        for a in range(4):
            zx = jnp.where(s % 2 == 0, 4 * b + a, 4 * a + b)
            for half in range(2):
                rows = pl.ds(pl.multiple_of(512 * half + 32 * zx, 32), 32)
                up[rows] = ref[a, 32 * half : 32 * half + 32, 0:1024]
                down[rows] = ref[a, 32 * half : 32 * half + 32, 1024:]
    for c in range(4):
        at = slice(256 * c, 256 * c + 256)
        u = dot(n2[...], up[:, at]) + bias[:, at]
        cdf = 0.5 * (1.0 + lax.erf(u * (0.5**0.5)))
        z[:, at] = (u * cdf).astype(BF)
        slope = cdf + u * jnp.exp(-0.5 * u * u) * 0.3989422804014327
        du[:, at] = (slope * dot_t(dm[...], down[at, :])).astype(BF)
    dn2_mine[...] = dot_t(du[0:HALF], up[...])
    dn2_theirs[...] = dot_t(du[HALF:], up[...]).astype(BF)


def hidden_grad_kernel(
    core, z, du, n2, down, g_own, g_yp, g_cp, g_dg, out, small, y_own, y_two, y_theirs
):
    y_own[...] = dot(z[block(0)], down[...])
    y_two[...] = dot(z[block(1)], down[...]).astype(BF)
    y_theirs[...] = dot(z[HALF:], down[...]).astype(BF)
    dm = jnp.concatenate([g[...] for g in (g_own, g_yp, g_cp, g_dg)], axis=0)
    d_up = t_dot(n2[...], du[...]).astype(BF)
    d_down = t_dot(z[...], dm).astype(BF)
    for zx in range(16):
        a, b = plane_place(core[0], zx)
        for half in range(2):
            rows = slice(512 * half + 32 * zx, 512 * half + 32 * zx + 32)
            out[a, b, 32 * half : 32 * half + 32, 0:1024] = d_up[rows]
            out[a, b, 32 * half : 32 * half + 32, 1024:] = d_down[rows]
    small[...] = jnp.zeros((8, WIDTH), F32)
    small[0:1] = jnp.sum(du[...].astype(F32), axis=0, keepdims=True)
    small[1:2] = jnp.sum(g_own[...].astype(F32), axis=0, keepdims=True)


def residual_kernel(two, got, g_own, g_yp, normed, scale, vec, da, dr, small):
    gain = vec[5:6]
    small[...] = jnp.zeros((8, WIDTH), F32)
    for b, ref in enumerate((g_own, g_yp)):
        dn2 = two[block(b)].astype(F32) + got[block(1 - b)].astype(F32)
        grad = ref[...].astype(F32) + norm_back(dn2, gain, normed[block(b)], scale[block(b), 0:1])
        low = grad.astype(BF)
        da[block(b)] = low
        if b == 0:
            dr[...] = grad
            small[0:1] = jnp.sum(low.astype(F32), axis=0, keepdims=True)
            small[1:2] = jnp.sum(dn2 * normed[block(b)], axis=0, keepdims=True)
            small[2:3] = jnp.sum(dn2, axis=0, keepdims=True)


def attend_grad_kernel(
    seq,
    core,
    da_mine,
    da_cp,
    w_own,
    w_yp,
    w_cp,
    w_dg,
    x_own,
    x_yp,
    x_cp,
    x_dg,
    qkv_w,
    qkv,
    lse,
    n1,
    o_own,
    o_yp,
    o_cp,
    o_dg,
    small_b,
    small_c,
    dn1_own,
    dn1_two,
    dn1_theirs,
    send,
    da,
    d_proj,
    rows_out,
    natural,
):
    s = seq[0]
    place = [jnp.bitwise_xor(s, m) for m in RELATIVE]
    da[0:HALF] = da_mine[...]
    da[HALF:] = da_cp[...]
    own_rows = pl.ds(pl.multiple_of(256 * s, 256), 256)
    grad_o = jnp.zeros((ROWS, 256), F32)
    for c, w in enumerate((w_own, w_yp, w_cp, w_dg)):
        cols = pl.ds(pl.multiple_of(256 * place[c], 256), 256)
        grad_o = grad_o + dot_t(da[:, cols], w[own_rows, :])
    do = grad_o.astype(BF)
    keep = key_keep(x_own, x_yp, x_cp, x_dg)
    q, k, v = qkv[:, 0:256], qkv[:, 256:512], qkv[:, 512:768]
    scaled = q * jnp.asarray(0.125, BF)
    keep_rows = jnp.broadcast_to(keep.astype(F32), (128, ROWS)).T[:, 0:1] > 0
    lse_cols = lse[...].T
    dq, dk, dv = (jnp.zeros((ROWS, 256), F32) for _ in range(3))
    for h in range(4):
        scores = jnp.where(keep_rows, dot_t(k, masked(scaled, h)), -1e30)
        probs = jnp.exp(scores - lse_cols[h : h + 1])
        do_h = masked(do, h)
        d_probs = dot_t(v, do_h)
        inner = jnp.sum(probs * d_probs, axis=0, keepdims=True)
        ds = (probs * (d_probs - inner)).astype(BF)
        dq = dq + t_dot(ds, masked(k, h))
        dk = dk + dot(ds, masked(q, h))
        dv = dv + dot(probs.astype(BF), do_h)
    d_proj[:, 0:256] = (dq * 0.125).astype(BF)
    d_proj[:, 256:512] = (dk * 0.125).astype(BF)
    d_proj[:, 512:768] = dv.astype(BF)
    d_gain = jnp.zeros((1, WIDTH), F32)
    d_shift = jnp.zeros((1, WIDTH), F32)
    for b, ref in enumerate((x_own, x_yp, x_cp, x_dg)):
        normed, _ = norm_stats(ref[...].astype(F32))
        part = dot_t(d_proj[block(b)], qkv_w[:, 0:QKV_COLS])
        d_gain = d_gain + jnp.sum(part * normed, axis=0, keepdims=True)
        d_shift = d_shift + jnp.sum(part, axis=0, keepdims=True)
        if b == 0:
            dn1_own[...] = part
        elif b == 1:
            dn1_two[...] = part.astype(BF)
        else:
            dn1_theirs[block(b - 2)] = part.astype(BF)
    natural[:, 0:QKV_COLS] = t_dot(n1[...], d_proj[...]).astype(BF)
    my_cols = pl.ds(pl.multiple_of(256 * s, 256), 256)
    for j, ref in enumerate((o_own, o_yp, o_cp, o_dg)):
        heads = jnp.concatenate([ref[block(b ^ j)] for b in range(4)], axis=0)
        rows = pl.ds(pl.multiple_of(256 * place[j], 256), 256)
        natural[rows, QKV_COLS : QKV_COLS + OUT_COLS] = t_dot(heads, da[:, my_cols]).astype(BF)
    rows_out[...] = jnp.zeros((EXTRA, WIDTH), F32)
    rows_out[0:1] = d_gain
    rows_out[1:2] = d_shift
    for start, first in ((0, 0), (512, 512)):
        sums = jnp.sum(d_proj[:, first : first + 256].astype(F32), axis=0, keepdims=True)
        sums = jnp.broadcast_to(sums, (8, 256)).astype(BF)
        at = pl.ds(pl.multiple_of(start + 128 * s, 128), 128)
        for c in (0, 1):
            rows_out[2 + c : 3 + c, at] = dot_t(sums, bias_hot(c))[0:1]
    rows_out[4:7] = small_c[0:3]
    rows_out[pl.ds(7 + s, 1)] = small_b[0:1]
    rows_out[11:12] = small_b[1:2]
    natural[:, QKV_COLS + OUT_COLS :] = rows_out[...].T.astype(BF)
    for zx in range(16):
        a, b = plane_place(core[0], zx)
        for half in range(2):
            rows = slice(512 * half + 32 * zx, 512 * half + 32 * zx + 32)
            send[a, b, 32 * half : 32 * half + 32] = natural[rows]


def input_grad_kernel(mine, got_cp, got_yp, dr, x_own, vec, out):
    normed, scale = norm_stats(x_own[...].astype(F32))
    dn1 = mine[...] + got_cp[block(0)].astype(F32) + got_yp[...].astype(F32)
    grad = dr[...] + norm_back(dn1, vec[0:1], normed, scale)
    out[:, 0] = grad[0:TOK]


def output_kernel(mine, got_cp, got_yp, r, vec, out):
    y = mine[...] + got_cp[block(0)].astype(F32) + got_yp[...].astype(F32)
    out[0] = (y + r[...] + vec[11:12])[0:TOK].astype(BF)


def sum_of(ref):
    total = ref[0].astype(F32)
    for d in range(1, ref.shape[0]):
        total = total + ref[d].astype(F32)
    return total


def sum_low_kernel(got, out):
    out[...] = sum_of(got).astype(BF)


def sum_line_kernel(places, got, own, to_1, to_2, to_3, total):
    total[...] = sum_of(got)
    own[...] = total[places[1]]
    for by, ref in ((1, to_1), (2, to_2), (3, to_3)):
        ref[...] = total[lax.rem(places[1] + by, 4)].astype(BF)


def sum_join_kernel(got, own, got_1, got_2, got_3, out):
    out[:, 0:REST] = sum_of(got).astype(BF)
    hidden = own[...]
    for ref in (got_1, got_2, got_3):
        hidden = hidden + ref[...].astype(F32)
    out[:, REST:] = hidden.astype(BF)


def sum_rest_kernel(got, down, up, qkv, out, *vectors):
    total = jnp.concatenate(
        [got[s].astype(F32) + got[4 + s].astype(F32) for s in range(4)], axis=0
    )
    down[0] = total[:, REST + 1024 :]
    cols = [
        jnp.concatenate(
            [
                total[8 * s : 8 * s + 8, REST + 128 * t : REST + 128 * t + 128]
                for s in range(4)
            ],
            axis=1,
        )
        for t in range(8)
    ]
    cols = jnp.concatenate(cols, axis=0)
    high = cols.astype(BF)
    low = (cols - high.astype(F32)).astype(BF)
    natural = dot_t(high, hidden_hot()) + dot_t(low, hidden_hot())
    for t in range(8):
        up[0, :, 512 * t : 512 * t + 512] = natural[8 * t : 8 * t + 8]
    for s in range(4):
        rows = slice(8 * s, 8 * s + 8)
        for i in range(3):
            at = 1024 * i + 256 * s
            qkv[0, :, at : at + 256] = total[rows, 256 * i : 256 * i + 256]
        out[0, :, 256 * s : 256 * s + 256] = total[rows, QKV_COLS : QKV_COLS + OUT_COLS]
    extra = sum(total[8 * s : 8 * s + 8, QKV_COLS + OUT_COLS : REST] for s in range(4))
    place = 0
    for ref in vectors:
        size = ref.shape[1]
        value = jnp.zeros((8, size), F32)
        for c in range(size // 8):
            column = jnp.broadcast_to(extra[:, place : place + 1], (8, size))
            hit = iota((8, size), 1) == iota((8, size), 0) + 8 * c
            value = jnp.where(hit, column, value)
            place += 1
        ref[...] = jnp.sum(value, axis=0, keepdims=True)


def body(
    inputs,
    token_mask,
    first_gain,
    first_shift,
    qkv_weight,
    qv_bias,
    out_weight,
    out_bias,
    second_gain,
    second_shift,
    up_weight,
    up_bias,
    down_weight,
    down_bias,
    cotangent,
):
    core = lax.axis_index("core").astype(jnp.int32).reshape(1)
    seq = lax.axis_index("yhi").astype(jnp.int32).reshape(1) * 2 + core
    z_place, x_place = lax.axis_index("z"), lax.axis_index("x")
    places = jnp.where(
        core == 0, jnp.stack([x_place, z_place]), jnp.stack([z_place, x_place])
    ).astype(jnp.int32)

    (send,) = call(
        prepare_kernel,
        [((2, 4, 8, JOINT), BF)],
        *hbm(
            qkv_weight,
            out_weight,
            up_weight,
            down_weight,
            first_gain,
            first_shift,
            qv_bias,
            out_bias,
            second_gain,
            second_shift,
            up_bias,
            down_bias,
        ),
    )
    x, g = call(
        tokens_kernel,
        [((PAD, WIDTH), BF, HBM), ((PAD, WIDTH), BF, HBM)],
        *hbm(inputs, token_mask, cotangent),
        scratch=[pltpu.VMEM((PAD, WIDTH), F32)],
        us=2,
        deps=(send,),
    )
    pieces = lax.all_to_all(
        send.reshape(64, JOINT), ("ylo", "yhi", "core"), 0, 0, tiled=True
    )
    x_yp, g_yp = over_y(x), over_y(g)
    x_cp, g_cp = over_core(x), over_core(g)
    (send,) = call(spread_kernel, [((4, 64, JOINT), BF)], pieces, deps=(x_cp, g_cp))
    pieces = exchange(send.reshape(256, JOINT), STAGE_A)
    send, line = call(
        line_kernel,
        [((4, 256, REST), BF, HBM), ((256, 2048), BF)],
        pieces,
        deps=(x_yp,),
    )
    got = exchange(send.reshape(1024, REST), STAGE_B)
    line = after(line, g_yp).reshape(4, 64, 2048)
    lines = [line] + [shift(line, STAGE_B, by) for by in (1, 2, 3)]
    xs = (x, x_yp, x_cp, over_core(x_yp))
    gs = (g, g_yp, g_cp, over_core(g_yp))
    w_qkv, w_own, vec = call(
        unpack_kernel,
        [((1024, QKV_COLS), BF), ((1024, OUT_COLS), BF), ((16, WIDTH), F32)],
        core,
        got.reshape(4, 4, 64, REST),
        scratch=[pltpu.VMEM((1024, EXTRA), F32)],
        scalars=1,
        deps=(g_yp,),
    )
    w_yp = over_y(w_own)
    ws = (w_own, w_yp, over_core(w_own), over_core(w_yp))

    n1, qkv, o, lse = call(
        attend_kernel,
        [
            ((ROWS, WIDTH), BF, HBM),
            ((ROWS, QKV_COLS), BF, HBM),
            ((ROWS, 256), BF, HBM),
            ((ROWS, 128), F32, HBM),
        ],
        seq,
        *xs,
        w_qkv,
        vec,
        scalars=1,
        us=8,
    )
    o_yp = over_y(o)
    os = (o, o_yp, over_core(o), over_core(o_yp))
    n2, z, du, dn2_mine, dn2_theirs, normed_2, scale_2, down_w, r = call(
        hidden_kernel,
        [
            ((ROWS, WIDTH), BF),
            ((ROWS, WIDTH), BF),
            ((ROWS, WIDTH), BF),
            ((HALF, WIDTH), F32),
            ((HALF, WIDTH), BF),
            ((HALF, WIDTH), F32, HBM),
            ((HALF, 128), F32, HBM),
            ((1024, WIDTH), BF),
            ((PAD, WIDTH), F32, HBM),
        ],
        seq,
        places,
        *hbm(o),
        *os[1:],
        *xs,
        *ws,
        vec,
        *lines,
        *gs,
        scratch=[
            pltpu.VMEM((ROWS, WIDTH), F32),
            pltpu.VMEM((1024, WIDTH), BF),
            pltpu.VMEM((ROWS, WIDTH), BF),
        ],
        scalars=2,
        us=12,
    )
    two = (dn2_mine + over_core(dn2_theirs).astype(F32)).astype(BF)
    two_yp = over_y(two)
    d_hidden, small_b, y_own, y_two, y_theirs = call(
        hidden_grad_kernel,
        [
            ((4, 4, 64, 2048), BF, HBM),
            ((8, WIDTH), F32),
            ((PAD, WIDTH), F32, HBM),
            ((PAD, WIDTH), BF, HBM),
            ((HALF, WIDTH), BF, HBM),
        ],
        core,
        z,
        du,
        n2,
        down_w,
        *gs,
        scalars=1,
        deps=(two,),
        us=300,
    )
    d_hidden = exchange(d_hidden.reshape(1024, 2048), STAGE_A)
    y_cp = over_core(y_theirs)
    da, dr, small_c = call(
        residual_kernel,
        [((HALF, WIDTH), BF), ((PAD, WIDTH), F32, HBM), ((8, WIDTH), F32)],
        two,
        two_yp,
        g,
        g_yp,
        *hbm(normed_2, scale_2),
        vec,
        deps=(y_theirs,),
        us=150,
    )
    da_cp = over_core(da)
    y_low = (y_two.astype(F32) + y_cp[PAD:].astype(F32)).astype(BF)
    y_yp = over_y(y_low)
    dn1_own, dn1_two, dn1_theirs, send = call(
        attend_grad_kernel,
        [
            ((PAD, WIDTH), F32, HBM),
            ((PAD, WIDTH), BF, HBM),
            ((HALF, WIDTH), BF, HBM),
            ((4, 4, 64, REST), BF, HBM),
        ],
        seq,
        core,
        da,
        da_cp,
        *ws,
        *xs,
        *hbm(w_qkv, qkv, lse, n1),
        *os,
        small_b,
        small_c,
        scratch=[
            pltpu.VMEM((ROWS, WIDTH), BF),
            pltpu.VMEM((ROWS, QKV_COLS), BF),
            pltpu.VMEM((EXTRA, WIDTH), F32),
            pltpu.VMEM((1024, REST), BF),
        ],
        scalars=2,
        us=15,
    )
    got = exchange(after(send.reshape(1024, REST), d_hidden), STAGE_A)
    dn1_cp = over_core(dn1_theirs)
    dn1_low = (dn1_two.astype(F32) + dn1_cp[PAD:].astype(F32)).astype(BF)
    dn1_yp = over_y(dn1_low)
    hidden_own, *parts = call(
        sum_line_kernel,
        [((64, 2048), F32)] + [((64, 2048), BF)] * 3,
        places,
        d_hidden.reshape(4, 4, 64, 2048),
        scratch=[pltpu.VMEM((4, 64, 2048), F32)],
        scalars=1,
    )
    parts = [shift(part, STAGE_B, by) for by, part in zip((1, 2, 3), parts)]
    (send,) = call(
        sum_low_kernel, [((256, REST), BF, HBM)], got.reshape(4, 256, REST), deps=(dn1_low, y_yp, hidden_own)
    )
    got = exchange(send, STAGE_B)
    (send,) = call(
        sum_join_kernel,
        [((64, JOINT), BF)],
        got.reshape(4, 64, REST),
        hidden_own,
        *parts,
        deps=(dn1_yp,),
    )
    got = lax.all_to_all(send, ("ylo", "yhi", "core"), 0, 0, tiled=True)
    (block_output,) = call(
        output_kernel, [((1, TOK, WIDTH), BF)], *hbm(y_own, y_cp, y_yp, r), vec
    )
    (g0,) = call(
        input_grad_kernel,
        [((TOK, 1, WIDTH), F32)],
        *hbm(dn1_own, dn1_cp, dn1_yp, dr, x),
        vec,
    )
    g0 = g0.transpose(1, 0, 2)
    d_down, d_up, d_qkv, d_out, d_fg, d_fs, d_qvb, d_ob, d_sg, d_ss, d_ub, d_db = call(
        sum_rest_kernel,
        [
            ((1, 32, WIDTH), F32),
            ((1, 8, 4096), F32),
            ((1, 8, 3072), F32),
            ((1, 8, WIDTH), F32),
        ]
        + [((1, n), F32) for n in (8, 8, 16, 8, 8, 8, 32, 8)],
        got.reshape(8, 8, JOINT),
        deps=(block_output, g0),
    )
    return (
        block_output,
        g0,
        d_fg,
        d_fs,
        d_qkv,
        d_qvb,
        d_out,
        d_ob,
        d_sg,
        d_ss,
        d_up,
        d_ub,
        d_down,
        d_db,
    )


def solution(mesh):
    fine = Mesh(mesh.devices.reshape(2, 4, 4, 2, 2), ALL)
    tokens = P(DP, SEQ, None)
    vector = P(None, ALL)
    matrix = P(None, ALL, None)
    return jax.shard_map(
        body,
        mesh=fine,
        in_specs=(
            tokens,
            P(DP, SEQ),
            vector,
            vector,
            matrix,
            vector,
            matrix,
            vector,
            vector,
            vector,
            matrix,
            vector,
            matrix,
            vector,
            tokens,
        ),
        out_specs=(
            tokens,
            tokens,
            vector,
            vector,
            matrix,
            vector,
            matrix,
            vector,
            vector,
            vector,
            matrix,
            vector,
            matrix,
            vector,
        ),
        check_vma=False,
    )
```

```python
import functools

import jax
import jax.numpy as jnp
from jax import lax
from jax.experimental import pallas as pl
from jax.experimental.pallas import tpu as pltpu
from jax.sharding import Mesh, PartitionSpec as P

TOK = 145
PAD = 160
ROWS = 4 * PAD
HALF = 2 * PAD
SCALE = 1e9
HBM = pltpu.HBM
WIDTH = 1024
BF = jnp.bfloat16
F32 = jnp.float32
DP = ("ylo", "z", "x")
SEQ = ("yhi", "core")
ALL = DP + SEQ
SWAP = [(0, 1), (1, 0)]
RELATIVE = (0, 2, 1, 3)
QKV_COLS = 768
OUT_COLS = 256
EXTRA = 128
REST = QKV_COLS + OUT_COLS + EXTRA
JOINT = REST + 2048


LINES_X = [[[(r * 4 + z) * 4 + x for x in range(4)] for z in range(4)] for r in range(2)]
LINES_Z = [[[(r * 4 + z) * 4 + x for z in range(4)] for x in range(4)] for r in range(2)]


def lines(along):
    return [
        [place * 4 + 2 * yhi + core for place in line]
        for core in range(2)
        for yhi in range(2)
        for half in along[core]
        for line in half
    ]


STAGE_A = lines((LINES_X, LINES_Z))
STAGE_B = lines((LINES_Z, LINES_X))


def exchange(v, groups):
    return lax.all_to_all(v, ALL, 0, 0, axis_index_groups=groups, tiled=True)


def shift(v, groups, by):
    pairs = [(line[i], line[(i + by) % 4]) for line in groups for i in range(4)]
    return lax.ppermute(v, ALL, pairs)


def over_y(v):
    return lax.ppermute(v, "yhi", SWAP)


def over_core(v):
    return lax.ppermute(v, "core", SWAP)


def dot(a, b):
    return jnp.dot(a, b, preferred_element_type=F32)


def dot_t(a, b):
    return lax.dot_general(a, b, (((1,), (1,)), ((), ())), preferred_element_type=F32)


def t_dot(a, b):
    return lax.dot_general(a, b, (((0,), (0,)), ((), ())), preferred_element_type=F32)


def iota(shape, dim):
    return lax.broadcasted_iota(jnp.int32, shape, dim)


def call(kernel, outs, *args, scratch=(), scalars=0, deps=(), us=0.0, room=32):
    vmem = pl.BlockSpec(memory_space=pltpu.VMEM)
    specs = [pl.BlockSpec(memory_space=pltpu.SMEM)] * scalars + [vmem] * (len(args) - scalars)
    specs += [pl.BlockSpec(memory_space=pl.ANY)] * len(deps)

    def run(*refs):
        kernel(*refs[: len(args)], *refs[len(args) + len(deps) :])

    return pl.pallas_call(
        run,
        out_shape=[(o[2] if len(o) > 2 else jax.ShapeDtypeStruct)(o[0], o[1]) for o in outs],
        in_specs=specs,
        out_specs=[vmem] * len(outs),
        scratch_shapes=list(scratch),
        compiler_params=pltpu.CompilerParams(vmem_limit_bytes=room * 2**20),
        cost_estimate=pl.CostEstimate(
            flops=int(us * SCALE), bytes_accessed=0, transcendentals=0
        ),
        name=getattr(kernel, "func", kernel).__name__.removesuffix("_kernel"),
    )(*args, *deps)


def hbm(*values):
    return tuple(pltpu.with_memory_space_constraint(v, HBM) for v in values)


def after(v, *deps):
    anywhere = pl.BlockSpec(memory_space=pl.ANY)
    return pl.pallas_call(
        lambda *refs: None,
        out_shape=jax.ShapeDtypeStruct(v.shape, v.dtype),
        in_specs=[anywhere] * (1 + len(deps)),
        out_specs=anywhere,
        input_output_aliases={0: 0},
        cost_estimate=pl.CostEstimate(flops=0, bytes_accessed=0, transcendentals=0),
        name="after",
    )(v, *deps)


def block(b):
    return slice(b * PAD, (b + 1) * PAD)


def norm_stats(v):
    average = jnp.mean(v, axis=-1, keepdims=True)
    centred = v - average
    variance = jnp.mean(centred * centred, axis=-1, keepdims=True)
    scale = lax.rsqrt(variance + 1e-06)
    return centred * scale, scale


def norm_back(grad, gain, normed, scale):
    e = grad * gain
    return scale * (
        e
        - jnp.mean(e, axis=-1, keepdims=True)
        - normed * jnp.mean(e * normed, axis=-1, keepdims=True)
    )


def piece_columns(refs):
    out = jnp.zeros((8, EXTRA), F32)
    lane = iota((8, EXTRA), 1)
    place = 0
    for ref in refs:
        size = ref.shape[1]
        for c in range(size // 8):
            spread = jnp.broadcast_to(ref[...].astype(F32), (8, size))
            hit = iota((8, size), 1) == iota((8, size), 0) + 8 * c
            column = jnp.sum(jnp.where(hit, spread, 0.0), axis=1, keepdims=True)
            out = jnp.where(lane == place, column, out)
            place += 1
    return out


def hidden_hot():
    row, col = iota((512, 512), 0), iota((512, 512), 1)
    hit = row == 32 * (col % 128 // 8) + 8 * (col // 128) + col % 8
    return jnp.where(hit, 1.0, 0.0).astype(BF)


def tokens_kernel(x, mask, g, out, g_out, tok):
    row = jnp.zeros((8, WIDTH), F32)
    tok[0:8] = row
    tok[0:1, 0:TOK] = mask[...].astype(F32)
    row = tok[0:8]
    lifted = [pltpu.roll(row, PAD * b, 1)[0:1] if b else row[0:1] for b in range(4)]
    tok[0:TOK] = x[0].astype(F32)
    for b in range(4):
        tok[TOK + b : TOK + b + 1] = lifted[b]
    tok[TOK + 4 :] = jnp.zeros((PAD - TOK - 4, WIDTH), F32)
    out[...] = tok[...].astype(BF)
    tok[0:TOK] = g[0].astype(F32)
    tok[TOK:] = jnp.zeros((PAD - TOK, WIDTH), F32)
    g_out[...] = tok[...].astype(BF)


def prepare_kernel(qkv, out_w, up, down, fg, fs, qvb, ob, sg, ss, ub, db, send):
    extra = piece_columns([fg, fs, qvb, ob, sg, ss, ub, db])
    rows = jnp.concatenate([up[0, :, 512 * t : 512 * t + 512] for t in range(8)], axis=0)
    up_cols = dot(rows, hidden_hot())
    for s in range(4):
        parts = [qkv[0, :, 1024 * i + 256 * s : 1024 * i + 256 * s + 256] for i in range(3)]
        parts = [p.astype(F32) for p in parts]
        parts.append(out_w[0, :, 256 * s : 256 * s + 256].astype(F32))
        parts.append(extra)
        parts += [up_cols[8 * t : 8 * t + 8, 128 * s : 128 * s + 128] for t in range(8)]
        parts.append(down[0, 8 * s : 8 * s + 8].astype(F32))
        piece = jnp.concatenate(parts, axis=1).astype(BF)
        for b in range(2):
            send[b, s] = piece


def spread_kernel(pieces, out):
    for d in range(4):
        out[d] = pieces[...]


def line_kernel(got, attend, hidden):
    for d in range(4):
        attend[d] = got[:, 0:REST]
    hidden[...] = got[:, REST:]


def unpack_kernel(core, got, w_qkv, w_out, vec, extra):
    for zx in range(16):
        a, b = plane_place(core[0], zx)
        for half in range(2):
            rows = slice(512 * half + 32 * zx, 512 * half + 32 * zx + 32)
            part = got[b, a, 32 * half : 32 * half + 32]
            w_qkv[rows] = part[:, 0:QKV_COLS]
            w_out[rows] = part[:, QKV_COLS : QKV_COLS + OUT_COLS]
            extra[rows] = part[:, QKV_COLS + OUT_COLS :].astype(F32)
    vec[...] = extra[...].T[0:16]


def bias_hot(c):
    row, col = iota((128, 256), 0), iota((128, 256), 1)
    hit = (col // 16 == row // 8) & (col % 16 == 8 * c + row % 8)
    return jnp.where(hit, 1.0, 0.0).astype(BF)


def plane_place(core, zx):
    z, x = zx // 4, zx % 4
    return jnp.where(core == 0, x, z), jnp.where(core == 0, z, x)


def head_mask(h):
    return iota((1, 256), 1) // 64 == h


def masked(v, h):
    return jnp.where(head_mask(h), v, jnp.zeros_like(v))


def key_keep(x_own, x_yp, x_cp, x_dg):
    refs = (x_own, x_yp, x_cp, x_dg)
    return sum(r[TOK + b : TOK + b + 1, 0:ROWS].astype(F32) for b, r in enumerate(refs)) > 0


def attend_kernel(seq, x_own, x_yp, x_cp, x_dg, w, vec, n1, qkv, o, lse):
    s = seq[0]
    gain, shift = vec[0:1], vec[1:2]
    for b, ref in enumerate((x_own, x_yp, x_cp, x_dg)):
        normed, _ = norm_stats(ref[...].astype(F32))
        n1[block(b)] = (normed * gain + shift).astype(BF)
    biases = []
    for start in (0, 512):
        at = pl.ds(pl.multiple_of(start + 128 * s, 128), 128)
        pieces = [jnp.broadcast_to(vec[2 + c : 3 + c, at], (8, 128)).astype(BF) for c in (0, 1)]
        biases.append((dot(pieces[0], bias_hot(0)) + dot(pieces[1], bias_hot(1)))[0:1])
    for i, bias in enumerate((biases[0], None, biases[1])):
        at = slice(256 * i, 256 * i + 256)
        proj = dot(n1[...], w[:, at])
        qkv[:, at] = (proj if bias is None else proj + bias).astype(BF)
    keep = key_keep(x_own, x_yp, x_cp, x_dg)
    q = qkv[:, 0:256] * jnp.asarray(0.125, BF)
    k, v = qkv[:, 256:512], qkv[:, 512:768]
    total = jnp.zeros((ROWS, 256), F32)
    logs = jnp.zeros((ROWS, 128), F32)
    for h in range(4):
        scores = jnp.where(keep, dot_t(masked(q, h), k), -1e30)
        peak = jnp.max(scores, axis=1, keepdims=True)
        powers = jnp.exp(scores - peak)
        weight = jnp.sum(powers, axis=1, keepdims=True)
        probs = (powers * (1.0 / weight)).astype(BF)
        total = total + dot(probs, masked(v, h))
        logs = jnp.where(iota((ROWS, 128), 1) == h, peak + jnp.log(weight), logs)
    o[...] = total.astype(BF)
    lse[...] = logs


def hidden_kernel(
    seq,
    places,
    o_own,
    o_yp,
    o_cp,
    o_dg,
    x_own,
    x_yp,
    x_cp,
    x_dg,
    w_own,
    w_yp,
    w_cp,
    w_dg,
    vec,
    line_own,
    line_1,
    line_2,
    line_3,
    g_own,
    g_yp,
    g_cp,
    g_dg,
    n2,
    z,
    du,
    dn2_mine,
    dn2_theirs,
    normed_out,
    scale_out,
    down,
    r_own,
    r,
    up,
    dm,
):
    s = seq[0]
    place = [jnp.bitwise_xor(s, m) for m in RELATIVE]
    for b, ref in enumerate((g_own, g_yp, g_cp, g_dg)):
        dm[block(b)] = ref[...]
    heads = []
    for j, ref in enumerate((o_own, o_yp, o_cp, o_dg)):
        heads.append(jnp.concatenate([ref[block(b ^ j)] for b in range(4)], axis=0))
    for c, w in enumerate((w_own, w_yp, w_cp, w_dg)):
        total = jnp.zeros((ROWS, 256), F32)
        for j in range(4):
            rows = pl.ds(pl.multiple_of(256 * place[j], 256), 256)
            total = total + dot(heads[j], w[rows, :])
        r[:, pl.ds(pl.multiple_of(256 * place[c], 256), 256)] = total
    gain, shift, b_out = vec[5:6], vec[6:7], vec[4:5]
    for b, ref in enumerate((x_own, x_yp, x_cp, x_dg)):
        rows = r[block(b)] + ref[...].astype(F32) + b_out
        if b == 0:
            r_own[...] = rows
        normed, scale = norm_stats(rows)
        n2[block(b)] = (normed * gain + shift).astype(BF)
        if b < 2:
            normed_out[block(b)] = normed
            scale_out[block(b)] = jnp.broadcast_to(scale, (PAD, 128))
    bias = vec[pl.ds(7 + s, 1)]
    for by, ref in enumerate((line_own, line_1, line_2, line_3)):
        b = lax.rem(places[1] + 4 - by, 4)
        for a in range(4):
            zx = jnp.where(s % 2 == 0, 4 * b + a, 4 * a + b)
            for half in range(2):
                rows = pl.ds(pl.multiple_of(512 * half + 32 * zx, 32), 32)
                up[rows] = ref[a, 32 * half : 32 * half + 32, 0:1024]
                down[rows] = ref[a, 32 * half : 32 * half + 32, 1024:]
    for c in range(4):
        at = slice(256 * c, 256 * c + 256)
        u = dot(n2[...], up[:, at]) + bias[:, at]
        cdf = 0.5 * (1.0 + lax.erf(u * (0.5**0.5)))
        z[:, at] = (u * cdf).astype(BF)
        slope = cdf + u * jnp.exp(-0.5 * u * u) * 0.3989422804014327
        du[:, at] = (slope * dot_t(dm[...], down[at, :])).astype(BF)
    dn2_mine[...] = dot_t(du[0:HALF], up[...])
    dn2_theirs[...] = dot_t(du[HALF:], up[...]).astype(BF)


def hidden_grad_kernel(
    core, z, du, n2, down, g_own, g_yp, g_cp, g_dg, out, small, y_own, y_two, y_theirs
):
    y_own[...] = dot(z[block(0)], down[...])
    y_two[...] = dot(z[block(1)], down[...]).astype(BF)
    y_theirs[...] = dot(z[HALF:], down[...]).astype(BF)
    dm = jnp.concatenate([g[...] for g in (g_own, g_yp, g_cp, g_dg)], axis=0)
    d_up = t_dot(n2[...], du[...]).astype(BF)
    d_down = t_dot(z[...], dm).astype(BF)
    for zx in range(16):
        a, b = plane_place(core[0], zx)
        for half in range(2):
            rows = slice(512 * half + 32 * zx, 512 * half + 32 * zx + 32)
            out[a, b, 32 * half : 32 * half + 32, 0:1024] = d_up[rows]
            out[a, b, 32 * half : 32 * half + 32, 1024:] = d_down[rows]
    small[...] = jnp.zeros((8, WIDTH), F32)
    small[0:1] = jnp.sum(du[...].astype(F32), axis=0, keepdims=True)
    small[1:2] = jnp.sum(g_own[...].astype(F32), axis=0, keepdims=True)


def residual_kernel(two, got, g_own, g_yp, normed, scale, vec, da, dr, small):
    gain = vec[5:6]
    small[...] = jnp.zeros((8, WIDTH), F32)
    for b, ref in enumerate((g_own, g_yp)):
        dn2 = two[block(b)].astype(F32) + got[block(1 - b)].astype(F32)
        grad = ref[...].astype(F32) + norm_back(dn2, gain, normed[block(b)], scale[block(b), 0:1])
        low = grad.astype(BF)
        da[block(b)] = low
        if b == 0:
            dr[...] = grad
            small[0:1] = jnp.sum(low.astype(F32), axis=0, keepdims=True)
            small[1:2] = jnp.sum(dn2 * normed[block(b)], axis=0, keepdims=True)
            small[2:3] = jnp.sum(dn2, axis=0, keepdims=True)


def attend_grad_kernel(
    seq,
    core,
    da_mine,
    da_cp,
    w_own,
    w_yp,
    w_cp,
    w_dg,
    x_own,
    x_yp,
    x_cp,
    x_dg,
    qkv_w,
    qkv,
    lse,
    n1,
    o_own,
    o_yp,
    o_cp,
    o_dg,
    small_b,
    small_c,
    dn1_own,
    dn1_two,
    dn1_theirs,
    send,
    da,
    d_proj,
    rows_out,
    natural,
):
    s = seq[0]
    place = [jnp.bitwise_xor(s, m) for m in RELATIVE]
    da[0:HALF] = da_mine[...]
    da[HALF:] = da_cp[...]
    own_rows = pl.ds(pl.multiple_of(256 * s, 256), 256)
    grad_o = jnp.zeros((ROWS, 256), F32)
    for c, w in enumerate((w_own, w_yp, w_cp, w_dg)):
        cols = pl.ds(pl.multiple_of(256 * place[c], 256), 256)
        grad_o = grad_o + dot_t(da[:, cols], w[own_rows, :])
    do = grad_o.astype(BF)
    keep = key_keep(x_own, x_yp, x_cp, x_dg)
    q, k, v = qkv[:, 0:256], qkv[:, 256:512], qkv[:, 512:768]
    scaled = q * jnp.asarray(0.125, BF)
    keep_rows = jnp.broadcast_to(keep.astype(F32), (128, ROWS)).T[:, 0:1] > 0
    lse_cols = lse[...].T
    dq, dk, dv = (jnp.zeros((ROWS, 256), F32) for _ in range(3))
    for h in range(4):
        scores = jnp.where(keep_rows, dot_t(k, masked(scaled, h)), -1e30)
        probs = jnp.exp(scores - lse_cols[h : h + 1])
        do_h = masked(do, h)
        d_probs = dot_t(v, do_h)
        inner = jnp.sum(probs * d_probs, axis=0, keepdims=True)
        ds = (probs * (d_probs - inner)).astype(BF)
        dq = dq + t_dot(ds, masked(k, h))
        dk = dk + dot(ds, masked(q, h))
        dv = dv + dot(probs.astype(BF), do_h)
    d_proj[:, 0:256] = (dq * 0.125).astype(BF)
    d_proj[:, 256:512] = (dk * 0.125).astype(BF)
    d_proj[:, 512:768] = dv.astype(BF)
    d_gain = jnp.zeros((1, WIDTH), F32)
    d_shift = jnp.zeros((1, WIDTH), F32)
    for b, ref in enumerate((x_own, x_yp, x_cp, x_dg)):
        normed, _ = norm_stats(ref[...].astype(F32))
        part = dot_t(d_proj[block(b)], qkv_w[:, 0:QKV_COLS])
        d_gain = d_gain + jnp.sum(part * normed, axis=0, keepdims=True)
        d_shift = d_shift + jnp.sum(part, axis=0, keepdims=True)
        if b == 0:
            dn1_own[...] = part
        elif b == 1:
            dn1_two[...] = part.astype(BF)
        else:
            dn1_theirs[block(b - 2)] = part.astype(BF)
    natural[:, 0:QKV_COLS] = t_dot(n1[...], d_proj[...]).astype(BF)
    my_cols = pl.ds(pl.multiple_of(256 * s, 256), 256)
    for j, ref in enumerate((o_own, o_yp, o_cp, o_dg)):
        heads = jnp.concatenate([ref[block(b ^ j)] for b in range(4)], axis=0)
        rows = pl.ds(pl.multiple_of(256 * place[j], 256), 256)
        natural[rows, QKV_COLS : QKV_COLS + OUT_COLS] = t_dot(heads, da[:, my_cols]).astype(BF)
    rows_out[...] = jnp.zeros((EXTRA, WIDTH), F32)
    rows_out[0:1] = d_gain
    rows_out[1:2] = d_shift
    for start, first in ((0, 0), (512, 512)):
        sums = jnp.sum(d_proj[:, first : first + 256].astype(F32), axis=0, keepdims=True)
        sums = jnp.broadcast_to(sums, (8, 256)).astype(BF)
        at = pl.ds(pl.multiple_of(start + 128 * s, 128), 128)
        for c in (0, 1):
            rows_out[2 + c : 3 + c, at] = dot_t(sums, bias_hot(c))[0:1]
    rows_out[4:7] = small_c[0:3]
    rows_out[pl.ds(7 + s, 1)] = small_b[0:1]
    rows_out[11:12] = small_b[1:2]
    natural[:, QKV_COLS + OUT_COLS :] = rows_out[...].T.astype(BF)
    for zx in range(16):
        a, b = plane_place(core[0], zx)
        for half in range(2):
            rows = slice(512 * half + 32 * zx, 512 * half + 32 * zx + 32)
            send[a, b, 32 * half : 32 * half + 32] = natural[rows]


def input_grad_kernel(mine, got_cp, got_yp, dr, x_own, vec, out):
    normed, scale = norm_stats(x_own[...].astype(F32))
    dn1 = mine[...] + got_cp[block(0)].astype(F32) + got_yp[...].astype(F32)
    grad = dr[...] + norm_back(dn1, vec[0:1], normed, scale)
    out[:, 0] = grad[0:TOK]


def output_kernel(mine, got_cp, got_yp, r, vec, out):
    y = mine[...] + got_cp[block(0)].astype(F32) + got_yp[...].astype(F32)
    out[0] = (y + r[...] + vec[11:12])[0:TOK].astype(BF)


def sum_of(ref):
    total = ref[0].astype(F32)
    for d in range(1, ref.shape[0]):
        total = total + ref[d].astype(F32)
    return total


def sum_low_kernel(got, out):
    out[...] = sum_of(got).astype(BF)


def sum_line_kernel(places, got, own, to_1, to_2, to_3, total):
    total[...] = sum_of(got)
    own[...] = total[places[1]]
    for by, ref in ((1, to_1), (2, to_2), (3, to_3)):
        ref[...] = total[lax.rem(places[1] + by, 4)].astype(BF)


def sum_join_kernel(got, own, got_1, got_2, got_3, out):
    out[:, 0:REST] = sum_of(got).astype(BF)
    hidden = own[...]
    for ref in (got_1, got_2, got_3):
        hidden = hidden + ref[...].astype(F32)
    out[:, REST:] = hidden.astype(BF)


def sum_rest_kernel(got, down, up, qkv, out, *vectors):
    total = jnp.concatenate(
        [got[s].astype(F32) + got[4 + s].astype(F32) for s in range(4)], axis=0
    )
    down[0] = total[:, REST + 1024 :]
    cols = [
        jnp.concatenate(
            [
                total[8 * s : 8 * s + 8, REST + 128 * t : REST + 128 * t + 128]
                for s in range(4)
            ],
            axis=1,
        )
        for t in range(8)
    ]
    cols = jnp.concatenate(cols, axis=0)
    high = cols.astype(BF)
    low = (cols - high.astype(F32)).astype(BF)
    natural = dot_t(high, hidden_hot()) + dot_t(low, hidden_hot())
    for t in range(8):
        up[0, :, 512 * t : 512 * t + 512] = natural[8 * t : 8 * t + 8]
    for s in range(4):
        rows = slice(8 * s, 8 * s + 8)
        for i in range(3):
            at = 1024 * i + 256 * s
            qkv[0, :, at : at + 256] = total[rows, 256 * i : 256 * i + 256]
        out[0, :, 256 * s : 256 * s + 256] = total[rows, QKV_COLS : QKV_COLS + OUT_COLS]
    extra = sum(total[8 * s : 8 * s + 8, QKV_COLS + OUT_COLS : REST] for s in range(4))
    place = 0
    for ref in vectors:
        size = ref.shape[1]
        value = jnp.zeros((8, size), F32)
        for c in range(size // 8):
            column = jnp.broadcast_to(extra[:, place : place + 1], (8, size))
            hit = iota((8, size), 1) == iota((8, size), 0) + 8 * c
            value = jnp.where(hit, column, value)
            place += 1
        ref[...] = jnp.sum(value, axis=0, keepdims=True)


def body(
    inputs,
    token_mask,
    first_gain,
    first_shift,
    qkv_weight,
    qv_bias,
    out_weight,
    out_bias,
    second_gain,
    second_shift,
    up_weight,
    up_bias,
    down_weight,
    down_bias,
    cotangent,
):
    core = lax.axis_index("core").astype(jnp.int32).reshape(1)
    seq = lax.axis_index("yhi").astype(jnp.int32).reshape(1) * 2 + core
    z_place, x_place = lax.axis_index("z"), lax.axis_index("x")
    places = jnp.where(
        core == 0, jnp.stack([x_place, z_place]), jnp.stack([z_place, x_place])
    ).astype(jnp.int32)

    (send,) = call(
        prepare_kernel,
        [((2, 4, 8, JOINT), BF)],
        *hbm(
            qkv_weight,
            out_weight,
            up_weight,
            down_weight,
            first_gain,
            first_shift,
            qv_bias,
            out_bias,
            second_gain,
            second_shift,
            up_bias,
            down_bias,
        ),
    )
    x, g = call(
        tokens_kernel,
        [((PAD, WIDTH), BF, HBM), ((PAD, WIDTH), BF, HBM)],
        *hbm(inputs, token_mask, cotangent),
        scratch=[pltpu.VMEM((PAD, WIDTH), F32)],
        us=2,
        deps=(send,),
    )
    pieces = lax.all_to_all(
        send.reshape(64, JOINT), ("ylo", "yhi", "core"), 0, 0, tiled=True
    )
    x_yp, g_yp = over_y(x), over_y(g)
    x_cp, g_cp = over_core(x), over_core(g)
    (send,) = call(spread_kernel, [((4, 64, JOINT), BF)], pieces, deps=(x_cp, g_cp))
    pieces = exchange(send.reshape(256, JOINT), STAGE_A)
    send, line = call(
        line_kernel,
        [((4, 256, REST), BF, HBM), ((256, 2048), BF, HBM)],
        pieces,
        deps=(x_yp,),
    )
    got = exchange(send.reshape(1024, REST), STAGE_B)
    line = after(line, g_yp).reshape(4, 64, 2048)
    lines = [line] + [shift(line, STAGE_B, by) for by in (1, 2, 3)]
    xs = (x, x_yp, x_cp, over_core(x_yp))
    gs = (g, g_yp, g_cp, over_core(g_yp))
    w_qkv, w_own, vec = call(
        unpack_kernel,
        [((1024, QKV_COLS), BF), ((1024, OUT_COLS), BF), ((16, WIDTH), F32)],
        core,
        got.reshape(4, 4, 64, REST),
        scratch=[pltpu.VMEM((1024, EXTRA), F32)],
        scalars=1,
        deps=(g_yp,),
    )
    w_yp = over_y(w_own)
    ws = (w_own, w_yp, over_core(w_own), over_core(w_yp))

    n1, qkv, o, lse = call(
        attend_kernel,
        [
            ((ROWS, WIDTH), BF, HBM),
            ((ROWS, QKV_COLS), BF, HBM),
            ((ROWS, 256), BF, HBM),
            ((ROWS, 128), F32, HBM),
        ],
        seq,
        *xs,
        w_qkv,
        vec,
        scalars=1,
        us=8,
    )
    o_yp = over_y(o)
    os = (o, o_yp, over_core(o), over_core(o_yp))
    n2, z, du, dn2_mine, dn2_theirs, normed_2, scale_2, down_w, r = call(
        hidden_kernel,
        [
            ((ROWS, WIDTH), BF),
            ((ROWS, WIDTH), BF),
            ((ROWS, WIDTH), BF),
            ((HALF, WIDTH), F32),
            ((HALF, WIDTH), BF),
            ((HALF, WIDTH), F32, HBM),
            ((HALF, 128), F32, HBM),
            ((1024, WIDTH), BF),
            ((PAD, WIDTH), F32, HBM),
        ],
        seq,
        places,
        *hbm(o),
        *os[1:],
        *xs,
        ws[0],
        *hbm(ws[1]),
        *ws[2:],
        vec,
        *lines,
        *hbm(g),
        *gs[1:],
        scratch=[
            pltpu.VMEM((ROWS, WIDTH), F32),
            pltpu.VMEM((1024, WIDTH), BF),
            pltpu.VMEM((ROWS, WIDTH), BF),
        ],
        scalars=2,
        us=12,
    )
    two = (dn2_mine + over_core(dn2_theirs).astype(F32)).astype(BF)
    two_yp = over_y(two)
    d_hidden, small_b, y_own, y_two, y_theirs = call(
        hidden_grad_kernel,
        [
            ((4, 4, 64, 2048), BF, HBM),
            ((8, WIDTH), F32),
            ((PAD, WIDTH), F32, HBM),
            ((PAD, WIDTH), BF, HBM),
            ((HALF, WIDTH), BF, HBM),
        ],
        core,
        z,
        du,
        n2,
        down_w,
        *gs,
        scalars=1,
        deps=(two,),
        us=300,
    )
    d_hidden = exchange(d_hidden.reshape(1024, 2048), STAGE_A)
    y_cp = over_core(y_theirs)
    da, dr, small_c = call(
        residual_kernel,
        [((HALF, WIDTH), BF), ((PAD, WIDTH), F32, HBM), ((8, WIDTH), F32)],
        two,
        two_yp,
        g,
        g_yp,
        *hbm(normed_2, scale_2),
        vec,
        deps=(y_theirs,),
        us=150,
    )
    da_cp = over_core(da)
    y_low = (y_two.astype(F32) + y_cp[PAD:].astype(F32)).astype(BF)
    y_yp = over_y(y_low)
    dn1_own, dn1_two, dn1_theirs, send = call(
        attend_grad_kernel,
        [
            ((PAD, WIDTH), F32, HBM),
            ((PAD, WIDTH), BF, HBM),
            ((HALF, WIDTH), BF, HBM),
            ((4, 4, 64, REST), BF, HBM),
        ],
        seq,
        core,
        da,
        da_cp,
        *ws,
        *xs,
        *hbm(w_qkv, qkv, lse, n1),
        *os,
        small_b,
        small_c,
        scratch=[
            pltpu.VMEM((ROWS, WIDTH), BF),
            pltpu.VMEM((ROWS, QKV_COLS), BF),
            pltpu.VMEM((EXTRA, WIDTH), F32),
            pltpu.VMEM((1024, REST), BF),
        ],
        scalars=2,
        us=15,
    )
    got = exchange(after(send.reshape(1024, REST), d_hidden), STAGE_A)
    dn1_cp = over_core(dn1_theirs)
    dn1_low = (dn1_two.astype(F32) + dn1_cp[PAD:].astype(F32)).astype(BF)
    dn1_yp = over_y(dn1_low)
    hidden_own, *parts = call(
        sum_line_kernel,
        [((64, 2048), F32)] + [((64, 2048), BF)] * 3,
        places,
        d_hidden.reshape(4, 4, 64, 2048),
        scratch=[pltpu.VMEM((4, 64, 2048), F32)],
        scalars=1,
    )
    parts = [shift(part, STAGE_B, by) for by, part in zip((1, 2, 3), parts)]
    (send,) = call(
        sum_low_kernel, [((256, REST), BF, HBM)], got.reshape(4, 256, REST), deps=(dn1_low, y_yp, hidden_own)
    )
    got = exchange(send, STAGE_B)
    (send,) = call(
        sum_join_kernel,
        [((64, JOINT), BF)],
        got.reshape(4, 64, REST),
        hidden_own,
        *parts,
        deps=(dn1_yp,),
    )
    got = lax.all_to_all(send, ("ylo", "yhi", "core"), 0, 0, tiled=True)
    (block_output,) = call(
        output_kernel, [((1, TOK, WIDTH), BF)], *hbm(y_own, y_cp, y_yp, r), vec
    )
    (g0,) = call(
        input_grad_kernel,
        [((TOK, 1, WIDTH), F32)],
        *hbm(dn1_own, dn1_cp, dn1_yp, dr, x),
        vec,
    )
    g0 = g0.transpose(1, 0, 2)
    d_down, d_up, d_qkv, d_out, d_fg, d_fs, d_qvb, d_ob, d_sg, d_ss, d_ub, d_db = call(
        sum_rest_kernel,
        [
            ((1, 32, WIDTH), F32),
            ((1, 8, 4096), F32),
            ((1, 8, 3072), F32),
            ((1, 8, WIDTH), F32),
        ]
        + [((1, n), F32) for n in (8, 8, 16, 8, 8, 8, 32, 8)],
        got.reshape(8, 8, JOINT),
        deps=(block_output, g0),
    )
    return (
        block_output,
        g0,
        d_fg,
        d_fs,
        d_qkv,
        d_qvb,
        d_out,
        d_ob,
        d_sg,
        d_ss,
        d_up,
        d_ub,
        d_down,
        d_db,
    )


def solution(mesh):
    fine = Mesh(mesh.devices.reshape(2, 4, 4, 2, 2), ALL)
    tokens = P(DP, SEQ, None)
    vector = P(None, ALL)
    matrix = P(None, ALL, None)
    return jax.shard_map(
        body,
        mesh=fine,
        in_specs=(
            tokens,
            P(DP, SEQ),
            vector,
            vector,
            matrix,
            vector,
            matrix,
            vector,
            vector,
            vector,
            matrix,
            vector,
            matrix,
            vector,
            tokens,
        ),
        out_specs=(
            tokens,
            tokens,
            vector,
            vector,
            matrix,
            vector,
            matrix,
            vector,
            vector,
            vector,
            matrix,
            vector,
            matrix,
            vector,
        ),
        check_vma=False,
    )
```

```python
import functools

import jax
import jax.numpy as jnp
from jax import lax
from jax.experimental import pallas as pl
from jax.experimental.pallas import tpu as pltpu
from jax.sharding import Mesh, PartitionSpec as P

TOK = 145
PAD = 160
ROWS = 4 * PAD
HALF = 2 * PAD
SCALE = 1e9
HBM = pltpu.HBM
WIDTH = 1024
BF = jnp.bfloat16
F32 = jnp.float32
DP = ("ylo", "z", "x")
SEQ = ("yhi", "core")
ALL = DP + SEQ
SWAP = [(0, 1), (1, 0)]
RELATIVE = (0, 2, 1, 3)
QKV_COLS = 768
OUT_COLS = 256
EXTRA = 128
REST = QKV_COLS + OUT_COLS + EXTRA
JOINT = REST + 2048


LINES_X = [[[(r * 4 + z) * 4 + x for x in range(4)] for z in range(4)] for r in range(2)]
LINES_Z = [[[(r * 4 + z) * 4 + x for z in range(4)] for x in range(4)] for r in range(2)]


def lines(along):
    return [
        [place * 4 + 2 * yhi + core for place in line]
        for core in range(2)
        for yhi in range(2)
        for half in along[core]
        for line in half
    ]


STAGE_A = lines((LINES_X, LINES_Z))
STAGE_B = lines((LINES_Z, LINES_X))


def exchange(v, groups):
    return lax.all_to_all(v, ALL, 0, 0, axis_index_groups=groups, tiled=True)


def shift(v, groups, by):
    pairs = [(line[i], line[(i + by) % 4]) for line in groups for i in range(4)]
    return lax.ppermute(v, ALL, pairs)


def over_y(v):
    return lax.ppermute(v, "yhi", SWAP)


def over_core(v):
    return lax.ppermute(v, "core", SWAP)


def dot(a, b):
    return jnp.dot(a, b, preferred_element_type=F32)


def dot_t(a, b):
    return lax.dot_general(a, b, (((1,), (1,)), ((), ())), preferred_element_type=F32)


def t_dot(a, b):
    return lax.dot_general(a, b, (((0,), (0,)), ((), ())), preferred_element_type=F32)


def iota(shape, dim):
    return lax.broadcasted_iota(jnp.int32, shape, dim)


def call(kernel, outs, *args, scratch=(), scalars=0, deps=(), us=0.0, room=32):
    vmem = pl.BlockSpec(memory_space=pltpu.VMEM)
    specs = [pl.BlockSpec(memory_space=pltpu.SMEM)] * scalars + [vmem] * (len(args) - scalars)
    specs += [pl.BlockSpec(memory_space=pl.ANY)] * len(deps)

    def run(*refs):
        kernel(*refs[: len(args)], *refs[len(args) + len(deps) :])

    return pl.pallas_call(
        run,
        out_shape=[(o[2] if len(o) > 2 else jax.ShapeDtypeStruct)(o[0], o[1]) for o in outs],
        in_specs=specs,
        out_specs=[vmem] * len(outs),
        scratch_shapes=list(scratch),
        compiler_params=pltpu.CompilerParams(vmem_limit_bytes=room * 2**20),
        cost_estimate=pl.CostEstimate(
            flops=int(us * SCALE), bytes_accessed=0, transcendentals=0
        ),
        name=getattr(kernel, "func", kernel).__name__.removesuffix("_kernel"),
    )(*args, *deps)


def hbm(*values):
    return tuple(pltpu.with_memory_space_constraint(v, HBM) for v in values)


def after(v, *deps):
    anywhere = pl.BlockSpec(memory_space=pl.ANY)
    return pl.pallas_call(
        lambda *refs: None,
        out_shape=jax.ShapeDtypeStruct(v.shape, v.dtype),
        in_specs=[anywhere] * (1 + len(deps)),
        out_specs=anywhere,
        input_output_aliases={0: 0},
        cost_estimate=pl.CostEstimate(flops=0, bytes_accessed=0, transcendentals=0),
        name="after",
    )(v, *deps)


def block(b):
    return slice(b * PAD, (b + 1) * PAD)


def norm_stats(v):
    average = jnp.mean(v, axis=-1, keepdims=True)
    centred = v - average
    variance = jnp.mean(centred * centred, axis=-1, keepdims=True)
    scale = lax.rsqrt(variance + 1e-06)
    return centred * scale, scale


def norm_back(grad, gain, normed, scale):
    e = grad * gain
    return scale * (
        e
        - jnp.mean(e, axis=-1, keepdims=True)
        - normed * jnp.mean(e * normed, axis=-1, keepdims=True)
    )


def piece_columns(refs):
    out = jnp.zeros((8, EXTRA), F32)
    lane = iota((8, EXTRA), 1)
    place = 0
    for ref in refs:
        size = ref.shape[1]
        for c in range(size // 8):
            spread = jnp.broadcast_to(ref[...].astype(F32), (8, size))
            hit = iota((8, size), 1) == iota((8, size), 0) + 8 * c
            column = jnp.sum(jnp.where(hit, spread, 0.0), axis=1, keepdims=True)
            out = jnp.where(lane == place, column, out)
            place += 1
    return out


def hidden_hot():
    row, col = iota((512, 512), 0), iota((512, 512), 1)
    hit = row == 32 * (col % 128 // 8) + 8 * (col // 128) + col % 8
    return jnp.where(hit, 1.0, 0.0).astype(BF)


def tokens_kernel(x, mask, g, out, g_out, tok):
    row = jnp.zeros((8, WIDTH), F32)
    tok[0:8] = row
    tok[0:1, 0:TOK] = mask[...].astype(F32)
    row = tok[0:8]
    lifted = [pltpu.roll(row, PAD * b, 1)[0:1] if b else row[0:1] for b in range(4)]
    tok[0:TOK] = x[0].astype(F32)
    for b in range(4):
        tok[TOK + b : TOK + b + 1] = lifted[b]
    tok[TOK + 4 :] = jnp.zeros((PAD - TOK - 4, WIDTH), F32)
    out[...] = tok[...].astype(BF)
    tok[0:TOK] = g[0].astype(F32)
    tok[TOK:] = jnp.zeros((PAD - TOK, WIDTH), F32)
    g_out[...] = tok[...].astype(BF)


def prepare_kernel(qkv, out_w, up, down, fg, fs, qvb, ob, sg, ss, ub, db, send):
    extra = piece_columns([fg, fs, qvb, ob, sg, ss, ub, db])
    rows = jnp.concatenate([up[0, :, 512 * t : 512 * t + 512] for t in range(8)], axis=0)
    up_cols = dot(rows, hidden_hot())
    for s in range(4):
        parts = [qkv[0, :, 1024 * i + 256 * s : 1024 * i + 256 * s + 256] for i in range(3)]
        parts = [p.astype(F32) for p in parts]
        parts.append(out_w[0, :, 256 * s : 256 * s + 256].astype(F32))
        parts.append(extra)
        parts += [up_cols[8 * t : 8 * t + 8, 128 * s : 128 * s + 128] for t in range(8)]
        parts.append(down[0, 8 * s : 8 * s + 8].astype(F32))
        piece = jnp.concatenate(parts, axis=1).astype(BF)
        for b in range(2):
            send[b, s] = piece


def spread_kernel(pieces, out):
    for d in range(4):
        out[d] = pieces[...]


def line_kernel(got, attend, hidden):
    for d in range(4):
        attend[d] = got[:, 0:REST]
    hidden[...] = got[:, REST:]


def unpack_kernel(core, got, w_qkv, w_out, vec, extra):
    for zx in range(16):
        a, b = plane_place(core[0], zx)
        for half in range(2):
            rows = slice(512 * half + 32 * zx, 512 * half + 32 * zx + 32)
            part = got[b, a, 32 * half : 32 * half + 32]
            w_qkv[rows] = part[:, 0:QKV_COLS]
            w_out[rows] = part[:, QKV_COLS : QKV_COLS + OUT_COLS]
            extra[rows] = part[:, QKV_COLS + OUT_COLS :].astype(F32)
    vec[...] = extra[...].T[0:16]


def bias_hot(c):
    row, col = iota((128, 256), 0), iota((128, 256), 1)
    hit = (col // 16 == row // 8) & (col % 16 == 8 * c + row % 8)
    return jnp.where(hit, 1.0, 0.0).astype(BF)


def plane_place(core, zx):
    z, x = zx // 4, zx % 4
    return jnp.where(core == 0, x, z), jnp.where(core == 0, z, x)


def head_mask(h):
    return iota((1, 256), 1) // 64 == h


def masked(v, h):
    return jnp.where(head_mask(h), v, jnp.zeros_like(v))


def key_keep(x_own, x_yp, x_cp, x_dg):
    refs = (x_own, x_yp, x_cp, x_dg)
    return sum(r[TOK + b : TOK + b + 1, 0:ROWS].astype(F32) for b, r in enumerate(refs)) > 0


def attend_kernel(seq, x_own, x_yp, x_cp, x_dg, w, vec, n1, qkv, o, lse):
    s = seq[0]
    gain, shift = vec[0:1], vec[1:2]
    for b, ref in enumerate((x_own, x_yp, x_cp, x_dg)):
        normed, _ = norm_stats(ref[...].astype(F32))
        n1[block(b)] = (normed * gain + shift).astype(BF)
    biases = []
    for start in (0, 512):
        at = pl.ds(pl.multiple_of(start + 128 * s, 128), 128)
        pieces = [jnp.broadcast_to(vec[2 + c : 3 + c, at], (8, 128)).astype(BF) for c in (0, 1)]
        biases.append((dot(pieces[0], bias_hot(0)) + dot(pieces[1], bias_hot(1)))[0:1])
    for i, bias in enumerate((biases[0], None, biases[1])):
        at = slice(256 * i, 256 * i + 256)
        proj = dot(n1[...], w[:, at])
        qkv[:, at] = (proj if bias is None else proj + bias).astype(BF)
    keep = key_keep(x_own, x_yp, x_cp, x_dg)
    q = qkv[:, 0:256] * jnp.asarray(0.125, BF)
    k, v = qkv[:, 256:512], qkv[:, 512:768]
    total = jnp.zeros((ROWS, 256), F32)
    logs = jnp.zeros((ROWS, 128), F32)
    for h in range(4):
        scores = jnp.where(keep, dot_t(masked(q, h), k), -1e30)
        peak = jnp.max(scores, axis=1, keepdims=True)
        powers = jnp.exp(scores - peak)
        weight = jnp.sum(powers, axis=1, keepdims=True)
        probs = (powers * (1.0 / weight)).astype(BF)
        total = total + dot(probs, masked(v, h))
        logs = jnp.where(iota((ROWS, 128), 1) == h, peak + jnp.log(weight), logs)
    o[...] = total.astype(BF)
    lse[...] = logs


def hidden_kernel(
    seq,
    places,
    o_own,
    o_yp,
    o_cp,
    o_dg,
    x_own,
    x_yp,
    x_cp,
    x_dg,
    w_own,
    w_yp,
    w_cp,
    w_dg,
    vec,
    line_own,
    line_1,
    line_2,
    line_3,
    g_own,
    g_yp,
    g_cp,
    g_dg,
    n2,
    z,
    du,
    dn2_mine,
    dn2_theirs,
    normed_out,
    scale_out,
    down,
    r_own,
    r,
    up,
    dm,
    heads,
):
    s = seq[0]
    place = [jnp.bitwise_xor(s, m) for m in RELATIVE]
    for b, ref in enumerate((g_own, g_yp, g_cp, g_dg)):
        dm[block(b)] = ref[...]
    for j, ref in enumerate((o_own, o_yp, o_cp, o_dg)):
        cols = pl.ds(pl.multiple_of(256 * place[j], 256), 256)
        for b in range(4):
            heads[block(b), cols] = ref[block(b ^ j)]
    for c, w in enumerate((w_own, w_yp, w_cp, w_dg)):
        r[:, pl.ds(pl.multiple_of(256 * place[c], 256), 256)] = dot(heads[...], w[...])
    gain, shift, b_out = vec[5:6], vec[6:7], vec[4:5]
    for b, ref in enumerate((x_own, x_yp, x_cp, x_dg)):
        rows = r[block(b)] + ref[...].astype(F32) + b_out
        if b == 0:
            r_own[...] = rows
        normed, scale = norm_stats(rows)
        n2[block(b)] = (normed * gain + shift).astype(BF)
        if b < 2:
            normed_out[block(b)] = normed
            scale_out[block(b)] = jnp.broadcast_to(scale, (PAD, 128))
    bias = vec[pl.ds(7 + s, 1)]
    for by, ref in enumerate((line_own, line_1, line_2, line_3)):
        b = lax.rem(places[1] + 4 - by, 4)
        for a in range(4):
            zx = jnp.where(s % 2 == 0, 4 * b + a, 4 * a + b)
            for half in range(2):
                rows = pl.ds(pl.multiple_of(512 * half + 32 * zx, 32), 32)
                up[rows] = ref[a, 32 * half : 32 * half + 32, 0:1024]
                down[rows] = ref[a, 32 * half : 32 * half + 32, 1024:]
    for c in range(4):
        at = slice(256 * c, 256 * c + 256)
        u = dot(n2[...], up[:, at]) + bias[:, at]
        cdf = 0.5 * (1.0 + lax.erf(u * (0.5**0.5)))
        z[:, at] = (u * cdf).astype(BF)
        slope = cdf + u * jnp.exp(-0.5 * u * u) * 0.3989422804014327
        du[:, at] = (slope * dot_t(dm[...], down[at, :])).astype(BF)
    dn2_mine[...] = dot_t(du[0:HALF], up[...])
    dn2_theirs[...] = dot_t(du[HALF:], up[...]).astype(BF)


def hidden_grad_kernel(
    core, z, du, n2, down, g_own, g_yp, g_cp, g_dg, out, small, y_own, y_two, y_theirs
):
    y_own[...] = dot(z[block(0)], down[...])
    y_two[...] = dot(z[block(1)], down[...]).astype(BF)
    y_theirs[...] = dot(z[HALF:], down[...]).astype(BF)
    dm = jnp.concatenate([g[...] for g in (g_own, g_yp, g_cp, g_dg)], axis=0)
    d_up = t_dot(n2[...], du[...]).astype(BF)
    d_down = t_dot(z[...], dm).astype(BF)
    for zx in range(16):
        a, b = plane_place(core[0], zx)
        for half in range(2):
            rows = slice(512 * half + 32 * zx, 512 * half + 32 * zx + 32)
            out[a, b, 32 * half : 32 * half + 32, 0:1024] = d_up[rows]
            out[a, b, 32 * half : 32 * half + 32, 1024:] = d_down[rows]
    small[...] = jnp.zeros((8, WIDTH), F32)
    small[0:1] = jnp.sum(du[...].astype(F32), axis=0, keepdims=True)
    small[1:2] = jnp.sum(g_own[...].astype(F32), axis=0, keepdims=True)


def residual_kernel(two, got, g_own, g_yp, normed, scale, vec, da, dr, small):
    gain = vec[5:6]
    small[...] = jnp.zeros((8, WIDTH), F32)
    for b, ref in enumerate((g_own, g_yp)):
        dn2 = two[block(b)].astype(F32) + got[block(1 - b)].astype(F32)
        grad = ref[...].astype(F32) + norm_back(dn2, gain, normed[block(b)], scale[block(b), 0:1])
        low = grad.astype(BF)
        da[block(b)] = low
        if b == 0:
            dr[...] = grad
            small[0:1] = jnp.sum(low.astype(F32), axis=0, keepdims=True)
            small[1:2] = jnp.sum(dn2 * normed[block(b)], axis=0, keepdims=True)
            small[2:3] = jnp.sum(dn2, axis=0, keepdims=True)


def attend_grad_kernel(
    seq,
    core,
    da_mine,
    da_cp,
    w_own,
    w_yp,
    w_cp,
    w_dg,
    x_own,
    x_yp,
    x_cp,
    x_dg,
    qkv_w,
    qkv,
    lse,
    n1,
    o_own,
    o_yp,
    o_cp,
    o_dg,
    small_b,
    small_c,
    dn1_own,
    dn1_two,
    dn1_theirs,
    send,
    da,
    d_proj,
    rows_out,
    natural,
    w_rows,
):
    s = seq[0]
    place = [jnp.bitwise_xor(s, m) for m in RELATIVE]
    da[0:HALF] = da_mine[...]
    da[HALF:] = da_cp[...]
    own_rows = pl.ds(pl.multiple_of(256 * s, 256), 256)
    for c, w in enumerate((w_own, w_yp, w_cp, w_dg)):
        cols = pl.ds(pl.multiple_of(256 * place[c], 256), 256)
        w_rows[:, cols] = w[own_rows, :]
    grad_o = dot_t(da[...], w_rows[...])
    do = grad_o.astype(BF)
    keep = key_keep(x_own, x_yp, x_cp, x_dg)
    q, k, v = qkv[:, 0:256], qkv[:, 256:512], qkv[:, 512:768]
    scaled = q * jnp.asarray(0.125, BF)
    keep_rows = jnp.broadcast_to(keep.astype(F32), (128, ROWS)).T[:, 0:1] > 0
    lse_cols = lse[...].T
    dq, dk, dv = (jnp.zeros((ROWS, 256), F32) for _ in range(3))
    for h in range(4):
        scores = jnp.where(keep_rows, dot_t(k, masked(scaled, h)), -1e30)
        probs = jnp.exp(scores - lse_cols[h : h + 1])
        do_h = masked(do, h)
        d_probs = dot_t(v, do_h)
        inner = jnp.sum(probs * d_probs, axis=0, keepdims=True)
        ds = (probs * (d_probs - inner)).astype(BF)
        dq = dq + t_dot(ds, masked(k, h))
        dk = dk + dot(ds, masked(q, h))
        dv = dv + dot(probs.astype(BF), do_h)
    d_proj[:, 0:256] = (dq * 0.125).astype(BF)
    d_proj[:, 256:512] = (dk * 0.125).astype(BF)
    d_proj[:, 512:768] = dv.astype(BF)
    d_gain = jnp.zeros((1, WIDTH), F32)
    d_shift = jnp.zeros((1, WIDTH), F32)
    for b, ref in enumerate((x_own, x_yp, x_cp, x_dg)):
        normed, _ = norm_stats(ref[...].astype(F32))
        part = dot_t(d_proj[block(b)], qkv_w[:, 0:QKV_COLS])
        d_gain = d_gain + jnp.sum(part * normed, axis=0, keepdims=True)
        d_shift = d_shift + jnp.sum(part, axis=0, keepdims=True)
        if b == 0:
            dn1_own[...] = part
        elif b == 1:
            dn1_two[...] = part.astype(BF)
        else:
            dn1_theirs[block(b - 2)] = part.astype(BF)
    natural[:, 0:QKV_COLS] = t_dot(n1[...], d_proj[...]).astype(BF)
    my_cols = pl.ds(pl.multiple_of(256 * s, 256), 256)
    for j, ref in enumerate((o_own, o_yp, o_cp, o_dg)):
        heads = jnp.concatenate([ref[block(b ^ j)] for b in range(4)], axis=0)
        rows = pl.ds(pl.multiple_of(256 * place[j], 256), 256)
        natural[rows, QKV_COLS : QKV_COLS + OUT_COLS] = t_dot(heads, da[:, my_cols]).astype(BF)
    rows_out[...] = jnp.zeros((EXTRA, WIDTH), F32)
    rows_out[0:1] = d_gain
    rows_out[1:2] = d_shift
    for start, first in ((0, 0), (512, 512)):
        sums = jnp.sum(d_proj[:, first : first + 256].astype(F32), axis=0, keepdims=True)
        sums = jnp.broadcast_to(sums, (8, 256)).astype(BF)
        at = pl.ds(pl.multiple_of(start + 128 * s, 128), 128)
        for c in (0, 1):
            rows_out[2 + c : 3 + c, at] = dot_t(sums, bias_hot(c))[0:1]
    rows_out[4:7] = small_c[0:3]
    rows_out[pl.ds(7 + s, 1)] = small_b[0:1]
    rows_out[11:12] = small_b[1:2]
    natural[:, QKV_COLS + OUT_COLS :] = rows_out[...].T.astype(BF)
    for zx in range(16):
        a, b = plane_place(core[0], zx)
        for half in range(2):
            rows = slice(512 * half + 32 * zx, 512 * half + 32 * zx + 32)
            send[a, b, 32 * half : 32 * half + 32] = natural[rows]


def input_grad_kernel(mine, got_cp, got_yp, dr, x_own, vec, out):
    normed, scale = norm_stats(x_own[...].astype(F32))
    dn1 = mine[...] + got_cp[block(0)].astype(F32) + got_yp[...].astype(F32)
    grad = dr[...] + norm_back(dn1, vec[0:1], normed, scale)
    out[:, 0] = grad[0:TOK]


def output_kernel(mine, got_cp, got_yp, r, vec, out):
    y = mine[...] + got_cp[block(0)].astype(F32) + got_yp[...].astype(F32)
    out[0] = (y + r[...] + vec[11:12])[0:TOK].astype(BF)


def sum_of(ref):
    total = ref[0].astype(F32)
    for d in range(1, ref.shape[0]):
        total = total + ref[d].astype(F32)
    return total


def sum_low_kernel(got, out):
    out[...] = sum_of(got).astype(BF)


def sum_line_kernel(places, got, own, to_1, to_2, to_3, total):
    total[...] = sum_of(got)
    own[...] = total[places[1]]
    for by, ref in ((1, to_1), (2, to_2), (3, to_3)):
        ref[...] = total[lax.rem(places[1] + by, 4)].astype(BF)


def sum_join_kernel(got, own, got_1, got_2, got_3, out):
    out[:, 0:REST] = sum_of(got).astype(BF)
    hidden = own[...]
    for ref in (got_1, got_2, got_3):
        hidden = hidden + ref[...].astype(F32)
    out[:, REST:] = hidden.astype(BF)


def sum_rest_kernel(got, down, up, qkv, out, *vectors):
    total = jnp.concatenate(
        [got[s].astype(F32) + got[4 + s].astype(F32) for s in range(4)], axis=0
    )
    down[0] = total[:, REST + 1024 :]
    cols = [
        jnp.concatenate(
            [
                total[8 * s : 8 * s + 8, REST + 128 * t : REST + 128 * t + 128]
                for s in range(4)
            ],
            axis=1,
        )
        for t in range(8)
    ]
    cols = jnp.concatenate(cols, axis=0)
    high = cols.astype(BF)
    low = (cols - high.astype(F32)).astype(BF)
    natural = dot_t(high, hidden_hot()) + dot_t(low, hidden_hot())
    for t in range(8):
        up[0, :, 512 * t : 512 * t + 512] = natural[8 * t : 8 * t + 8]
    for s in range(4):
        rows = slice(8 * s, 8 * s + 8)
        for i in range(3):
            at = 1024 * i + 256 * s
            qkv[0, :, at : at + 256] = total[rows, 256 * i : 256 * i + 256]
        out[0, :, 256 * s : 256 * s + 256] = total[rows, QKV_COLS : QKV_COLS + OUT_COLS]
    extra = sum(total[8 * s : 8 * s + 8, QKV_COLS + OUT_COLS : REST] for s in range(4))
    place = 0
    for ref in vectors:
        size = ref.shape[1]
        value = jnp.zeros((8, size), F32)
        for c in range(size // 8):
            column = jnp.broadcast_to(extra[:, place : place + 1], (8, size))
            hit = iota((8, size), 1) == iota((8, size), 0) + 8 * c
            value = jnp.where(hit, column, value)
            place += 1
        ref[...] = jnp.sum(value, axis=0, keepdims=True)


def body(
    inputs,
    token_mask,
    first_gain,
    first_shift,
    qkv_weight,
    qv_bias,
    out_weight,
    out_bias,
    second_gain,
    second_shift,
    up_weight,
    up_bias,
    down_weight,
    down_bias,
    cotangent,
):
    core = lax.axis_index("core").astype(jnp.int32).reshape(1)
    seq = lax.axis_index("yhi").astype(jnp.int32).reshape(1) * 2 + core
    z_place, x_place = lax.axis_index("z"), lax.axis_index("x")
    places = jnp.where(
        core == 0, jnp.stack([x_place, z_place]), jnp.stack([z_place, x_place])
    ).astype(jnp.int32)

    (send,) = call(
        prepare_kernel,
        [((2, 4, 8, JOINT), BF)],
        *hbm(
            qkv_weight,
            out_weight,
            up_weight,
            down_weight,
            first_gain,
            first_shift,
            qv_bias,
            out_bias,
            second_gain,
            second_shift,
            up_bias,
            down_bias,
        ),
    )
    x, g = call(
        tokens_kernel,
        [((PAD, WIDTH), BF, HBM), ((PAD, WIDTH), BF, HBM)],
        *hbm(inputs, token_mask, cotangent),
        scratch=[pltpu.VMEM((PAD, WIDTH), F32)],
        us=2,
        deps=(send,),
    )
    pieces = lax.all_to_all(
        send.reshape(64, JOINT), ("ylo", "yhi", "core"), 0, 0, tiled=True
    )
    x_yp, g_yp = over_y(x), over_y(g)
    x_cp, g_cp = over_core(x), over_core(g)
    (send,) = call(spread_kernel, [((4, 64, JOINT), BF)], pieces, deps=(x_cp, g_cp))
    pieces = exchange(send.reshape(256, JOINT), STAGE_A)
    send, line = call(
        line_kernel,
        [((4, 256, REST), BF, HBM), ((256, 2048), BF, HBM)],
        pieces,
        deps=(x_yp,),
    )
    got = exchange(send.reshape(1024, REST), STAGE_B)
    line = after(line, g_yp).reshape(4, 64, 2048)
    lines = [line] + [shift(line, STAGE_B, by) for by in (1, 2, 3)]
    xs = (x, x_yp, x_cp, over_core(x_yp))
    gs = (g, g_yp, g_cp, over_core(g_yp))
    w_qkv, w_own, vec = call(
        unpack_kernel,
        [((1024, QKV_COLS), BF), ((1024, OUT_COLS), BF), ((16, WIDTH), F32)],
        core,
        got.reshape(4, 4, 64, REST),
        scratch=[pltpu.VMEM((1024, EXTRA), F32)],
        scalars=1,
        deps=(g_yp,),
    )
    w_yp = over_y(w_own)
    ws = (w_own, w_yp, over_core(w_own), over_core(w_yp))

    n1, qkv, o, lse = call(
        attend_kernel,
        [
            ((ROWS, WIDTH), BF, HBM),
            ((ROWS, QKV_COLS), BF, HBM),
            ((ROWS, 256), BF, HBM),
            ((ROWS, 128), F32, HBM),
        ],
        seq,
        *xs,
        w_qkv,
        vec,
        scalars=1,
        us=8,
    )
    o_yp = over_y(o)
    os = (o, o_yp, over_core(o), over_core(o_yp))
    n2, z, du, dn2_mine, dn2_theirs, normed_2, scale_2, down_w, r = call(
        hidden_kernel,
        [
            ((ROWS, WIDTH), BF),
            ((ROWS, WIDTH), BF),
            ((ROWS, WIDTH), BF),
            ((HALF, WIDTH), F32),
            ((HALF, WIDTH), BF),
            ((HALF, WIDTH), F32, HBM),
            ((HALF, 128), F32, HBM),
            ((1024, WIDTH), BF),
            ((PAD, WIDTH), F32, HBM),
        ],
        seq,
        places,
        *hbm(o),
        *os[1:],
        *xs,
        ws[0],
        *hbm(ws[1]),
        *ws[2:],
        vec,
        *lines,
        *hbm(g),
        *gs[1:],
        scratch=[
            pltpu.VMEM((ROWS, WIDTH), F32),
            pltpu.VMEM((1024, WIDTH), BF),
            pltpu.VMEM((ROWS, WIDTH), BF),
            pltpu.VMEM((ROWS, WIDTH), BF),
        ],
        scalars=2,
        us=12,
    )
    two = (dn2_mine + over_core(dn2_theirs).astype(F32)).astype(BF)
    two_yp = over_y(two)
    d_hidden, small_b, y_own, y_two, y_theirs = call(
        hidden_grad_kernel,
        [
            ((4, 4, 64, 2048), BF, HBM),
            ((8, WIDTH), F32),
            ((PAD, WIDTH), F32, HBM),
            ((PAD, WIDTH), BF, HBM),
            ((HALF, WIDTH), BF, HBM),
        ],
        core,
        z,
        du,
        n2,
        down_w,
        *gs,
        scalars=1,
        deps=(two,),
        us=300,
    )
    d_hidden = exchange(d_hidden.reshape(1024, 2048), STAGE_A)
    y_cp = over_core(y_theirs)
    da, dr, small_c = call(
        residual_kernel,
        [((HALF, WIDTH), BF), ((PAD, WIDTH), F32, HBM), ((8, WIDTH), F32)],
        two,
        two_yp,
        g,
        g_yp,
        *hbm(normed_2, scale_2),
        vec,
        deps=(y_theirs,),
        us=150,
    )
    da_cp = over_core(da)
    y_low = (y_two.astype(F32) + y_cp[PAD:].astype(F32)).astype(BF)
    y_yp = over_y(y_low)
    dn1_own, dn1_two, dn1_theirs, send = call(
        attend_grad_kernel,
        [
            ((PAD, WIDTH), F32, HBM),
            ((PAD, WIDTH), BF, HBM),
            ((HALF, WIDTH), BF, HBM),
            ((4, 4, 64, REST), BF, HBM),
        ],
        seq,
        core,
        da,
        da_cp,
        *ws,
        *xs,
        *hbm(w_qkv, qkv, lse, n1),
        *os,
        small_b,
        small_c,
        scratch=[
            pltpu.VMEM((ROWS, WIDTH), BF),
            pltpu.VMEM((ROWS, QKV_COLS), BF),
            pltpu.VMEM((EXTRA, WIDTH), F32),
            pltpu.VMEM((1024, REST), BF),
            pltpu.VMEM((256, WIDTH), BF),
        ],
        scalars=2,
        us=15,
    )
    got = exchange(after(send.reshape(1024, REST), d_hidden), STAGE_A)
    dn1_cp = over_core(dn1_theirs)
    dn1_low = (dn1_two.astype(F32) + dn1_cp[PAD:].astype(F32)).astype(BF)
    dn1_yp = over_y(dn1_low)
    hidden_own, *parts = call(
        sum_line_kernel,
        [((64, 2048), F32)] + [((64, 2048), BF)] * 3,
        places,
        d_hidden.reshape(4, 4, 64, 2048),
        scratch=[pltpu.VMEM((4, 64, 2048), F32)],
        scalars=1,
    )
    parts = [shift(part, STAGE_B, by) for by, part in zip((1, 2, 3), parts)]
    (send,) = call(
        sum_low_kernel, [((256, REST), BF, HBM)], got.reshape(4, 256, REST), deps=(dn1_low, y_yp, hidden_own)
    )
    got = exchange(send, STAGE_B)
    (send,) = call(
        sum_join_kernel,
        [((64, JOINT), BF)],
        got.reshape(4, 64, REST),
        hidden_own,
        *parts,
        deps=(dn1_yp,),
    )
    got = lax.all_to_all(send, ("ylo", "yhi", "core"), 0, 0, tiled=True)
    (block_output,) = call(
        output_kernel, [((1, TOK, WIDTH), BF)], *hbm(y_own, y_cp, y_yp, r), vec
    )
    (g0,) = call(
        input_grad_kernel,
        [((TOK, 1, WIDTH), F32)],
        *hbm(dn1_own, dn1_cp, dn1_yp, dr, x),
        vec,
    )
    g0 = g0.transpose(1, 0, 2)
    d_down, d_up, d_qkv, d_out, d_fg, d_fs, d_qvb, d_ob, d_sg, d_ss, d_ub, d_db = call(
        sum_rest_kernel,
        [
            ((1, 32, WIDTH), F32),
            ((1, 8, 4096), F32),
            ((1, 8, 3072), F32),
            ((1, 8, WIDTH), F32),
        ]
        + [((1, n), F32) for n in (8, 8, 16, 8, 8, 8, 32, 8)],
        got.reshape(8, 8, JOINT),
        deps=(block_output, g0),
    )
    return (
        block_output,
        g0,
        d_fg,
        d_fs,
        d_qkv,
        d_qvb,
        d_out,
        d_ob,
        d_sg,
        d_ss,
        d_up,
        d_ub,
        d_down,
        d_db,
    )


def solution(mesh):
    fine = Mesh(mesh.devices.reshape(2, 4, 4, 2, 2), ALL)
    tokens = P(DP, SEQ, None)
    vector = P(None, ALL)
    matrix = P(None, ALL, None)
    return jax.shard_map(
        body,
        mesh=fine,
        in_specs=(
            tokens,
            P(DP, SEQ),
            vector,
            vector,
            matrix,
            vector,
            matrix,
            vector,
            vector,
            vector,
            matrix,
            vector,
            matrix,
            vector,
            tokens,
        ),
        out_specs=(
            tokens,
            tokens,
            vector,
            vector,
            matrix,
            vector,
            matrix,
            vector,
            vector,
            vector,
            matrix,
            vector,
            matrix,
            vector,
        ),
        check_vma=False,
    )
```

```python
import functools

import jax
import jax.numpy as jnp
from jax import lax
from jax.experimental import pallas as pl
from jax.experimental.pallas import tpu as pltpu
from jax.sharding import Mesh, PartitionSpec as P

TOK = 145
PAD = 160
ROWS = 4 * PAD
HALF = 2 * PAD
SCALE = 1e9
HBM = pltpu.HBM
WIDTH = 1024
BF = jnp.bfloat16
F32 = jnp.float32
DP = ("ylo", "z", "x")
SEQ = ("yhi", "core")
ALL = DP + SEQ
SWAP = [(0, 1), (1, 0)]
RELATIVE = (0, 2, 1, 3)
QKV_COLS = 768
OUT_COLS = 256
EXTRA = 128
REST = QKV_COLS + OUT_COLS + EXTRA
JOINT = REST + 2048


LINES_X = [[[(r * 4 + z) * 4 + x for x in range(4)] for z in range(4)] for r in range(2)]
LINES_Z = [[[(r * 4 + z) * 4 + x for z in range(4)] for x in range(4)] for r in range(2)]


def lines(along):
    return [
        [place * 4 + 2 * yhi + core for place in line]
        for core in range(2)
        for yhi in range(2)
        for half in along[core]
        for line in half
    ]


STAGE_A = lines((LINES_X, LINES_Z))
STAGE_B = lines((LINES_Z, LINES_X))


def exchange(v, groups):
    return lax.all_to_all(v, ALL, 0, 0, axis_index_groups=groups, tiled=True)


def shift(v, groups, by):
    pairs = [(line[i], line[(i + by) % 4]) for line in groups for i in range(4)]
    return lax.ppermute(v, ALL, pairs)


def over_y(v):
    return lax.ppermute(v, "yhi", SWAP)


def over_core(v):
    return lax.ppermute(v, "core", SWAP)


def dot(a, b):
    return jnp.dot(a, b, preferred_element_type=F32)


def dot_t(a, b):
    return lax.dot_general(a, b, (((1,), (1,)), ((), ())), preferred_element_type=F32)


def t_dot(a, b):
    return lax.dot_general(a, b, (((0,), (0,)), ((), ())), preferred_element_type=F32)


def iota(shape, dim):
    return lax.broadcasted_iota(jnp.int32, shape, dim)


def call(kernel, outs, *args, scratch=(), scalars=0, deps=(), us=0.0, room=32):
    vmem = pl.BlockSpec(memory_space=pltpu.VMEM)
    specs = [pl.BlockSpec(memory_space=pltpu.SMEM)] * scalars + [vmem] * (len(args) - scalars)
    specs += [pl.BlockSpec(memory_space=pl.ANY)] * len(deps)

    def run(*refs):
        kernel(*refs[: len(args)], *refs[len(args) + len(deps) :])

    return pl.pallas_call(
        run,
        out_shape=[(o[2] if len(o) > 2 else jax.ShapeDtypeStruct)(o[0], o[1]) for o in outs],
        in_specs=specs,
        out_specs=[vmem] * len(outs),
        scratch_shapes=list(scratch),
        compiler_params=pltpu.CompilerParams(vmem_limit_bytes=room * 2**20),
        cost_estimate=pl.CostEstimate(
            flops=int(us * SCALE), bytes_accessed=0, transcendentals=0
        ),
        name=getattr(kernel, "func", kernel).__name__.removesuffix("_kernel"),
    )(*args, *deps)


def hbm(*values):
    return tuple(pltpu.with_memory_space_constraint(v, HBM) for v in values)


def after(v, *deps):
    anywhere = pl.BlockSpec(memory_space=pl.ANY)
    return pl.pallas_call(
        lambda *refs: None,
        out_shape=jax.ShapeDtypeStruct(v.shape, v.dtype),
        in_specs=[anywhere] * (1 + len(deps)),
        out_specs=anywhere,
        input_output_aliases={0: 0},
        cost_estimate=pl.CostEstimate(flops=0, bytes_accessed=0, transcendentals=0),
        name="after",
    )(v, *deps)


def block(b):
    return slice(b * PAD, (b + 1) * PAD)


def norm_stats(v):
    average = jnp.mean(v, axis=-1, keepdims=True)
    centred = v - average
    variance = jnp.mean(centred * centred, axis=-1, keepdims=True)
    scale = lax.rsqrt(variance + 1e-06)
    return centred * scale, scale


def norm_back(grad, gain, normed, scale):
    e = grad * gain
    return scale * (
        e
        - jnp.mean(e, axis=-1, keepdims=True)
        - normed * jnp.mean(e * normed, axis=-1, keepdims=True)
    )


def piece_columns(refs):
    out = jnp.zeros((8, EXTRA), F32)
    lane = iota((8, EXTRA), 1)
    place = 0
    for ref in refs:
        size = ref.shape[1]
        for c in range(size // 8):
            spread = jnp.broadcast_to(ref[...].astype(F32), (8, size))
            hit = iota((8, size), 1) == iota((8, size), 0) + 8 * c
            column = jnp.sum(jnp.where(hit, spread, 0.0), axis=1, keepdims=True)
            out = jnp.where(lane == place, column, out)
            place += 1
    return out


def hidden_hot():
    row, col = iota((512, 512), 0), iota((512, 512), 1)
    hit = row == 32 * (col % 128 // 8) + 8 * (col // 128) + col % 8
    return jnp.where(hit, 1.0, 0.0).astype(BF)


def tokens_kernel(x, mask, g, out, g_out, tok):
    row = jnp.zeros((8, WIDTH), F32)
    tok[0:8] = row
    tok[0:1, 0:TOK] = mask[...].astype(F32)
    row = tok[0:8]
    lifted = [pltpu.roll(row, PAD * b, 1)[0:1] if b else row[0:1] for b in range(4)]
    tok[0:TOK] = x[0].astype(F32)
    for b in range(4):
        tok[TOK + b : TOK + b + 1] = lifted[b]
    tok[TOK + 4 :] = jnp.zeros((PAD - TOK - 4, WIDTH), F32)
    out[...] = tok[...].astype(BF)
    tok[0:TOK] = g[0].astype(F32)
    tok[TOK:] = jnp.zeros((PAD - TOK, WIDTH), F32)
    g_out[...] = tok[...].astype(BF)


def prepare_kernel(qkv, out_w, up, down, fg, fs, qvb, ob, sg, ss, ub, db, send):
    extra = piece_columns([fg, fs, qvb, ob, sg, ss, ub, db])
    rows = jnp.concatenate([up[0, :, 512 * t : 512 * t + 512] for t in range(8)], axis=0)
    up_cols = dot(rows, hidden_hot())
    for s in range(4):
        parts = [qkv[0, :, 1024 * i + 256 * s : 1024 * i + 256 * s + 256] for i in range(3)]
        parts = [p.astype(F32) for p in parts]
        parts.append(out_w[0, :, 256 * s : 256 * s + 256].astype(F32))
        parts.append(extra)
        parts += [up_cols[8 * t : 8 * t + 8, 128 * s : 128 * s + 128] for t in range(8)]
        parts.append(down[0, 8 * s : 8 * s + 8].astype(F32))
        piece = jnp.concatenate(parts, axis=1).astype(BF)
        for b in range(2):
            send[b, s] = piece


def spread_kernel(pieces, out):
    for d in range(4):
        out[d] = pieces[...]


def line_kernel(got, attend, hidden):
    for d in range(4):
        attend[d] = got[:, 0:REST]
    hidden[...] = got[:, REST:]


def unpack_kernel(core, got, w_qkv, w_out, vec, extra):
    for zx in range(16):
        a, b = plane_place(core[0], zx)
        for half in range(2):
            rows = slice(512 * half + 32 * zx, 512 * half + 32 * zx + 32)
            part = got[b, a, 32 * half : 32 * half + 32]
            w_qkv[rows] = part[:, 0:QKV_COLS]
            w_out[rows] = part[:, QKV_COLS : QKV_COLS + OUT_COLS]
            extra[rows] = part[:, QKV_COLS + OUT_COLS :].astype(F32)
    vec[...] = extra[...].T[0:16]


def bias_hot(c):
    row, col = iota((128, 256), 0), iota((128, 256), 1)
    hit = (col // 16 == row // 8) & (col % 16 == 8 * c + row % 8)
    return jnp.where(hit, 1.0, 0.0).astype(BF)


def plane_place(core, zx):
    z, x = zx // 4, zx % 4
    return jnp.where(core == 0, x, z), jnp.where(core == 0, z, x)


def head_mask(h):
    return iota((1, 256), 1) // 64 == h


def masked(v, h):
    return jnp.where(head_mask(h), v, jnp.zeros_like(v))


def key_keep(x_own, x_yp, x_cp, x_dg):
    refs = (x_own, x_yp, x_cp, x_dg)
    return sum(r[TOK + b : TOK + b + 1, 0:ROWS].astype(F32) for b, r in enumerate(refs)) > 0


def attend_kernel(seq, x_own, x_yp, x_cp, x_dg, w, vec, n1, qkv, o, lse):
    s = seq[0]
    gain, shift = vec[0:1], vec[1:2]
    for b, ref in enumerate((x_own, x_yp, x_cp, x_dg)):
        normed, _ = norm_stats(ref[...].astype(F32))
        n1[block(b)] = (normed * gain + shift).astype(BF)
    biases = []
    for start in (0, 512):
        at = pl.ds(pl.multiple_of(start + 128 * s, 128), 128)
        pieces = [jnp.broadcast_to(vec[2 + c : 3 + c, at], (8, 128)).astype(BF) for c in (0, 1)]
        biases.append((dot(pieces[0], bias_hot(0)) + dot(pieces[1], bias_hot(1)))[0:1])
    for i, bias in enumerate((biases[0], None, biases[1])):
        at = slice(256 * i, 256 * i + 256)
        proj = dot(n1[...], w[:, at])
        qkv[:, at] = (proj if bias is None else proj + bias).astype(BF)
    keep = key_keep(x_own, x_yp, x_cp, x_dg)
    q = qkv[:, 0:256] * jnp.asarray(0.125, BF)
    k, v = qkv[:, 256:512], qkv[:, 512:768]
    total = jnp.zeros((ROWS, 256), F32)
    logs = jnp.zeros((ROWS, 128), F32)
    for h in range(4):
        scores = jnp.where(keep, dot_t(masked(q, h), k), -1e30)
        peak = jnp.max(scores, axis=1, keepdims=True)
        powers = jnp.exp(scores - peak)
        weight = jnp.sum(powers, axis=1, keepdims=True)
        total = total + dot(powers.astype(BF), masked(v, h)) * (1.0 / weight)
        logs = jnp.where(iota((ROWS, 128), 1) == h, peak + jnp.log(weight), logs)
    o[...] = total.astype(BF)
    lse[...] = logs


def hidden_kernel(
    seq,
    places,
    o_own,
    o_yp,
    o_cp,
    o_dg,
    x_own,
    x_yp,
    x_cp,
    x_dg,
    w_own,
    w_yp,
    w_cp,
    w_dg,
    vec,
    line_own,
    line_1,
    line_2,
    line_3,
    g_own,
    g_yp,
    g_cp,
    g_dg,
    n2,
    z,
    du,
    dn2_mine,
    dn2_theirs,
    normed_out,
    scale_out,
    down,
    r_own,
    r,
    up,
    dm,
):
    s = seq[0]
    place = [jnp.bitwise_xor(s, m) for m in RELATIVE]
    for b, ref in enumerate((g_own, g_yp, g_cp, g_dg)):
        dm[block(b)] = ref[...]
    heads = []
    for j, ref in enumerate((o_own, o_yp, o_cp, o_dg)):
        heads.append(jnp.concatenate([ref[block(b ^ j)] for b in range(4)], axis=0))
    for c, w in enumerate((w_own, w_yp, w_cp, w_dg)):
        total = jnp.zeros((ROWS, 256), F32)
        for j in range(4):
            rows = pl.ds(pl.multiple_of(256 * place[j], 256), 256)
            total = total + dot(heads[j], w[rows, :])
        r[:, pl.ds(pl.multiple_of(256 * place[c], 256), 256)] = total
    gain, shift, b_out = vec[5:6], vec[6:7], vec[4:5]
    for b, ref in enumerate((x_own, x_yp, x_cp, x_dg)):
        rows = r[block(b)] + ref[...].astype(F32) + b_out
        if b == 0:
            r_own[...] = rows
        normed, scale = norm_stats(rows)
        n2[block(b)] = (normed * gain + shift).astype(BF)
        if b < 2:
            normed_out[block(b)] = normed
            scale_out[block(b)] = jnp.broadcast_to(scale, (PAD, 128))
    bias = vec[pl.ds(7 + s, 1)]
    for by, ref in enumerate((line_own, line_1, line_2, line_3)):
        b = lax.rem(places[1] + 4 - by, 4)
        for a in range(4):
            zx = jnp.where(s % 2 == 0, 4 * b + a, 4 * a + b)
            for half in range(2):
                rows = pl.ds(pl.multiple_of(512 * half + 32 * zx, 32), 32)
                up[rows] = ref[a, 32 * half : 32 * half + 32, 0:1024]
                down[rows] = ref[a, 32 * half : 32 * half + 32, 1024:]
    for c in range(4):
        at = slice(256 * c, 256 * c + 256)
        u = dot(n2[...], up[:, at]) + bias[:, at]
        cdf = 0.5 * (1.0 + lax.erf(u * (0.5**0.5)))
        z[:, at] = (u * cdf).astype(BF)
        slope = cdf + u * jnp.exp(-0.5 * u * u) * 0.3989422804014327
        du[:, at] = (slope * dot_t(dm[...], down[at, :])).astype(BF)
    dn2_mine[...] = dot_t(du[0:HALF], up[...])
    dn2_theirs[...] = dot_t(du[HALF:], up[...]).astype(BF)


def hidden_grad_kernel(
    core, z, du, n2, down, g_own, g_yp, g_cp, g_dg, out, small, y_own, y_two, y_theirs
):
    y_own[...] = dot(z[block(0)], down[...])
    y_two[...] = dot(z[block(1)], down[...]).astype(BF)
    y_theirs[...] = dot(z[HALF:], down[...]).astype(BF)
    dm = jnp.concatenate([g[...] for g in (g_own, g_yp, g_cp, g_dg)], axis=0)
    d_up = t_dot(n2[...], du[...]).astype(BF)
    d_down = t_dot(z[...], dm).astype(BF)
    for zx in range(16):
        a, b = plane_place(core[0], zx)
        for half in range(2):
            rows = slice(512 * half + 32 * zx, 512 * half + 32 * zx + 32)
            out[a, b, 32 * half : 32 * half + 32, 0:1024] = d_up[rows]
            out[a, b, 32 * half : 32 * half + 32, 1024:] = d_down[rows]
    small[...] = jnp.zeros((8, WIDTH), F32)
    small[0:1] = jnp.sum(du[...].astype(F32), axis=0, keepdims=True)
    small[1:2] = jnp.sum(g_own[...].astype(F32), axis=0, keepdims=True)


def residual_kernel(two, got, g_own, g_yp, normed, scale, vec, da, dr, small):
    gain = vec[5:6]
    small[...] = jnp.zeros((8, WIDTH), F32)
    for b, ref in enumerate((g_own, g_yp)):
        dn2 = two[block(b)].astype(F32) + got[block(1 - b)].astype(F32)
        grad = ref[...].astype(F32) + norm_back(dn2, gain, normed[block(b)], scale[block(b), 0:1])
        low = grad.astype(BF)
        da[block(b)] = low
        if b == 0:
            dr[...] = grad
            small[0:1] = jnp.sum(low.astype(F32), axis=0, keepdims=True)
            small[1:2] = jnp.sum(dn2 * normed[block(b)], axis=0, keepdims=True)
            small[2:3] = jnp.sum(dn2, axis=0, keepdims=True)


def attend_grad_kernel(
    seq,
    core,
    da_mine,
    da_cp,
    w_own,
    w_yp,
    w_cp,
    w_dg,
    x_own,
    x_yp,
    x_cp,
    x_dg,
    qkv_w,
    qkv,
    lse,
    n1,
    o_own,
    o_yp,
    o_cp,
    o_dg,
    small_b,
    small_c,
    dn1_own,
    dn1_two,
    dn1_theirs,
    send,
    da,
    d_proj,
    rows_out,
    natural,
):
    s = seq[0]
    place = [jnp.bitwise_xor(s, m) for m in RELATIVE]
    da[0:HALF] = da_mine[...]
    da[HALF:] = da_cp[...]
    own_rows = pl.ds(pl.multiple_of(256 * s, 256), 256)
    grad_o = jnp.zeros((ROWS, 256), F32)
    for c, w in enumerate((w_own, w_yp, w_cp, w_dg)):
        cols = pl.ds(pl.multiple_of(256 * place[c], 256), 256)
        grad_o = grad_o + dot_t(da[:, cols], w[own_rows, :])
    do = grad_o.astype(BF)
    keep = key_keep(x_own, x_yp, x_cp, x_dg)
    q, k, v = qkv[:, 0:256], qkv[:, 256:512], qkv[:, 512:768]
    scaled = q * jnp.asarray(0.125, BF)
    keep_rows = jnp.broadcast_to(keep.astype(F32), (128, ROWS)).T[:, 0:1] > 0
    lse_cols = lse[...].T
    dq, dk, dv = (jnp.zeros((ROWS, 256), F32) for _ in range(3))
    for h in range(4):
        scores = jnp.where(keep_rows, dot_t(k, masked(scaled, h)), -1e30)
        probs = jnp.exp(scores - lse_cols[h : h + 1])
        do_h = masked(do, h)
        d_probs = dot_t(v, do_h)
        inner = jnp.sum(probs * d_probs, axis=0, keepdims=True)
        ds = (probs * (d_probs - inner)).astype(BF)
        dq = dq + t_dot(ds, masked(k, h))
        dk = dk + dot(ds, masked(q, h))
        dv = dv + dot(probs.astype(BF), do_h)
    d_proj[:, 0:256] = (dq * 0.125).astype(BF)
    d_proj[:, 256:512] = (dk * 0.125).astype(BF)
    d_proj[:, 512:768] = dv.astype(BF)
    d_gain = jnp.zeros((1, WIDTH), F32)
    d_shift = jnp.zeros((1, WIDTH), F32)
    for b, ref in enumerate((x_own, x_yp, x_cp, x_dg)):
        normed, _ = norm_stats(ref[...].astype(F32))
        part = dot_t(d_proj[block(b)], qkv_w[:, 0:QKV_COLS])
        d_gain = d_gain + jnp.sum(part * normed, axis=0, keepdims=True)
        d_shift = d_shift + jnp.sum(part, axis=0, keepdims=True)
        if b == 0:
            dn1_own[...] = part
        elif b == 1:
            dn1_two[...] = part.astype(BF)
        else:
            dn1_theirs[block(b - 2)] = part.astype(BF)
    natural[:, 0:QKV_COLS] = t_dot(n1[...], d_proj[...]).astype(BF)
    my_cols = pl.ds(pl.multiple_of(256 * s, 256), 256)
    for j, ref in enumerate((o_own, o_yp, o_cp, o_dg)):
        heads = jnp.concatenate([ref[block(b ^ j)] for b in range(4)], axis=0)
        rows = pl.ds(pl.multiple_of(256 * place[j], 256), 256)
        natural[rows, QKV_COLS : QKV_COLS + OUT_COLS] = t_dot(heads, da[:, my_cols]).astype(BF)
    rows_out[...] = jnp.zeros((EXTRA, WIDTH), F32)
    rows_out[0:1] = d_gain
    rows_out[1:2] = d_shift
    for start, first in ((0, 0), (512, 512)):
        sums = jnp.sum(d_proj[:, first : first + 256].astype(F32), axis=0, keepdims=True)
        sums = jnp.broadcast_to(sums, (8, 256)).astype(BF)
        at = pl.ds(pl.multiple_of(start + 128 * s, 128), 128)
        for c in (0, 1):
            rows_out[2 + c : 3 + c, at] = dot_t(sums, bias_hot(c))[0:1]
    rows_out[4:7] = small_c[0:3]
    rows_out[pl.ds(7 + s, 1)] = small_b[0:1]
    rows_out[11:12] = small_b[1:2]
    natural[:, QKV_COLS + OUT_COLS :] = rows_out[...].T.astype(BF)
    for zx in range(16):
        a, b = plane_place(core[0], zx)
        for half in range(2):
            rows = slice(512 * half + 32 * zx, 512 * half + 32 * zx + 32)
            send[a, b, 32 * half : 32 * half + 32] = natural[rows]


def input_grad_kernel(mine, got_cp, got_yp, dr, x_own, vec, out):
    normed, scale = norm_stats(x_own[...].astype(F32))
    dn1 = mine[...] + got_cp[block(0)].astype(F32) + got_yp[...].astype(F32)
    grad = dr[...] + norm_back(dn1, vec[0:1], normed, scale)
    out[:, 0] = grad[0:TOK]


def output_kernel(mine, got_cp, got_yp, r, vec, out):
    y = mine[...] + got_cp[block(0)].astype(F32) + got_yp[...].astype(F32)
    out[0] = (y + r[...] + vec[11:12])[0:TOK].astype(BF)


def sum_of(ref):
    total = ref[0].astype(F32)
    for d in range(1, ref.shape[0]):
        total = total + ref[d].astype(F32)
    return total


def sum_low_kernel(got, out):
    out[...] = sum_of(got).astype(BF)


def sum_line_kernel(places, got, own, to_1, to_2, to_3, total):
    total[...] = sum_of(got)
    own[...] = total[places[1]]
    for by, ref in ((1, to_1), (2, to_2), (3, to_3)):
        ref[...] = total[lax.rem(places[1] + by, 4)].astype(BF)


def sum_join_kernel(got, own, got_1, got_2, got_3, out):
    out[:, 0:REST] = sum_of(got).astype(BF)
    hidden = own[...]
    for ref in (got_1, got_2, got_3):
        hidden = hidden + ref[...].astype(F32)
    out[:, REST:] = hidden.astype(BF)


def sum_rest_kernel(got, down, up, qkv, out, *vectors):
    total = jnp.concatenate(
        [got[s].astype(F32) + got[4 + s].astype(F32) for s in range(4)], axis=0
    )
    down[0] = total[:, REST + 1024 :]
    cols = [
        jnp.concatenate(
            [
                total[8 * s : 8 * s + 8, REST + 128 * t : REST + 128 * t + 128]
                for s in range(4)
            ],
            axis=1,
        )
        for t in range(8)
    ]
    cols = jnp.concatenate(cols, axis=0)
    high = cols.astype(BF)
    low = (cols - high.astype(F32)).astype(BF)
    natural = dot_t(high, hidden_hot()) + dot_t(low, hidden_hot())
    for t in range(8):
        up[0, :, 512 * t : 512 * t + 512] = natural[8 * t : 8 * t + 8]
    for s in range(4):
        rows = slice(8 * s, 8 * s + 8)
        for i in range(3):
            at = 1024 * i + 256 * s
            qkv[0, :, at : at + 256] = total[rows, 256 * i : 256 * i + 256]
        out[0, :, 256 * s : 256 * s + 256] = total[rows, QKV_COLS : QKV_COLS + OUT_COLS]
    extra = sum(total[8 * s : 8 * s + 8, QKV_COLS + OUT_COLS : REST] for s in range(4))
    place = 0
    for ref in vectors:
        size = ref.shape[1]
        value = jnp.zeros((8, size), F32)
        for c in range(size // 8):
            column = jnp.broadcast_to(extra[:, place : place + 1], (8, size))
            hit = iota((8, size), 1) == iota((8, size), 0) + 8 * c
            value = jnp.where(hit, column, value)
            place += 1
        ref[...] = jnp.sum(value, axis=0, keepdims=True)


def body(
    inputs,
    token_mask,
    first_gain,
    first_shift,
    qkv_weight,
    qv_bias,
    out_weight,
    out_bias,
    second_gain,
    second_shift,
    up_weight,
    up_bias,
    down_weight,
    down_bias,
    cotangent,
):
    core = lax.axis_index("core").astype(jnp.int32).reshape(1)
    seq = lax.axis_index("yhi").astype(jnp.int32).reshape(1) * 2 + core
    z_place, x_place = lax.axis_index("z"), lax.axis_index("x")
    places = jnp.where(
        core == 0, jnp.stack([x_place, z_place]), jnp.stack([z_place, x_place])
    ).astype(jnp.int32)

    (send,) = call(
        prepare_kernel,
        [((2, 4, 8, JOINT), BF)],
        *hbm(
            qkv_weight,
            out_weight,
            up_weight,
            down_weight,
            first_gain,
            first_shift,
            qv_bias,
            out_bias,
            second_gain,
            second_shift,
            up_bias,
            down_bias,
        ),
    )
    x, g = call(
        tokens_kernel,
        [((PAD, WIDTH), BF, HBM), ((PAD, WIDTH), BF, HBM)],
        *hbm(inputs, token_mask, cotangent),
        scratch=[pltpu.VMEM((PAD, WIDTH), F32)],
        us=2,
        deps=(send,),
    )
    pieces = lax.all_to_all(
        send.reshape(64, JOINT), ("ylo", "yhi", "core"), 0, 0, tiled=True
    )
    x_yp, g_yp = over_y(x), over_y(g)
    x_cp, g_cp = over_core(x), over_core(g)
    (send,) = call(spread_kernel, [((4, 64, JOINT), BF)], pieces, deps=(x_cp, g_cp))
    pieces = exchange(send.reshape(256, JOINT), STAGE_A)
    send, line = call(
        line_kernel,
        [((4, 256, REST), BF, HBM), ((256, 2048), BF, HBM)],
        pieces,
        deps=(x_yp,),
    )
    got = exchange(send.reshape(1024, REST), STAGE_B)
    line = after(line, g_yp).reshape(4, 64, 2048)
    lines = [line] + [shift(line, STAGE_B, by) for by in (1, 2, 3)]
    xs = (x, x_yp, x_cp, over_core(x_yp))
    gs = (g, g_yp, g_cp, over_core(g_yp))
    w_qkv, w_own, vec = call(
        unpack_kernel,
        [((1024, QKV_COLS), BF), ((1024, OUT_COLS), BF), ((16, WIDTH), F32)],
        core,
        got.reshape(4, 4, 64, REST),
        scratch=[pltpu.VMEM((1024, EXTRA), F32)],
        scalars=1,
        deps=(g_yp,),
    )
    w_yp = over_y(w_own)
    ws = (w_own, w_yp, over_core(w_own), over_core(w_yp))

    n1, qkv, o, lse = call(
        attend_kernel,
        [
            ((ROWS, WIDTH), BF, HBM),
            ((ROWS, QKV_COLS), BF, HBM),
            ((ROWS, 256), BF, HBM),
            ((ROWS, 128), F32, HBM),
        ],
        seq,
        *xs,
        w_qkv,
        vec,
        scalars=1,
        us=8,
    )
    o_yp = over_y(o)
    os = (o, o_yp, over_core(o), over_core(o_yp))
    n2, z, du, dn2_mine, dn2_theirs, normed_2, scale_2, down_w, r = call(
        hidden_kernel,
        [
            ((ROWS, WIDTH), BF),
            ((ROWS, WIDTH), BF),
            ((ROWS, WIDTH), BF),
            ((HALF, WIDTH), F32),
            ((HALF, WIDTH), BF),
            ((HALF, WIDTH), F32, HBM),
            ((HALF, 128), F32, HBM),
            ((1024, WIDTH), BF),
            ((PAD, WIDTH), F32, HBM),
        ],
        seq,
        places,
        *hbm(o),
        *os[1:],
        *xs,
        ws[0],
        *hbm(ws[1]),
        *ws[2:],
        vec,
        *lines,
        *hbm(g),
        *gs[1:],
        scratch=[
            pltpu.VMEM((ROWS, WIDTH), F32),
            pltpu.VMEM((1024, WIDTH), BF),
            pltpu.VMEM((ROWS, WIDTH), BF),
        ],
        scalars=2,
        us=12,
    )
    two = (dn2_mine + over_core(dn2_theirs).astype(F32)).astype(BF)
    two_yp = over_y(two)
    d_hidden, small_b, y_own, y_two, y_theirs = call(
        hidden_grad_kernel,
        [
            ((4, 4, 64, 2048), BF, HBM),
            ((8, WIDTH), F32),
            ((PAD, WIDTH), F32, HBM),
            ((PAD, WIDTH), BF, HBM),
            ((HALF, WIDTH), BF, HBM),
        ],
        core,
        z,
        du,
        n2,
        down_w,
        *gs,
        scalars=1,
        deps=(two,),
        us=300,
    )
    d_hidden = exchange(d_hidden.reshape(1024, 2048), STAGE_A)
    y_cp = over_core(y_theirs)
    da, dr, small_c = call(
        residual_kernel,
        [((HALF, WIDTH), BF), ((PAD, WIDTH), F32, HBM), ((8, WIDTH), F32)],
        two,
        two_yp,
        g,
        g_yp,
        *hbm(normed_2, scale_2),
        vec,
        deps=(y_theirs,),
        us=150,
    )
    da_cp = over_core(da)
    y_low = (y_two.astype(F32) + y_cp[PAD:].astype(F32)).astype(BF)
    y_yp = over_y(y_low)
    dn1_own, dn1_two, dn1_theirs, send = call(
        attend_grad_kernel,
        [
            ((PAD, WIDTH), F32, HBM),
            ((PAD, WIDTH), BF, HBM),
            ((HALF, WIDTH), BF, HBM),
            ((4, 4, 64, REST), BF, HBM),
        ],
        seq,
        core,
        da,
        da_cp,
        *ws,
        *xs,
        *hbm(w_qkv, qkv, lse, n1),
        *os,
        small_b,
        small_c,
        scratch=[
            pltpu.VMEM((ROWS, WIDTH), BF),
            pltpu.VMEM((ROWS, QKV_COLS), BF),
            pltpu.VMEM((EXTRA, WIDTH), F32),
            pltpu.VMEM((1024, REST), BF),
        ],
        scalars=2,
        us=15,
    )
    got = exchange(after(send.reshape(1024, REST), d_hidden), STAGE_A)
    dn1_cp = over_core(dn1_theirs)
    dn1_low = (dn1_two.astype(F32) + dn1_cp[PAD:].astype(F32)).astype(BF)
    dn1_yp = over_y(dn1_low)
    hidden_own, *parts = call(
        sum_line_kernel,
        [((64, 2048), F32)] + [((64, 2048), BF)] * 3,
        places,
        d_hidden.reshape(4, 4, 64, 2048),
        scratch=[pltpu.VMEM((4, 64, 2048), F32)],
        scalars=1,
    )
    parts = [shift(part, STAGE_B, by) for by, part in zip((1, 2, 3), parts)]
    (send,) = call(
        sum_low_kernel, [((256, REST), BF, HBM)], got.reshape(4, 256, REST), deps=(dn1_low, y_yp, hidden_own)
    )
    got = exchange(send, STAGE_B)
    (send,) = call(
        sum_join_kernel,
        [((64, JOINT), BF)],
        got.reshape(4, 64, REST),
        hidden_own,
        *parts,
        deps=(dn1_yp,),
    )
    got = lax.all_to_all(send, ("ylo", "yhi", "core"), 0, 0, tiled=True)
    (block_output,) = call(
        output_kernel, [((1, TOK, WIDTH), BF)], *hbm(y_own, y_cp, y_yp, r), vec
    )
    (g0,) = call(
        input_grad_kernel,
        [((TOK, 1, WIDTH), F32)],
        *hbm(dn1_own, dn1_cp, dn1_yp, dr, x),
        vec,
    )
    g0 = g0.transpose(1, 0, 2)
    d_down, d_up, d_qkv, d_out, d_fg, d_fs, d_qvb, d_ob, d_sg, d_ss, d_ub, d_db = call(
        sum_rest_kernel,
        [
            ((1, 32, WIDTH), F32),
            ((1, 8, 4096), F32),
            ((1, 8, 3072), F32),
            ((1, 8, WIDTH), F32),
        ]
        + [((1, n), F32) for n in (8, 8, 16, 8, 8, 8, 32, 8)],
        got.reshape(8, 8, JOINT),
        deps=(block_output, g0),
    )
    return (
        block_output,
        g0,
        d_fg,
        d_fs,
        d_qkv,
        d_qvb,
        d_out,
        d_ob,
        d_sg,
        d_ss,
        d_up,
        d_ub,
        d_down,
        d_db,
    )


def solution(mesh):
    fine = Mesh(mesh.devices.reshape(2, 4, 4, 2, 2), ALL)
    tokens = P(DP, SEQ, None)
    vector = P(None, ALL)
    matrix = P(None, ALL, None)
    return jax.shard_map(
        body,
        mesh=fine,
        in_specs=(
            tokens,
            P(DP, SEQ),
            vector,
            vector,
            matrix,
            vector,
            matrix,
            vector,
            vector,
            vector,
            matrix,
            vector,
            matrix,
            vector,
            tokens,
        ),
        out_specs=(
            tokens,
            tokens,
            vector,
            vector,
            matrix,
            vector,
            matrix,
            vector,
            vector,
            vector,
            matrix,
            vector,
            matrix,
            vector,
        ),
        check_vma=False,
    )
```
